32 devices in a mesh: ctx: 16 (over z, y, x), fsdp: 2 (over core).
Axes of the slice: x: 2, y: 2, z: 4, core: 2. Of those that a mesh axis runs over, the one named last changes fastest.
Arguments:
- tokens: bfloat16 [2, 2048, 2048], P('fsdp', 'ctx'), may hold values from -6 to 6
- cotangent: bfloat16 [2, 2048, 2048], P('fsdp', 'ctx'), may hold values from -6 to 6
- doc_starts: int32 [2, 4], P('fsdp'), may hold values from 0 to 2047, as said below
- routes: int32 [2, 2048, 6], P('fsdp', 'ctx'), may hold values from 0 to 15, all different within a row; in each aligned block of 128 rows (0 to 127, 128 to 255, ..., all dimensions but the last counted through in order) at most 68 rows name the same one
- attn_gain: float32 [2048], P(('ctx', 'fsdp')), may hold values from 0.25 to 1.75
- q_weight: float32 [2048, 3072], P(('ctx', 'fsdp')), may hold values from -0.125 to 0.125
- kva_weight: float32 [2048, 576], P(('ctx', 'fsdp')), may hold values from -0.125 to 0.125
- kv_gain: float32 [512], P(('ctx', 'fsdp')), may hold values from 0.25 to 1.75
- kvb_weight: float32 [512, 4096], P(('ctx', 'fsdp')), may hold values from -0.25 to 0.25
- o_weight: float32 [2048, 2048], P(None, ('ctx', 'fsdp')), may hold values from -2 to 2
- ffn_gain: float32 [2048], P(('ctx', 'fsdp')), may hold values from 0.25 to 1.75
- router_weight: float32 [2048, 16], P(('ctx', 'fsdp')), may hold values from -0.0625 to 0.0625
- shared_gate: float32 [2048, 2816], P(('ctx', 'fsdp')), may hold values from -0.125 to 0.125
- shared_up: float32 [2048, 2816], P(('ctx', 'fsdp')), may hold values from -0.125 to 0.125
- shared_down: float32 [2816, 2048], P(None, ('ctx', 'fsdp')), may hold values from -0.109375 to 0.109375
- expert_gate: float32 [16, 2048, 1408], P('ctx', 'fsdp'), may hold values from -0.125 to 0.125
- expert_up: float32 [16, 2048, 1408], P('ctx', 'fsdp'), may hold values from -0.125 to 0.125
- expert_down: float32 [16, 1408, 2048], P('ctx', None, 'fsdp'), may hold values from -0.15625 to 0.15625
Outputs:
- output: bfloat16 [2, 2048, 2048], P('fsdp', 'ctx')
- input_grad: bfloat16 [2, 2048, 2048], P('fsdp', 'ctx')
- attn_gain_grad: float32 [2048], P(('ctx', 'fsdp'))
- q_weight_grad: float32 [2048, 3072], P(('ctx', 'fsdp'))
- kva_weight_grad: float32 [2048, 576], P(('ctx', 'fsdp'))
- kv_gain_grad: float32 [512], P(('ctx', 'fsdp'))
- kvb_weight_grad: float32 [512, 4096], P(('ctx', 'fsdp'))
- o_weight_grad: float32 [2048, 2048], P(None, ('ctx', 'fsdp'))
- ffn_gain_grad: float32 [2048], P(('ctx', 'fsdp'))
- router_weight_grad: float32 [2048, 16], P(('ctx', 'fsdp'))
- shared_gate_grad: float32 [2048, 2816], P(('ctx', 'fsdp'))
- shared_up_grad: float32 [2048, 2816], P(('ctx', 'fsdp'))
- shared_down_grad: float32 [2816, 2048], P(None, ('ctx', 'fsdp'))
- expert_gate_grad: float32 [16, 2048, 1408], P('ctx', 'fsdp')
- expert_up_grad: float32 [16, 2048, 1408], P('ctx', 'fsdp')
- expert_down_grad: float32 [16, 1408, 2048], P('ctx', None, 'fsdp')
The draws below stay inside these ranges and needn't reach their ends.
Inputs may be any that keep to these rules, and one draw needn't show every extreme that they name: `doc_starts`: per sequence 4 increasing starts, the first 0; the second document begins within the first 128 positions and ends within the last 128; in some sequence the last start is the last position. `routes`: in each device's aligned block of 128 rows no expert is named by more than 68 rows, a bound that some block reaches.
All inputs are finite; a program needn't handle non-finite values.
Results may differ from the reference program's by a relative error of at most 0.019.
The reference program's roundings to bfloat16 on the way count: a program that leaves them out, or rounds other values in their place, can miss the bound.
Values may be sent and summed in bfloat16 or wider, within the bound.
A program may use at most 512 MiB of HBM per device.

```python
import math
import jax
import jax.numpy as jnp
import numpy as np
from jax import lax

D = 2048
HEADS = 16
NOPE = 128
ROPE = 64
VDIM = 128
RANK = 512
FE = 1408
SHARED = 2816
TOP = 6
TOK_DEV = 128
SEQS = 2
SEQ = 2048
EXPERTS = 16
CAP = 68
N_CTX = 16


def draw_doc_starts(key, part):
    key = jax.random.fold_in(key, 11)
    first_key, second_key, third_key, fourth_key = jax.random.split(key, 4)
    opening = jax.random.randint(first_key, (SEQS, 1), 1, TOK_DEV // 2)
    closing = jax.random.randint(second_key, (SEQS, 1), SEQ - TOK_DEV + 1, SEQ - TOK_DEV // 2)
    trailing = jax.random.randint(third_key, (SEQS, 1), SEQ - TOK_DEV // 2 + 1, SEQ)
    chosen_row = jax.random.randint(fourth_key, (), 0, SEQS)
    rows = jnp.arange(SEQS, dtype=jnp.int32)[:, None]
    trailing = jnp.where(rows == chosen_row, SEQ - 1, trailing)
    return jnp.concatenate([jnp.zeros((SEQS, 1), jnp.int32), opening, closing, trailing], axis=1).astype(jnp.int32)


def shard_levels(stream_key, dims, cuts, smallest, high):
    def one(position, shards_of):
        heights = jax.random.uniform(jax.random.fold_in(jax.random.fold_in(stream_key, 6), position), (shards_of,), jnp.float32, smallest / len(cuts), high / len(cuts))
        return jnp.repeat(jnp.exp(heights), dims[position] // shards_of).reshape((-1,) + (1,) * (len(dims) - position - 1))

    factor_of = one(*cuts[0])
    for cut in cuts[1:]:
        factor_of = factor_of * one(*cut)
    return factor_of


def assign_block(key, own, number, rows, amount, top, reach, skew):
    ranking = jax.random.permutation(key, amount)
    crowded, common = shares(amount, rows * top, reach, skew, True), shares(amount, rows * top, reach, skew, False)
    places = jnp.arange(amount)

    def named(sizes, turn):
        used = int((sizes > 0).sum())
        fixed = max(1, used // 4)
        passed = fixed + (places - fixed + turn * (used - fixed)) % max(1, amount - fixed)
        return jnp.zeros((amount,), jnp.int32).at[ranking[jnp.where(places < fixed, places, passed)]].set(jnp.asarray(sizes, jnp.int32))

    sizes = jnp.where(number % 4 == 0, named(crowded, number // 4), named(common, number - number // 4 - 1))
    mixed = jax.random.permutation(jax.random.fold_in(own, 3), amount)
    source_of, taker = mixed[0:amount // 2 * 2:2], mixed[1:amount // 2 * 2:2]
    room = jnp.minimum(sizes[source_of] - 1, reach - sizes[taker]) // 2
    room = jnp.where((source_of == ranking[0]) | (taker == ranking[0]) | (sizes[taker] == 0), 0, jnp.maximum(room, 0))
    passed = jax.random.randint(jax.random.fold_in(own, 4), (amount // 2,), 0, 1 << 20) % (room + 1)
    sizes = sizes.at[source_of].add(-passed).at[taker].add(passed)
    members = jnp.searchsorted(jnp.cumsum(sizes), jnp.arange(rows * top), side="right").astype(jnp.int32)
    table = members.reshape(top, rows).T
    table = table[jax.random.permutation(jax.random.fold_in(own, 1), rows)]
    turn = jax.random.randint(jax.random.fold_in(own, 2), (rows, 1), 0, top)
    return jnp.take_along_axis(table, (jnp.arange(top)[None, :] + turn) % top, axis=1)


def shares(amount, total, limit, lean, full):
    weights = [(1 << 20) // math.isqrt(rank ** lean) + 1 for rank in range(1, amount + 1)]
    largest = limit if full else min(limit, max(-(-total // amount), total * weights[0] // sum(weights)))
    least = 1 if total - largest >= amount - 1 else 0
    given, rest = [largest] + [least] * (amount - 1), total - largest - least * (amount - 1)
    while rest > 0:
        movable = [i for i in range(1, amount) if given[i] < largest] or [i for i in range(1, amount) if given[i] < limit]
        pool, left = sum([weights[i] for i in movable]), rest
        for i in movable:
            more = min(limit - given[i], max(1, left * weights[i] // pool), rest)
            given[i] = given[i] + more
            rest = rest - more
    return np.array(given)


def normal_values(key, shape, spread, most, shards=(), held_as=jnp.bfloat16):
    factor_of = shard_levels(key, shape, shards, -0.22, 0.18) if shards else 1.0
    drawn = jax.random.normal(key, shape, jnp.float32) * spread * factor_of
    return jnp.minimum(jnp.maximum(drawn, -most), most).astype(held_as)


def setup_inputs(seed: int = 0) -> dict:
    seeds = jax.random.split(jax.random.key(seed), 19)
    tokens = normal_values(seeds[0], (SEQS, SEQ, D), 1.0, 6.0, ((0, 2), (1, 16)))
    cotangent = normal_values(seeds[1], (SEQS, SEQ, D), 1.0, 6.0, ((0, 2), (1, 16)))
    doc_starts = draw_doc_starts(jax.random.fold_in(seeds[18], 71), 0)
    routes_keys = jax.random.split(jax.random.fold_in(seeds[3], 1), SEQS * SEQ // TOK_DEV)
    routes_turns = jax.random.permutation(jax.random.fold_in(seeds[3], 3), SEQS * SEQ // TOK_DEV)
    routes = jax.vmap(lambda own, number: assign_block(jax.random.fold_in(seeds[3], 2), own, number, TOK_DEV, EXPERTS, TOP, CAP, 1))(routes_keys, routes_turns).reshape((SEQS, SEQ, TOP))
    attn_gain = jnp.clip(1.0 + 0.15 * jax.random.normal(seeds[4], (D,), jnp.float32), 0.25, 1.75)
    q_weight = normal_values(seeds[5], (D, HEADS * (NOPE + ROPE)), D ** -0.5, 0.125, ((0, 32),), jnp.float32)
    kva_weight = normal_values(seeds[6], (D, RANK + ROPE), D ** -0.5, 0.125, ((0, 32),), jnp.float32)
    kv_gain = jnp.clip(1.0 + 0.15 * jax.random.normal(seeds[7], (RANK,), jnp.float32), 0.25, 1.75)
    kvb_weight = normal_values(seeds[8], (RANK, HEADS * (NOPE + VDIM)), RANK ** -0.5, 0.25, ((0, 32),), jnp.float32)
    o_weight = normal_values(seeds[9], (HEADS * VDIM, D), (max(HEADS * VDIM // 256, 1)) ** -0.5, 2.0, ((1, 32),), jnp.float32)
    ffn_gain = jnp.clip(1.0 + 0.15 * jax.random.normal(seeds[10], (D,), jnp.float32), 0.25, 1.75)
    router_weight = normal_values(seeds[11], (D, EXPERTS), (4 * D) ** -0.5, 0.0625, ((0, 32),), jnp.float32)
    shared_gate = normal_values(seeds[12], (D, SHARED), D ** -0.5, 0.125, ((0, 32),), jnp.float32)
    shared_up = normal_values(seeds[13], (D, SHARED), D ** -0.5, 0.125, ((0, 32),), jnp.float32)
    shared_down = normal_values(seeds[14], (SHARED, D), SHARED ** -0.5, 0.109375, ((1, 32),), jnp.float32)
    expert_gate = normal_values(seeds[15], (EXPERTS, D, FE), D ** -0.5, 0.125, ((0, 16), (1, 2)), jnp.float32)
    expert_up = normal_values(seeds[16], (EXPERTS, D, FE), D ** -0.5, 0.125, ((0, 16), (1, 2)), jnp.float32)
    expert_down = normal_values(seeds[17], (EXPERTS, FE, D), FE ** -0.5, 0.15625, ((0, 16), (2, 2)), jnp.float32)
    return dict(tokens=tokens, cotangent=cotangent, doc_starts=doc_starts, routes=routes, attn_gain=attn_gain, q_weight=q_weight, kva_weight=kva_weight, kv_gain=kv_gain, kvb_weight=kvb_weight, o_weight=o_weight, ffn_gain=ffn_gain, router_weight=router_weight, shared_gate=shared_gate, shared_up=shared_up, shared_down=shared_down, expert_gate=expert_gate, expert_up=expert_up, expert_down=expert_down)


@jax.custom_vjp
def low(v):
    return lax.optimization_barrier(v.astype(jnp.bfloat16)).astype(jnp.float32)

@jax.custom_vjp
def low_back(v):
    return v

def low_keep(v):
    return (low(v), None)

def low_pass(kept, grad):
    return (grad,)

def back_keep(v):
    return (v, None)

def back_low(kept, grad):
    return (low(grad),)
low.defvjp(low_keep, low_pass)
low_back.defvjp(back_keep, back_low)
EPS = 1e-06
THETA = 10000.0
NEG = -1e+30

def rounded_both(values):
    return low(low_back(values))

def matmul_high(left, right):
    return jnp.matmul(left, right, precision=lax.Precision.HIGHEST)

def rms_norm(values, gain):
    return values * lax.rsqrt(lax.optimization_barrier(jnp.mean(values * values, axis=-1, keepdims=True)) + EPS) * gain

def silu(values):
    return values * jax.nn.sigmoid(values)

def softmax_last(values):
    shifted = jnp.exp(values - lax.optimization_barrier(jnp.max(values, axis=-1, keepdims=True)))
    return shifted / lax.optimization_barrier(jnp.sum(shifted, axis=-1, keepdims=True))

def doc_index(starts, positions):
    return lax.optimization_barrier(jnp.sum((positions[:, None] >= starts[None, :]).astype(jnp.int32), axis=1)) - 1

def dealt_positions(rows):
    half = TOK_DEV // 2
    owner = rows // TOK_DEV
    within = rows % TOK_DEV
    return jnp.where(within < half, owner * half + within, (2 * N_CTX - 1 - owner) * half + within - half).astype(jnp.int32)

def rope_tables(positions):
    half = ROPE // 2
    frequency = THETA ** (-jnp.arange(half, dtype=jnp.float32) / half)
    angles = positions.astype(jnp.float32)[:, None] * frequency[None, :]
    return (jnp.cos(angles), jnp.sin(angles))

def rotate_pairs(values, cosines, sines):
    half = values.shape[-1] // 2
    first = values[..., :half]
    second = values[..., half:]
    return jnp.concatenate([first * cosines - second * sines, second * cosines + first * sines], axis=-1)

def slot_targets(picks):
    flat = picks.reshape(N_CTX, TOK_DEV * TOP)
    onehot = (flat[:, :, None] == jnp.arange(EXPERTS, dtype=jnp.int32)[None, None, :]).astype(jnp.int32)
    running = jnp.cumsum(onehot, axis=1)
    slots = lax.optimization_barrier(jnp.sum(onehot * (running - 1), axis=2))
    return (flat * CAP + slots).astype(jnp.int32)

def apply_expert(operands):
    rows, gate_proj, up_proj, down_proj = operands
    hidden = low(silu(low_back(matmul_high(rows, gate_proj))) * low_back(matmul_high(rows, up_proj)))
    return rounded_both(matmul_high(hidden, down_proj))

def sequence_forward(inputs, starts, picks, rounded):
    gain_one, query_proj, down_latent, gain_latent, up_latent, out_proj, gain_two, router_proj, shared_in_gate, shared_in_up, shared_out_proj, expert_in_gate, expert_in_up, expert_out_proj = rounded
    positions = dealt_positions(jnp.arange(SEQ, dtype=jnp.int32))
    cosines, sines = rope_tables(positions)
    normed = low(rms_norm(inputs, gain_one))
    query_raw = low_back(matmul_high(normed, query_proj)).reshape(SEQ, HEADS, NOPE + ROPE)
    query_rot = rotate_pairs(query_raw[:, :, NOPE:], cosines[:, None, :], sines[:, None, :])
    queries = rounded_both(jnp.concatenate([query_raw[:, :, :NOPE], query_rot], axis=-1))
    compressed = low_back(matmul_high(normed, down_latent))
    latent = low(rms_norm(compressed[:, :RANK], gain_latent))
    key_rope = rounded_both(rotate_pairs(compressed[:, RANK:], cosines, sines))
    expanded = low(matmul_high(latent, up_latent)).reshape(SEQ, HEADS, NOPE + VDIM)
    keys = jnp.concatenate([expanded[:, :, :NOPE], jnp.broadcast_to(key_rope[:, None, :], (SEQ, HEADS, ROPE))], axis=-1)
    values = expanded[:, :, NOPE:]
    documents = doc_index(starts, positions)
    scale = (NOPE + ROPE) ** (-0.5)
    qblock = min(512, SEQ)

    def attend(index):
        first = index * qblock
        block_queries = lax.dynamic_slice_in_dim(queries, first, qblock, 0)
        block_pos = lax.dynamic_slice_in_dim(positions, first, qblock, 0)
        block_docs = doc_index(starts, block_pos)
        scores = low_back(scale * jnp.einsum('qhd,khd->hqk', block_queries, keys, precision=lax.Precision.HIGHEST))
        allowed = (block_docs[:, None] == documents[None, :]) & (positions[None, :] <= block_pos[:, None])
        probs = low(softmax_last(jnp.where(allowed[None], scores, NEG)))
        return jnp.einsum('hqk,khd->qhd', probs, values, precision=lax.Precision.HIGHEST)
    attended = lax.map(jax.checkpoint(attend), jnp.arange(SEQ // qblock, dtype=jnp.int32)).reshape(SEQ, HEADS * VDIM)
    attn_out = low_back(matmul_high(rounded_both(attended), out_proj))
    resid = inputs + attn_out
    ffn_in = low(rms_norm(resid, gain_two))
    logits = low_back(matmul_high(ffn_in, router_proj))
    chosen = (picks[:, :, None] == jnp.arange(EXPERTS, dtype=jnp.int32)[None, None, :]).astype(jnp.float32)
    gates = softmax_last(lax.optimization_barrier(jnp.sum(chosen * logits[:, None, :], axis=-1)))
    shared_hidden = low(silu(low_back(matmul_high(ffn_in, shared_in_gate))) * low_back(matmul_high(ffn_in, shared_in_up)))
    shared_result = low_back(matmul_high(shared_hidden, shared_out_proj))
    targets = slot_targets(picks)
    owners = jnp.broadcast_to(jnp.arange(N_CTX, dtype=jnp.int32)[:, None], (N_CTX, TOK_DEV * TOP))
    sources = jnp.broadcast_to(ffn_in.reshape(N_CTX, TOK_DEV, 1, D), (N_CTX, TOK_DEV, TOP, D)).reshape(N_CTX, TOK_DEV * TOP, D)
    buffers = jnp.zeros((N_CTX, EXPERTS * CAP, D), jnp.float32).at[owners, targets].add(sources)
    expert_rows = low_back(buffers.reshape(N_CTX, EXPERTS, CAP, D).transpose(1, 0, 2, 3).reshape(EXPERTS, N_CTX * CAP, D))
    expert_result = lax.map(jax.checkpoint(apply_expert), (expert_rows, expert_in_gate, expert_in_up, expert_out_proj))
    result_blocks = expert_result.reshape(EXPERTS, N_CTX, CAP, D).transpose(1, 0, 2, 3).reshape(N_CTX, EXPERTS * CAP, D)
    per_pick = result_blocks[owners, targets].reshape(SEQ, TOP, D)
    routed = lax.optimization_barrier(jnp.sum(gates[:, :, None] * per_pick, axis=1))
    return resid + routed + shared_result

def reference(tokens, cotangent, doc_starts, routes, attn_gain, q_weight, kva_weight, kv_gain, kvb_weight, o_weight, ffn_gain, router_weight, shared_gate, shared_up, shared_down, expert_gate, expert_up, expert_down):

    def forward(inputs, *masters):
        rounded = tuple((low(master) for master in masters))

        def per_sequence(operands):
            return sequence_forward(operands[0], operands[1], operands[2], rounded)
        return lax.map(jax.checkpoint(per_sequence), (inputs, doc_starts, routes))
    outputs, pullback = jax.vjp(forward, tokens.astype(jnp.float32), attn_gain, q_weight, kva_weight, kv_gain, kvb_weight, o_weight, ffn_gain, router_weight, shared_gate, shared_up, shared_down, expert_gate, expert_up, expert_down)
    grads = pullback(cotangent.astype(jnp.float32))
    return (outputs.astype(jnp.bfloat16), grads[0].astype(jnp.bfloat16), grads[1], grads[2], grads[3], grads[4], grads[5], grads[6], grads[7], grads[8], grads[9], grads[10], grads[11], grads[12], grads[13], grads[14])
```

```python
import functools

import jax
import jax.numpy as jnp
from jax import lax
from jax.experimental import pallas as pl
from jax.experimental.pallas import tpu as pltpu
from jax.sharding import PartitionSpec as P

D = 2048
HEADS = 16
NOPE = 128
ROPE = 64
VDIM = 128
RANK = 512
HEAD = NOPE + ROPE
KV = NOPE + VDIM

EPS = 1e-06
THETA = 10000.0
NEG = -1e30
MESH = pl.DeviceIdType.MESH

ZXY, ZYX = ("z", "x", "y"), ("z", "y", "x")
XYZ, YXZ = ("x", "y", "z"), ("y", "x", "z")


def pieces(rows):
    if rows == 128:
        return (
            (0, 32, ZXY),
            (32, 32, ZYX),
            (64, 16, ZXY),
            (80, 16, ZYX),
            (96, 16, XYZ),
            (112, 16, YXZ),
        )
    if rows % 32 == 0:
        return ((0, rows // 2, ZXY), (rows // 2, rows // 2, ZYX))
    return ((0, rows, ZXY),)


def maybe(cond, fn):
    if cond is None:
        fn()
    else:
        pl.when(cond)(fn)


def both(first, second):
    if first is None:
        return second
    if second is None:
        return first
    return jnp.logical_and(first, second)


class Place:
    def __init__(self, n, cores):
        self.n, self.cores, self.lines = n, cores, n // 4
        self.c, self.f = lax.axis_index("ctx"), lax.axis_index("fsdp")
        self.z, self.y, self.x = self.split(self.c)
        z, y, x, top = self.z, self.y, self.x, self.lines - 1
        self.peers = {
            ("z", 1): (self.index(jnp.minimum(z + 1, top), y, x), z < top),
            ("z", -1): (self.index(jnp.maximum(z - 1, 0), y, x), z > 0),
            ("y", 1): (self.index(z, 1 - y, x), None),
            ("x", 1): (self.index(z, y, 1 - x), None),
        }

    @staticmethod
    def split(c):
        return c // 4, (c // 2) % 2, c % 2

    @staticmethod
    def index(z, y, x):
        return z * 4 + y * 2 + x

    def owner(self, rel):
        oz = self.z + rel["z"]
        cond = None if rel["z"] == 0 else (oz >= 0) & (oz < self.lines)
        oz = jnp.clip(oz, 0, self.lines - 1)
        oy = 1 - self.y if rel["y"] else self.y
        ox = 1 - self.x if rel["x"] else self.x
        return cond, self.index(oz, oy, ox)


SLOT = {("z", 1): 0, ("z", -1): 1, ("y", 1): 2, ("x", 1): 3}


def offsets(n, order):
    lines = n // 4
    found = []
    for a in range(1 - lines, lines):
        for y in range(2):
            for x in range(2):
                rel = {"z": a, "y": y, "x": x}
                used = [k for k, d in enumerate(order) if rel[d] != 0]
                found.append((rel, used[-1] if used else -1, abs(a) + y + x))
    return found


class Gather:
    peers = "near"

    def __init__(self, rows, cols, dtype, place):
        self.rows, self.cols, self.dtype, self.place = rows, cols, dtype, place

    def setup(self, n, cores):
        self.n, self.parts = n, pieces(self.rows)
        k = len(self.parts)
        self.out = jax.ShapeDtypeStruct((n * self.rows, self.cols), self.dtype)
        self.out_spec = pl.BlockSpec(memory_space=pl.ANY)
        self.scratch = [
            pltpu.SemaphoreType.DMA((k, 4, n)),
            pltpu.SemaphoreType.DMA((k, n)),
            pltpu.SemaphoreType.DMA((k,)),
        ]

    def events(self, at, src, out, send_sem, recv_sem, own_sem):
        n, parts = self.n, self.parts
        sent, kept, events = [], [], []

        def rows_of(i, owner):
            return pl.ds(self.place(owner, parts[i][0]), parts[i][1])

        def send(i, owner, key, cond, first):
            peer, ok = at.peers[key]
            there = out.at[rows_of(i, owner)]
            copy = pltpu.make_async_remote_copy(
                src_ref=src.at[pl.ds(parts[i][0], parts[i][1])] if first else there,
                dst_ref=there,
                send_sem=send_sem.at[i, SLOT[key], owner],
                recv_sem=recv_sem.at[i, owner],
                device_id={"ctx": peer},
                device_id_type=MESH,
            )
            cond = both(cond, ok)
            maybe(cond, copy.start)
            sent.append((cond, copy))

        def onward(i, rel, last, cond, owner, first):
            order = parts[i][2]
            if last >= 0 and order[last] == "z":
                send(i, owner, ("z", 1 if rel["z"] < 0 else -1), cond, first)
            for d in order[last + 1 :]:
                if d == "z":
                    send(i, owner, ("z", 1), cond, first)
                    send(i, owner, ("z", -1), cond, first)
                else:
                    send(i, owner, (d, 1), cond, first)

        def begin():
            for i in range(len(parts)):
                onward(i, {"z": 0, "y": 0, "x": 0}, -1, None, at.c, True)
            for i, (start, rows, order) in enumerate(parts):
                copy = pltpu.make_async_copy(
                    src.at[pl.ds(start, rows)], out.at[rows_of(i, at.c)], own_sem.at[i]
                )
                copy.start()
                kept.append(copy)

        def arrive(i, rel, last):
            cond, owner = at.owner(rel)
            there = out.at[rows_of(i, owner)]
            maybe(
                cond,
                lambda: pltpu.make_async_copy(there, there, recv_sem.at[i, owner]).wait(),
            )
            onward(i, rel, last, cond, owner, False)

        def end():
            for cond, copy in sent:
                maybe(cond, copy.wait_send)
            for copy in kept:
                copy.wait()

        events.append((-1, begin))
        for i, part in enumerate(parts):
            for rel, last, hops in offsets(n, part[2]):
                if last >= 0:
                    events.append((hops, functools.partial(arrive, i, rel, last)))
        events.append((1000, end))
        return events


class Reduce:
    peers = "near"

    def __init__(self, rows, cols, place):
        self.rows, self.cols, self.place = rows, cols, place
        self.dtype = jnp.bfloat16

    def setup(self, n, cores):
        self.n, self.parts = n, pieces(self.rows)
        lines, k = n // 4, len(self.parts)
        self.size = {"z": lines, "y": 2, "x": 2}
        self.table, total = [], 0
        for start, rows, order in self.parts:
            entry, ahead = {}, 1
            for d in order:
                entry[d] = total
                total += rows * ahead * (lines + 1 if d == "z" else 1)
                ahead *= self.size[d]
            self.table.append(entry)
        self.out = jax.ShapeDtypeStruct((self.rows, self.cols), jnp.float32)
        self.out_spec = pl.BlockSpec(memory_space=pltpu.VMEM)
        self.scratch = [
            pltpu.VMEM((total, self.cols), self.dtype),
            pltpu.VMEM((n * self.rows, self.cols), self.dtype),
            pltpu.SemaphoreType.DMA((k, 4, n)),
            pltpu.SemaphoreType.DMA((k, 4, n)),
            pltpu.SemaphoreType.DMA((k, n)),
        ]

    def held_rows(self, i, d, owner, line, up):
        start, rows, order = self.parts[i]
        oz, oy, ox = Place.split(owner)
        have = {"z": oz, "y": oy, "x": ox}
        number = 0
        for e in order[: order.index(d)]:
            number = number * self.size[e] + have[e]
        if d == "z":
            lines = self.size["z"]
            number = number * (lines + 1) + (oz if up else jnp.where(oz == line, lines, oz))
        return pl.ds(pl.multiple_of(self.table[i][d] + number * rows, 16), rows)

    def events(self, at, src, out, held, own, send_sem, recv_sem, own_sem):
        n, parts, lines = self.n, self.parts, self.n // 4
        sent, events = [], []

        def coming(i, rel, last):
            order = parts[i][2]
            come = []
            if last >= 0 and order[last] == "z":
                come.append(("z", 1 if rel["z"] < 0 else -1))
            for d in order[last + 1 :]:
                come += [("z", 1), ("z", -1)] if d == "z" else [(d, 1)]
            return come

        def fetch(i, owner):
            start, rows, order = parts[i]
            mine = pl.ds(pl.multiple_of(owner * self.rows + start, 16), rows)
            return pltpu.make_async_copy(
                src.at[pl.ds(self.place(owner, start), rows)], own.at[mine], own_sem.at[i, owner]
            )

        def begin(i, rel, last):
            if coming(i, rel, last):
                cond, owner = at.owner(rel)
                maybe(cond, fetch(i, owner).start)

        def tiles(rows, body):
            def step(r, carry):
                body(r * 16)
                return carry

            lax.fori_loop(0, rows // 16, step, 0)

        def tile(start, r):
            return pl.ds(pl.multiple_of(start + r, 16), 16)

        def work(i, rel, last):
            start, rows, order = parts[i]
            cond, owner = at.owner(rel)
            come = coming(i, rel, last)
            first = owner * self.rows + start
            mine = pl.ds(pl.multiple_of(first, 16), rows)

            def arrived(d, way, add):
                ok = at.peers[(d, way)][1]
                got = self.held_rows(i, d, owner, at.z, way < 0)

                def take():
                    there = held.at[got]
                    pltpu.make_async_copy(there, there, recv_sem.at[i, SLOT[(d, way)], owner]).wait()
                    tiles(rows, lambda r: add(r, tile(got.start, r)))

                maybe(ok, take)

            def add_on(r, got):
                to = tile(first, r)
                own[to] = (own[to].astype(jnp.float32) + held[got].astype(jnp.float32)).astype(
                    self.dtype
                )

            def add_last(r, got):
                to = tile(start, r)
                out[to] = out[to] + held[got].astype(jnp.float32)

            def keep(r):
                out[tile(start, r)] = own[tile(first, r)].astype(jnp.float32)

            def take_all():
                fetch(i, owner).wait()
                if last < 0:
                    tiles(rows, keep)
                for d, way in come:
                    arrived(d, way, add_last if last < 0 else add_on)

            if come:
                maybe(cond, take_all)
            if last >= 0:
                d = order[last]
                way = 1 if d != "z" or rel["z"] > 0 else -1
                peer, ok = at.peers[(d, way)]
                there = self.held_rows(i, d, owner, at.z + (way if d == "z" else 0), way > 0)
                copy = pltpu.make_async_remote_copy(
                    src_ref=own.at[mine] if come else src.at[pl.ds(self.place(owner, start), rows)],
                    dst_ref=held.at[there],
                    send_sem=send_sem.at[i, SLOT[(d, way)], owner],
                    recv_sem=recv_sem.at[i, SLOT[(d, -way if d == "z" else 1)], owner],
                    device_id={"ctx": peer},
                    device_id_type=MESH,
                )
                maybe(cond, copy.start)
                sent.append((cond, copy))

        def end():
            for cond, copy in sent:
                maybe(cond, copy.wait_send)

        for i, part in enumerate(parts):
            for rel, last, hops in offsets(n, part[2]):
                events.append((-1, functools.partial(begin, i, rel, last)))
                events.append((lines + 2 - hops, functools.partial(work, i, rel, last)))
        events.append((1000, end))
        return events


class Exchange:
    peers = "all"

    def __init__(self, rows, cols, dtype, spread=False):
        self.rows, self.cols, self.dtype, self.spread = rows, cols, dtype, spread

    def setup(self, n, cores):
        self.n, self.cores = n, cores
        shape = (n, cores, self.rows, self.cols) if self.spread else (n, self.rows, self.cols)
        self.out = jax.ShapeDtypeStruct(shape, self.dtype)
        self.out_spec = pl.BlockSpec(memory_space=pl.ANY)
        self.scratch = [
            pltpu.SemaphoreType.DMA((n,)),
            pltpu.SemaphoreType.DMA((n,)),
            pltpu.SemaphoreType.DMA((1,)),
        ]
        if self.spread:
            self.scratch += [pltpu.SemaphoreType.DMA((n, cores))] * 2

    def events(self, at, src, out, send_sem, recv_sem, own_sem, *pair_sems):
        n, cores = self.n, self.cores
        sent, kept, events = [], [], []

        def there(owner):
            return out.at[owner, at.f] if self.spread else out.at[owner]

        def share(owner, first):
            for k in range(1, cores):
                core = lax.rem(at.f + k, cores)
                copy = pltpu.make_async_remote_copy(
                    src_ref=src.at[owner] if first else there(owner),
                    dst_ref=there(owner),
                    send_sem=pair_sems[0].at[owner, core],
                    recv_sem=pair_sems[1].at[owner, at.f],
                    device_id={"fsdp": core},
                    device_id_type=MESH,
                )
                copy.start()
                sent.append(copy)

        def begin():
            for k in range(1, n):
                peer = lax.rem(at.c + k, n)
                copy = pltpu.make_async_remote_copy(
                    src_ref=src.at[peer],
                    dst_ref=there(at.c),
                    send_sem=send_sem.at[peer],
                    recv_sem=recv_sem.at[at.c],
                    device_id={"ctx": peer},
                    device_id_type=MESH,
                )
                copy.start()
                sent.append(copy)
            copy = pltpu.make_async_copy(src.at[at.c], there(at.c), own_sem.at[0])
            copy.start()
            kept.append(copy)
            if self.spread:
                share(at.c, True)

        def arrive(k):
            owner = lax.rem(at.c + k, n)
            block = there(owner)
            pltpu.make_async_copy(block, block, recv_sem.at[owner]).wait()
            if self.spread:
                share(owner, False)

        def end():
            if self.spread:
                for owner in range(n):
                    for k in range(1, cores):
                        core = lax.rem(at.f + k, cores)
                        block = out.at[owner, core]
                        pltpu.make_async_copy(block, block, pair_sems[1].at[owner, core]).wait()
            for copy in sent:
                copy.wait_send()
            for copy in kept:
                copy.wait()

        events.append((-1, begin))
        for k in range(1, n):
            events.append((100 + k, functools.partial(arrive, k)))
        events.append((1000, end))
        return events


def communicate(name, number, n, cores, ops, arrays):
    for op in ops:
        op.setup(n, cores)
    everyone = any(op.peers == "all" for op in ops)
    spread = any(getattr(op, "spread", False) for op in ops)

    def kernel(*refs):
        at = Place(n, cores)
        k = len(ops)
        barrier = pltpu.get_barrier_semaphore()
        if everyone:
            for j in range(1, n):
                pl.semaphore_signal(
                    barrier, 1, device_id={"ctx": lax.rem(at.c + j, n)}, device_id_type=MESH
                )
            count = n - 1
        else:
            for peer, ok in at.peers.values():
                maybe(
                    ok,
                    lambda peer=peer: pl.semaphore_signal(
                        barrier, 1, device_id={"ctx": peer}, device_id_type=MESH
                    ),
                )
            count = 2 + (at.z > 0).astype(jnp.int32) + (at.z < at.lines - 1).astype(jnp.int32)
        if spread:
            for j in range(1, cores):
                pl.semaphore_signal(
                    barrier, 1, device_id={"fsdp": lax.rem(at.f + j, cores)}, device_id_type=MESH
                )
            count = count + cores - 1
        pl.semaphore_wait(barrier, count)
        events, first = [], 2 * k
        for number_, op in enumerate(ops):
            mine = refs[first : first + len(op.scratch)]
            first += len(op.scratch)
            events += op.events(at, refs[number_], refs[k + number_], *mine)
        for _, event in sorted(events, key=lambda e: e[0]):
            event()

    return pl.pallas_call(
        kernel,
        out_shape=[op.out for op in ops],
        in_specs=[pl.BlockSpec(memory_space=pl.ANY)] * len(ops),
        out_specs=[op.out_spec for op in ops],
        scratch_shapes=[s for op in ops for s in op.scratch],
        compiler_params=pltpu.CompilerParams(
            collective_id=number, has_side_effects=True, vmem_limit_bytes=48 << 20
        ),
        name=name,
    )(*arrays)


def doc_index(starts, positions):
    return jnp.sum((positions[:, None] >= starts[None, :]).astype(jnp.int32), axis=1) - 1


def rope_tables(positions):
    half = ROPE // 2
    frequency = THETA ** (-jnp.arange(half, dtype=jnp.float32) / half)
    angles = positions.astype(jnp.float32)[:, None] * frequency[None, :]
    return (jnp.cos(angles), jnp.sin(angles))


def rotate_pairs(values, cosines, sines):
    half = values.shape[-1] // 2
    first = values[..., :half]
    second = values[..., half:]
    return jnp.concatenate(
        [first * cosines - second * sines, second * cosines + first * sines], axis=-1
    )


def rms_forward(values, gain):
    factor = lax.rsqrt(jnp.mean(values * values, axis=-1, keepdims=True) + EPS)
    normal = values * factor
    return (normal * gain, normal, factor)


def rms_backward(grad_out, normal, factor, gain):
    scaled = grad_out * gain
    grad_in = factor * (scaled - normal * jnp.mean(scaled * normal, axis=-1, keepdims=True))
    return (grad_in, jnp.sum(grad_out * normal, axis=0))


def silu_parts(values):
    sigmoid = jax.nn.sigmoid(values)
    return (values * sigmoid, sigmoid * (1.0 + values * (1.0 - sigmoid)))


def dot(left, right):
    return jnp.dot(left, right, preferred_element_type=jnp.float32)


def dot_t(left, right):
    return lax.dot_general(left, right, (((1,), (1,)), ((), ())), preferred_element_type=jnp.float32)


def t_dot(left, right):
    return lax.dot_general(left, right, (((0,), (0,)), ((), ())), preferred_element_type=jnp.float32)


def two_parts(values):
    high = lax.reduce_precision(values, 8, 7)
    return high.astype(jnp.bfloat16), (values - high).astype(jnp.bfloat16)


def padded(values, columns):
    short = -values.shape[-1] % columns
    if not short:
        return values
    return jnp.pad(values, [(0, 0)] * (values.ndim - 1) + [(0, short)])


def shards(
    tokens,
    cotangent,
    doc_starts,
    routes,
    attn_gain,
    q_weight,
    kva_weight,
    kv_gain,
    kvb_weight,
    o_weight,
    ffn_gain,
    router_weight,
    shared_gate,
    shared_up,
    shared_down,
    expert_gate,
    expert_up,
    expert_down,
):
    low = jnp.bfloat16
    wide = jnp.float32
    n, cores = lax.axis_size("ctx"), lax.axis_size("fsdp")
    here = lax.axis_index("ctx")
    t = tokens.shape[1]
    half = t // 2
    seq = n * t
    ws = q_weight.shape[0]
    kr = kvb_weight.shape[0]
    copies = n // HEADS
    shared = shared_gate.shape[1]
    w = shared // n
    picks_count = routes.shape[2]
    capacity = 10 * t * picks_count // (7 * n)
    slots_count = -(-capacity // 8) * 8
    scale = HEAD ** (-0.5)
    starts = doc_starts[0]

    def run(name, number, ops, arrays):
        return communicate(name, number, n, cores, ops, arrays)

    def by_position(owner, start):
        if start < half:
            return pl.multiple_of(owner * half + start, 16)
        return pl.multiple_of((2 * n - 1 - owner) * half + start - half, 16)

    def by_row(rows):
        return lambda owner, start: pl.multiple_of(owner * rows + start, 16)

    def to_owners(values):
        columns = values.shape[-1]
        pair = values.reshape(2, n, half, columns)
        return jnp.concatenate([pair[0], pair[1][::-1]], axis=1)

    def to_positions(values):
        columns = values.shape[-1]
        return jnp.concatenate(
            [
                values[:, :half].reshape(n * half, columns),
                values[::-1, half:].reshape(n * half, columns),
            ]
        )

    small = jnp.concatenate(
        [
            kva_weight,
            router_weight,
            attn_gain[:, None],
            ffn_gain[:, None],
            jnp.pad(kv_gain, (0, ws - kr))[:, None],
        ],
        axis=1,
    ).astype(low)
    small = lax.all_gather(padded(small, 128), ("ctx", "fsdp"), axis=0, tiled=True)
    first = RANK + ROPE
    kva_full = small[:, :first]
    router_full = small[:, first : first + n]
    gain_one = small[:, first + n].astype(wide)
    gain_two = small[:, first + n + 1].astype(wide)
    gain_latent = small[:, first + n + 2].reshape(n * cores, ws)[:, :kr].reshape(-1).astype(wide)

    head_part = jnp.concatenate(
        [
            q_weight.astype(low).reshape(ws, HEADS, HEAD).transpose(1, 0, 2),
            kvb_weight.astype(low)
            .reshape(kr, HEADS, KV)
            .transpose(1, 0, 2)
            .reshape(HEADS, ws, kr * KV // ws),
        ],
        axis=-1,
    )
    if copies > 1:
        head_part = jnp.repeat(head_part, copies, axis=0)
    head_columns = head_part.shape[-1]
    shared_part = padded(
        jnp.concatenate(
            [
                v.astype(low).reshape(ws, n, w)
                for v in (shared_gate, shared_up, jnp.transpose(shared_down))
            ],
            axis=-1,
        ).transpose(1, 0, 2),
        128,
    )
    shared_columns = shared_part.shape[-1]

    inputs_all, head_all = run(
        "gather_tokens",
        0,
        [Gather(t, D, low, by_position), Exchange(ws, head_columns, low, True)],
        [tokens[0], head_part],
    )
    out_proj = lax.all_gather(o_weight.astype(low), ("ctx", "fsdp"), axis=1, tiled=True)
    picks_all = lax.all_gather(routes[0], "ctx", axis=0, tiled=True)
    (shared_all,) = run(
        "shared_weights",
        1,
        [Exchange(ws, shared_columns, low, True)],
        [lax.optimization_barrier((shared_part, inputs_all))[0]],
    )
    grad_low = cotangent[0]
    grad = grad_low.astype(wide)
    grad_all = lax.all_gather(grad_low, "ctx", axis=0, tiled=True)
    query_proj = lax.all_gather(q_weight.astype(low), ("ctx", "fsdp"), axis=0, tiled=True)
    experts = (
        lax.all_gather(expert_gate[0].astype(low), "fsdp", axis=0, tiled=True),
        lax.all_gather(expert_up[0].astype(low), "fsdp", axis=0, tiled=True),
        lax.all_gather(expert_down[0].astype(low), "fsdp", axis=1, tiled=True),
    )

    head_all = head_all.reshape(D, head_columns)
    q_head = head_all[:, :HEAD]
    kvb_head = head_all[:, HEAD:].reshape(RANK, KV)
    shared_all = shared_all.reshape(D, shared_columns)
    gate_cols, up_cols, down_rows = (shared_all[:, i * w : (i + 1) * w] for i in range(3))

    positions = jnp.arange(seq, dtype=jnp.int32)
    cosines, sines = rope_tables(positions)
    normed_all = rms_forward(inputs_all.astype(wide), gain_one)[0].astype(low)
    query_raw = dot(normed_all, q_head)
    queries = jnp.concatenate(
        [query_raw[:, :NOPE], rotate_pairs(query_raw[:, NOPE:], cosines, sines)], axis=-1
    ).astype(low)
    compressed = dot(normed_all, kva_full)
    latent_all = rms_forward(compressed[:, :RANK], gain_latent)[0].astype(low)
    rope_all = rotate_pairs(compressed[:, RANK:], cosines, sines).astype(low)
    kv_head = dot(latent_all, kvb_head).astype(low)
    keys = jnp.concatenate([kv_head[:, :NOPE], rope_all], axis=-1)
    values = kv_head[:, NOPE:]
    documents = doc_index(starts, positions)
    query_pos, query_cos, query_sin, query_doc = positions, cosines, sines, documents

    def queries_here(rows):
        if copies == 1:
            return rows
        if rows.ndim == 1:
            return queries_here(rows[:, None])[:, 0]
        blocks = to_owners(rows).reshape(n // copies, copies, t, rows.shape[-1])
        return lax.dynamic_index_in_dim(blocks, here % copies, 1, False).reshape(-1, rows.shape[-1])

    def queries_back(rows):
        if copies == 1:
            return to_owners(rows)
        blocks = rows.reshape(n // copies, 1, t, rows.shape[-1])
        mine = (jnp.arange(copies) == here % copies)[None, :, None, None]
        return jnp.where(mine, blocks, jnp.zeros((), rows.dtype)).reshape(n, t, rows.shape[-1])

    def of_heads(blocks):
        columns = blocks.shape[-1]
        if copies > 1:
            blocks = blocks.reshape(HEADS, copies, t, columns)
            blocks = jnp.sum(blocks.astype(wide), axis=1).astype(blocks.dtype)
        return blocks.transpose(1, 0, 2).reshape(t, HEADS * columns)

    queries, query_pos, query_doc = (queries_here(v) for v in (queries, query_pos, query_doc))
    query_cos, query_sin = queries_here(query_cos), queries_here(query_sin)
    allowed = (query_doc[:, None] == documents[None, :]) & (
        positions[None, :] <= query_pos[:, None]
    )
    scores = jnp.where(allowed, scale * dot_t(queries, keys), NEG)
    peak = jnp.max(scores, axis=-1, keepdims=True)
    total = jnp.sum(jnp.exp(scores - peak), axis=-1, keepdims=True)
    log_total = peak + jnp.log(total)
    probs_low = jnp.exp(scores - log_total).astype(low)
    attended = dot(probs_low, values)

    (attn_blocks,) = run(
        "attended", 2, [Exchange(t, VDIM, low)], [queries_back(attended.astype(low))]
    )
    attn_values = of_heads(attn_blocks)

    inputs = tokens[0].astype(wide)
    normed_one, normal_one, factor_one = rms_forward(inputs, gain_one)
    normed_low = normed_one.astype(low)
    resid = inputs + dot(attn_values, out_proj)
    normed_two, normal_two, factor_two = rms_forward(resid, gain_two)
    ffn_in = normed_two.astype(low)

    (ffn_all,) = run("gather_ffn", 3, [Gather(t, D, low, by_row(t))], [ffn_in])

    chosen = jnp.any(
        picks_all[:, :, None] == jnp.arange(n, dtype=jnp.int32)[None, None, :], axis=1
    )
    logits = jnp.where(chosen, dot(ffn_all, router_full), NEG)
    shifted = jnp.where(chosen, jnp.exp(logits - jnp.max(logits, axis=-1, keepdims=True)), 0.0)
    gates_all = shifted / jnp.sum(shifted, axis=-1, keepdims=True)
    gate_here = lax.dynamic_index_in_dim(gates_all, here, 1, False).reshape(n, t)
    taken = lax.dynamic_index_in_dim(chosen, here, 1, False).reshape(n, t)
    slots = jnp.where(taken, jnp.cumsum(taken.astype(jnp.int32), axis=1) - 1, -1)
    onehot = slots[:, None, :] == jnp.arange(slots_count, dtype=jnp.int32)[None, :, None]
    onehot_low = onehot.astype(low)
    rows = n * slots_count

    def to_slots(values):
        return (
            jnp.einsum(
                "nst,ntd->nsd", onehot_low, values.reshape(n, t, D), preferred_element_type=wide
            )
            .astype(low)
            .reshape(rows, D)
        )

    def to_rows(values):
        return jnp.einsum(
            "nst,nsd->ntd", onehot_low, values.reshape(n, slots_count, D), preferred_element_type=wide
        ).reshape(seq, D)

    row_gate = jnp.sum(jnp.where(onehot, gate_here[:, None, :], 0.0), axis=2).reshape(rows, 1)
    arrived = to_slots(ffn_all)
    arrived_grad = to_slots(grad_all)
    pre_gate = dot(arrived, experts[0])
    pre_up = dot(arrived, experts[1])
    expert_act, expert_slope = silu_parts(pre_gate)
    expert_hidden = (expert_act * pre_up).astype(low)
    expert_result = dot(expert_hidden, experts[2]).astype(low)
    pick_grad = (row_gate * arrived_grad.astype(wide)).astype(low)
    row_gate_grad = jnp.sum(expert_result.astype(wide) * arrived_grad.astype(wide), axis=-1)
    gate_grad_here = jnp.sum(
        jnp.where(onehot, row_gate_grad.reshape(n, slots_count, 1), 0.0), axis=1
    )

    shared_pre_gate = dot(ffn_all, gate_cols)
    shared_pre_up = dot(ffn_all, up_cols)
    shared_act, shared_slope = silu_parts(shared_pre_gate)
    shared_hidden = (shared_act * shared_pre_up).astype(low)
    out_part = (
        gate_here.reshape(seq, 1) * to_rows(expert_result) + dot_t(shared_hidden, down_rows)
    ).astype(low)

    shared_hidden_grad = dot(grad_all, down_rows)
    shared_gate_low = (shared_hidden_grad * shared_pre_up * shared_slope).astype(low)
    shared_up_low = (shared_hidden_grad * shared_act).astype(low)

    hidden_grad = dot_t(pick_grad, experts[2])
    pre_gate_grad = (hidden_grad * pre_up * expert_slope).astype(low)
    pre_up_grad = (hidden_grad * expert_act).astype(low)
    row_grad = (dot_t(pre_gate_grad, experts[0]) + dot_t(pre_up_grad, experts[1])).astype(low)
    ffn_part = (
        to_rows(row_grad) + dot_t(shared_gate_low, gate_cols) + dot_t(shared_up_low, up_cols)
    ).astype(low)

    ffn_in_grad, gate_blocks = run(
        "reduce_ffn",
        4,
        [Reduce(t, D, by_row(t)), Exchange(8, t, wide)],
        [ffn_part, jnp.pad(gate_grad_here[:, None, :], ((0, 0), (0, 7), (0, 0)))],
    )
    routed = lax.psum_scatter(out_part, "ctx", scatter_dimension=0, tiled=True)
    output = (resid + routed.astype(wide)).astype(low)

    out_w_grad = t_dot(expert_hidden, pick_grad)
    in_gate_grad = t_dot(arrived, pre_gate_grad)
    in_up_grad = t_dot(arrived, pre_up_grad)
    expert_grads = (
        lax.psum_scatter(in_gate_grad.astype(low), "fsdp", scatter_dimension=0, tiled=True),
        lax.psum_scatter(in_up_grad.astype(low), "fsdp", scatter_dimension=0, tiled=True),
        lax.psum_scatter(out_w_grad.astype(low), "fsdp", scatter_dimension=1, tiled=True),
    )
    shared_grads = padded(
        jnp.concatenate(
            [
                t_dot(ffn_all, shared_gate_low),
                t_dot(ffn_all, shared_up_low),
                t_dot(grad_all, shared_hidden),
            ],
            axis=1,
        ).astype(low),
        128,
    ).reshape(n, cores, ws, shared_columns)
    shared_grads = lax.psum_scatter(shared_grads, "fsdp", scatter_dimension=1, tiled=True)[:, 0]

    gates = lax.dynamic_slice_in_dim(gates_all, here * t, t, 0)
    gate_grad = jnp.transpose(gate_blocks[:, 0, :])
    mixed = jnp.sum(gates * gate_grad, axis=-1, keepdims=True)
    logit_grad = (gates * (gate_grad - mixed)).astype(low)
    router_grad = t_dot(ffn_in, logit_grad)
    ffn_in_grad = ffn_in_grad + dot_t(logit_grad, router_full)
    resid_part, gain_two_grad = rms_backward(ffn_in_grad, normal_two, factor_two, gain_two)
    resid_grad = grad + resid_part
    attn_grad_low = resid_grad.astype(low)
    grad_attended = dot_t(attn_grad_low, out_proj).astype(low)
    grad_blocks = grad_attended.reshape(t, HEADS, VDIM).transpose(1, 0, 2)
    if copies > 1:
        grad_blocks = jnp.repeat(grad_blocks, copies, axis=0)
    (grad_att_blocks,) = run("grad_attended", 5, [Exchange(t, VDIM, low)], [grad_blocks])
    out_proj_grad = t_dot(attn_values, attn_grad_low).astype(low)
    out_proj_grad = lax.psum_scatter(
        out_proj_grad, ("ctx", "fsdp"), scatter_dimension=1, tiled=True
    )

    grad_att = queries_here(to_positions(grad_att_blocks))
    delta = jnp.sum(grad_att.astype(wide) * attended, axis=-1, keepdims=True)
    probs = jnp.exp(scores - log_total)
    grad_probs = dot_t(grad_att, values)
    grad_scores = (probs * (grad_probs - delta)).astype(low)
    value_grad = t_dot(probs_low, grad_att)
    key_grad = t_dot(grad_scores, queries) * scale
    query_grad = (dot(grad_scores, keys) * scale).astype(low).astype(wide)
    raw_grad = jnp.concatenate(
        [query_grad[:, :NOPE], rotate_pairs(query_grad[:, NOPE:], query_cos, -query_sin)], axis=-1
    ).astype(low)
    kv_grad = jnp.concatenate([key_grad[:, :NOPE], value_grad], axis=-1)
    kv_high, kv_rest = two_parts(kv_grad)
    latent_part = dot_t(kv_high, kvb_head) + dot_t(kv_rest, kvb_head)
    latent_part = padded(jnp.concatenate([latent_part, key_grad[:, NOPE:]], axis=1).astype(low), 128)
    query_blocks, latent_sum = run(
        "reduce_latent",
        6,
        [Exchange(t, 2 * NOPE, low), Reduce(t, latent_part.shape[1], by_position)],
        [padded(queries_back(raw_grad), 2 * NOPE), latent_part],
    )
    up_latent_grad = t_dot(latent_all, kv_high) + t_dot(latent_all, kv_rest)
    query_proj_grad = t_dot(queries_here(normed_all), raw_grad)
    head_grads = jnp.concatenate(
        [query_proj_grad, up_latent_grad.reshape(D, head_columns - HEAD)], axis=1
    ).astype(low)
    head_grads = lax.psum_scatter(
        head_grads.reshape(n, cores, ws, head_columns), "fsdp", scatter_dimension=1, tiled=True
    )[:, 0]

    compressed_here = dot(normed_low, kva_full)
    unused, latent_normal, latent_factor = rms_forward(compressed_here[:, :RANK], gain_latent)
    my_rows = jnp.arange(t, dtype=jnp.int32)
    my_positions = jnp.where(
        my_rows < half, here * half + my_rows, (2 * n - 1 - here) * half + my_rows - half
    )
    my_cosines, my_sines = rope_tables(my_positions)
    comp_latent_grad, gain_latent_grad = rms_backward(
        latent_sum[:, :RANK], latent_normal, latent_factor, gain_latent
    )
    rope_sum = latent_sum[:, RANK : RANK + ROPE].astype(low).astype(wide)
    rope_back = rotate_pairs(rope_sum, my_cosines, -my_sines)
    comp_grad = jnp.concatenate([comp_latent_grad, rope_back], axis=-1).astype(low)
    raw_here = of_heads(query_blocks[:, :, :HEAD])
    normed_grad = dot_t(raw_here, query_proj) + dot_t(comp_grad, kva_full)
    input_part, gain_one_grad = rms_backward(normed_grad, normal_one, factor_one, gain_one)
    input_grad = (resid_grad + input_part).astype(low)

    down_latent_grad = t_dot(normed_low, comp_grad)
    latent_column = jnp.pad(gain_latent_grad.reshape(n * cores, kr), ((0, 0), (0, ws - kr)))
    small_grads = padded(
        jnp.concatenate(
            [
                down_latent_grad,
                router_grad,
                gain_one_grad[:, None],
                gain_two_grad[:, None],
                latent_column.reshape(D, 1),
            ],
            axis=1,
        ).astype(low),
        128,
    )
    small_columns = small_grads.shape[1]
    small_grads = lax.psum_scatter(
        small_grads.reshape(n, cores, ws, small_columns), "fsdp", scatter_dimension=1, tiled=True
    ).reshape(n * ws, small_columns)
    head_blocks, shared_blocks, small_sum = run(
        "weight_grads",
        7,
        [
            Exchange(ws, head_columns, low),
            Exchange(ws, shared_columns, low),
            Reduce(ws, small_columns, by_row(ws)),
        ],
        [head_grads, shared_grads, small_grads],
    )
    head_sum = jnp.sum(
        head_blocks.astype(wide).reshape(HEADS, copies, ws, head_columns), axis=1
    )
    q_weight_grad = head_sum[:, :, :HEAD].transpose(1, 0, 2).reshape(ws, HEADS * HEAD)
    kvb_weight_grad = (
        head_sum[:, :, HEAD:].reshape(HEADS, kr, KV).transpose(1, 0, 2).reshape(kr, HEADS * KV)
    )
    shared_out = [
        shared_blocks[:, :, i * w : (i + 1) * w]
        .transpose(1, 0, 2)
        .reshape(ws, shared)
        .astype(wide)
        for i in range(3)
    ]
    return (
        output[None],
        input_grad[None],
        small_sum[:, first + n],
        q_weight_grad,
        small_sum[:, :first],
        small_sum[:kr, first + n + 2],
        kvb_weight_grad,
        out_proj_grad.astype(wide),
        small_sum[:, first + n + 1],
        small_sum[:, first : first + n],
        shared_out[0],
        shared_out[1],
        jnp.transpose(shared_out[2]),
        expert_grads[0][None].astype(wide),
        expert_grads[1][None].astype(wide),
        expert_grads[2][None].astype(wide),
    )


def solution(mesh):
    return jax.shard_map(
        shards,
        mesh=mesh,
        in_specs=(
            P("fsdp", "ctx", None),
            P("fsdp", "ctx", None),
            P("fsdp", None),
            P("fsdp", "ctx", None),
            P(("ctx", "fsdp")),
            P(("ctx", "fsdp"), None),
            P(("ctx", "fsdp"), None),
            P(("ctx", "fsdp")),
            P(("ctx", "fsdp"), None),
            P(None, ("ctx", "fsdp")),
            P(("ctx", "fsdp")),
            P(("ctx", "fsdp"), None),
            P(("ctx", "fsdp"), None),
            P(("ctx", "fsdp"), None),
            P(None, ("ctx", "fsdp")),
            P("ctx", "fsdp", None),
            P("ctx", "fsdp", None),
            P("ctx", None, "fsdp"),
        ),
        out_specs=(
            P("fsdp", "ctx", None),
            P("fsdp", "ctx", None),
            P(("ctx", "fsdp")),
            P(("ctx", "fsdp"), None),
            P(("ctx", "fsdp"), None),
            P(("ctx", "fsdp")),
            P(("ctx", "fsdp"), None),
            P(None, ("ctx", "fsdp")),
            P(("ctx", "fsdp")),
            P(("ctx", "fsdp"), None),
            P(("ctx", "fsdp"), None),
            P(("ctx", "fsdp"), None),
            P(None, ("ctx", "fsdp")),
            P("ctx", "fsdp", None),
            P("ctx", "fsdp", None),
            P("ctx", None, "fsdp"),
        ),
        check_vma=False,
    )
```

```python
import functools

import jax
import jax.numpy as jnp
from jax import lax
from jax.experimental import pallas as pl
from jax.experimental.pallas import tpu as pltpu
from jax.sharding import PartitionSpec as P

D = 2048
HEADS = 16
NOPE = 128
ROPE = 64
VDIM = 128
RANK = 512
HEAD = NOPE + ROPE
KV = NOPE + VDIM

EPS = 1e-06
THETA = 10000.0
NEG = -1e30
MESH = pl.DeviceIdType.MESH

ZXY, ZYX = ("z", "x", "y"), ("z", "y", "x")
XYZ, YXZ = ("x", "y", "z"), ("y", "x", "z")


def pieces(rows):
    if rows == 128:
        return (
            (0, 32, ZXY),
            (32, 32, ZYX),
            (64, 16, ZXY),
            (80, 16, ZYX),
            (96, 16, XYZ),
            (112, 16, YXZ),
        )
    if rows == 64:
        return ((0, 32, ZXY), (32, 16, ZYX), (48, 16, YXZ))
    if rows % 32 == 0:
        return ((0, rows // 2, ZXY), (rows // 2, rows // 2, ZYX))
    return ((0, rows, ZXY),)


def maybe(cond, fn):
    if cond is None:
        fn()
    else:
        pl.when(cond)(fn)


def both(first, second):
    if first is None:
        return second
    if second is None:
        return first
    return jnp.logical_and(first, second)


class Place:
    def __init__(self, n, cores):
        self.n, self.cores, self.lines = n, cores, n // 4
        self.c, self.f = lax.axis_index("ctx"), lax.axis_index("fsdp")
        self.z, self.y, self.x = self.split(self.c)
        z, y, x, top = self.z, self.y, self.x, self.lines - 1
        self.peers = {
            ("z", 1): (self.index(jnp.minimum(z + 1, top), y, x), z < top),
            ("z", -1): (self.index(jnp.maximum(z - 1, 0), y, x), z > 0),
            ("y", 1): (self.index(z, 1 - y, x), None),
            ("x", 1): (self.index(z, y, 1 - x), None),
        }

    @staticmethod
    def split(c):
        return c // 4, (c // 2) % 2, c % 2

    @staticmethod
    def index(z, y, x):
        return z * 4 + y * 2 + x

    def owner(self, rel):
        oz = self.z + rel["z"]
        cond = None if rel["z"] == 0 else (oz >= 0) & (oz < self.lines)
        oz = jnp.clip(oz, 0, self.lines - 1)
        oy = 1 - self.y if rel["y"] else self.y
        ox = 1 - self.x if rel["x"] else self.x
        return cond, self.index(oz, oy, ox)


SLOT = {("z", 1): 0, ("z", -1): 1, ("y", 1): 2, ("x", 1): 3}


def offsets(n, order):
    lines = n // 4
    found = []
    for a in range(1 - lines, lines):
        for y in range(2):
            for x in range(2):
                rel = {"z": a, "y": y, "x": x}
                used = [k for k, d in enumerate(order) if rel[d] != 0]
                found.append((rel, used[-1] if used else -1, abs(a) + y + x))
    return found


class Gather:
    peers = "near"

    def __init__(self, rows, cols, dtype, place, spread=False):
        self.rows, self.cols, self.dtype, self.place = rows, cols, dtype, place
        self.spread = spread

    def setup(self, n, cores):
        self.n, self.cores, self.parts = n, cores, pieces(self.rows)
        k = len(self.parts)
        count = n * cores if self.spread else n
        self.out = jax.ShapeDtypeStruct((count * self.rows, self.cols), self.dtype)
        self.out_spec = pl.BlockSpec(memory_space=pl.ANY)
        self.scratch = [
            pltpu.SemaphoreType.DMA((k, 4, n)),
            pltpu.SemaphoreType.DMA((k, n)),
            pltpu.SemaphoreType.DMA((k,)),
        ]
        if self.spread:
            self.scratch += [pltpu.SemaphoreType.DMA((k, n, cores))] * 2

    def events(self, at, src, out, send_sem, recv_sem, own_sem, *pair_sems):
        n, cores, parts = self.n, self.cores, self.parts
        sent, kept, events = [], [], []

        def rows_of(i, owner, core=None):
            if self.spread:
                owner = owner * cores + (at.f if core is None else core)
            return pl.ds(self.place(owner, parts[i][0]), parts[i][1])

        def pair_copy(i, rel, k):
            cond, owner = at.owner(rel)
            core = lax.rem(at.f + k, cores)
            there = out.at[rows_of(i, owner)]
            here = src.at[pl.ds(parts[i][0], parts[i][1])]
            return cond, pltpu.make_async_remote_copy(
                src_ref=there if any(rel.values()) else here,
                dst_ref=there,
                send_sem=pair_sems[0].at[i, owner, core],
                recv_sem=pair_sems[1].at[i, owner, at.f],
                device_id={"fsdp": core},
                device_id_type=MESH,
            )

        def go(make):
            cond, copy = make()
            maybe(cond, copy.start)
            sent.append(make)

        def share(i, rel):
            for k in range(1, cores):
                go(functools.partial(pair_copy, i, rel, k))

        def link_copy(i, rel, key):
            cond, owner = at.owner(rel)
            peer, ok = at.peers[key]
            there = out.at[rows_of(i, owner)]
            here = src.at[pl.ds(parts[i][0], parts[i][1])]
            return both(cond, ok), pltpu.make_async_remote_copy(
                src_ref=there if any(rel.values()) else here,
                dst_ref=there,
                send_sem=send_sem.at[i, SLOT[key], owner],
                recv_sem=recv_sem.at[i, owner],
                device_id={"ctx": peer},
                device_id_type=MESH,
            )

        def onward(i, rel, last):
            order = parts[i][2]
            keys = []
            if last >= 0 and order[last] == "z":
                keys.append(("z", 1 if rel["z"] < 0 else -1))
            for d in order[last + 1 :]:
                keys += [("z", 1), ("z", -1)] if d == "z" else [(d, 1)]
            for key in keys:
                go(functools.partial(link_copy, i, rel, key))

        def begin():
            still = {"z": 0, "y": 0, "x": 0}
            for i in range(len(parts)):
                onward(i, still, -1)
            for i, (start, rows, order) in enumerate(parts):
                copy = pltpu.make_async_copy(
                    src.at[pl.ds(start, rows)], out.at[rows_of(i, at.c)], own_sem.at[i]
                )
                copy.start()
                kept.append(copy)
                if self.spread:
                    share(i, still)

        def arrive(i, rel, last):
            cond, owner = at.owner(rel)
            there = out.at[rows_of(i, owner)]
            maybe(
                cond,
                lambda: pltpu.make_async_copy(there, there, recv_sem.at[i, owner]).wait(),
            )
            onward(i, rel, last)
            if self.spread:
                share(i, rel)

        def end():
            if self.spread:
                for i in range(len(parts)):
                    for owner in range(n):
                        for k in range(1, cores):
                            core = lax.rem(at.f + k, cores)
                            there = out.at[rows_of(i, owner, core)]
                            pltpu.make_async_copy(
                                there, there, pair_sems[1].at[i, owner, core]
                            ).wait()
            for make in sent:
                cond, copy = make()
                maybe(cond, copy.wait_send)
            for copy in kept:
                copy.wait()

        events.append((-1, begin))
        for i, part in enumerate(parts):
            for rel, last, hops in offsets(n, part[2]):
                if last >= 0:
                    events.append((hops, functools.partial(arrive, i, rel, last)))
        events.append((1000, end))
        return events


class Fold:
    def __init__(self, n, cores, rows, cols, dtype):
        self.n, self.cores, self.rows, self.cols, self.dtype = n, cores, rows, cols, dtype
        self.scratch = [
            pltpu.VMEM((cores - 1, n, rows, cols), dtype),
            pltpu.VMEM((n, rows, cols), dtype),
            pltpu.SemaphoreType.DMA((cores,)),
            pltpu.SemaphoreType.DMA((cores,)),
            pltpu.SemaphoreType.DMA((1,)),
        ]

    def events(self, at, src, held, total, send_sem, recv_sem, own_sem):
        cores, sent = self.cores, []

        def begin():
            for k in range(1, cores):
                core = lax.rem(at.f + k, cores)
                copy = pltpu.make_async_remote_copy(
                    src_ref=src.at[:, core],
                    dst_ref=held.at[cores - 1 - k],
                    send_sem=send_sem.at[k],
                    recv_sem=recv_sem.at[cores - k],
                    device_id={"fsdp": core},
                    device_id_type=MESH,
                )
                copy.start()
                sent.append(copy)
            pltpu.make_async_copy(src.at[:, at.f], total, own_sem.at[0]).start()

        def work():
            pltpu.make_async_copy(src.at[:, at.f], total, own_sem.at[0]).wait()
            for k in range(1, cores):
                pltpu.make_async_copy(held.at[k - 1], held.at[k - 1], recv_sem.at[k]).wait()
            tiles = self.rows // 16

            def step(j, carry):
                owner, to = j // tiles, pl.ds(pl.multiple_of(lax.rem(j, tiles) * 16, 16), 16)
                value = total[owner, to].astype(jnp.float32)
                for k in range(cores - 1):
                    value = value + held[k, owner, to].astype(jnp.float32)
                total[owner, to] = value.astype(self.dtype)
                return carry

            lax.fori_loop(0, self.n * tiles, step, 0)
            for copy in sent:
                copy.wait_send()

        return [(-3, begin), (-2, work)]


class Reduce:
    peers = "near"

    def __init__(self, rows, cols, place, fold=False):
        self.rows, self.cols, self.place = rows, cols, place
        self.dtype = jnp.bfloat16
        self.spread = fold

    def setup(self, n, cores):
        self.n, self.parts = n, pieces(self.rows)
        lines, k = n // 4, len(self.parts)
        self.size = {"z": lines, "y": 2, "x": 2}
        self.table, total = [], 0
        for start, rows, order in self.parts:
            entry, ahead = {}, 1
            for d in order:
                entry[d] = total
                total += rows * ahead * (lines + 1 if d == "z" else 1)
                ahead *= self.size[d]
            self.table.append(entry)
        self.out = jax.ShapeDtypeStruct((self.rows, self.cols), jnp.float32)
        self.out_spec = pl.BlockSpec(memory_space=pltpu.VMEM)
        self.scratch = [
            pltpu.VMEM((total, self.cols), self.dtype),
            pltpu.SemaphoreType.DMA((k, 4, n)),
            pltpu.SemaphoreType.DMA((k, 4, n)),
        ]
        if self.spread:
            self.fold = Fold(n, cores, self.rows, self.cols, self.dtype)
            self.scratch += self.fold.scratch
        else:
            self.own_first, own_total = [], 0
            for start, rows, order in self.parts:
                self.own_first.append(own_total)
                own_total += rows * (n if order[2] == "z" else n // 2)
            self.scratch += [
                pltpu.VMEM((own_total, self.cols), self.dtype),
                pltpu.SemaphoreType.DMA((k, n)),
            ]

    def own_rows(self, i, owner, first, count):
        start, rows, order = self.parts[i]
        if self.spread:
            return owner, pl.ds(pl.multiple_of(start + first, 16), count)
        oz, oy, ox = Place.split(owner)
        number = {"z": owner, "y": oz * 2 + ox, "x": oz * 2 + oy}[order[2]]
        at = self.own_first[i] + number * rows + first
        return (pl.ds(pl.multiple_of(at, 16), count),)

    def held_rows(self, i, d, owner, line, up):
        start, rows, order = self.parts[i]
        oz, oy, ox = Place.split(owner)
        have = {"z": oz, "y": oy, "x": ox}
        number = 0
        for e in order[: order.index(d)]:
            number = number * self.size[e] + have[e]
        if d == "z":
            lines = self.size["z"]
            number = number * (lines + 1) + (oz if up else jnp.where(oz == line, lines, oz))
        return pl.ds(pl.multiple_of(self.table[i][d] + number * rows, 16), rows)

    def events(self, at, src, out, held, send_sem, recv_sem, *more):
        n, parts, lines = self.n, self.parts, self.n // 4
        sent, events = [], []
        if self.spread:
            events += self.fold.events(at, src, *more)
            own = more[1]
        else:
            own, own_sem = more

        def coming(i, rel, last):
            order = parts[i][2]
            come = []
            if last >= 0 and order[last] == "z":
                come.append(("z", 1 if rel["z"] < 0 else -1))
            for d in order[last + 1 :]:
                come += [("z", 1), ("z", -1)] if d == "z" else [(d, 1)]
            return come

        def fetch(i, owner):
            start, rows, order = parts[i]
            return pltpu.make_async_copy(
                src.at[pl.ds(self.place(owner, start), rows)],
                own.at[self.own_rows(i, owner, 0, rows)],
                own_sem.at[i, owner],
            )

        def begin(i, rel, last):
            if coming(i, rel, last):
                cond, owner = at.owner(rel)
                maybe(cond, fetch(i, owner).start)

        def tiles(rows, body):
            def step(r, carry):
                body(r * 16)
                return carry

            lax.fori_loop(0, rows // 16, step, 0)

        def tile(start, r):
            return pl.ds(pl.multiple_of(start + r, 16), 16)

        def work(i, rel, last):
            start, rows, order = parts[i]
            cond, owner = at.owner(rel)
            come = coming(i, rel, last)

            def arrived(d, way, add):
                ok = at.peers[(d, way)][1]
                got = self.held_rows(i, d, owner, at.z, way < 0)

                def take():
                    there = held.at[got]
                    pltpu.make_async_copy(there, there, recv_sem.at[i, SLOT[(d, way)], owner]).wait()
                    tiles(rows, lambda r: add(r, tile(got.start, r)))

                maybe(ok, take)

            def add_on(r, got):
                to = self.own_rows(i, owner, r, 16)
                own[to] = (own[to].astype(jnp.float32) + held[got].astype(jnp.float32)).astype(
                    self.dtype
                )

            def add_last(r, got):
                to = tile(start, r)
                out[to] = out[to] + held[got].astype(jnp.float32)

            def keep(r):
                out[tile(start, r)] = own[self.own_rows(i, owner, r, 16)].astype(jnp.float32)

            def take_all():
                if not self.spread:
                    fetch(i, owner).wait()
                if last < 0:
                    tiles(rows, keep)
                for d, way in come:
                    arrived(d, way, add_last if last < 0 else add_on)

            if come:
                maybe(cond, take_all)
            if last >= 0:
                make = functools.partial(link_copy, i, rel, last)
                cond, copy = make()
                maybe(cond, copy.start)
                sent.append(make)

        def link_copy(i, rel, last):
            start, rows, order = parts[i]
            cond, owner = at.owner(rel)
            d = order[last]
            way = 1 if d != "z" or rel["z"] > 0 else -1
            peer, ok = at.peers[(d, way)]
            there = self.held_rows(i, d, owner, at.z + (way if d == "z" else 0), way > 0)
            if coming(i, rel, last) or self.spread:
                mine = own.at[self.own_rows(i, owner, 0, rows)]
            else:
                mine = src.at[pl.ds(self.place(owner, start), rows)]
            return cond, pltpu.make_async_remote_copy(
                src_ref=mine,
                dst_ref=held.at[there],
                send_sem=send_sem.at[i, SLOT[(d, way)], owner],
                recv_sem=recv_sem.at[i, SLOT[(d, -way if d == "z" else 1)], owner],
                device_id={"ctx": peer},
                device_id_type=MESH,
            )

        def end():
            for make in sent:
                cond, copy = make()
                maybe(cond, copy.wait_send)

        for i, part in enumerate(parts):
            for rel, last, hops in offsets(n, part[2]):
                if not self.spread:
                    events.append((-1, functools.partial(begin, i, rel, last)))
                events.append((lines + 2 - hops, functools.partial(work, i, rel, last)))
        events.append((1000, end))
        return events


class Exchange:
    peers = "all"

    def __init__(self, rows, cols, dtype, spread=False, fold=False):
        self.rows, self.cols, self.dtype = rows, cols, dtype
        self.share, self.spread, self.folds = spread, spread or fold, fold

    def setup(self, n, cores):
        self.n, self.cores = n, cores
        shape = (n, cores, self.rows, self.cols) if self.share else (n, self.rows, self.cols)
        self.out = jax.ShapeDtypeStruct(shape, self.dtype)
        self.out_spec = pl.BlockSpec(memory_space=pl.ANY)
        self.scratch = [
            pltpu.SemaphoreType.DMA((n,)),
            pltpu.SemaphoreType.DMA((n,)),
            pltpu.SemaphoreType.DMA((1,)),
        ]
        if self.share:
            self.scratch += [pltpu.SemaphoreType.DMA((n, cores))] * 2
        if self.folds:
            self.fold = Fold(n, cores, self.rows, self.cols, self.dtype)
            self.scratch += self.fold.scratch

    def events(self, at, src, out, send_sem, recv_sem, own_sem, *more):
        n, cores = self.n, self.cores
        sent, kept, events = [], [], []
        pair_sems = more[:2]
        if self.folds:
            events += self.fold.events(at, src, *more)
            src = more[1]

        def there(owner):
            return out.at[owner, at.f] if self.share else out.at[owner]

        def pair_copy(k, step):
            owner, core = lax.rem(at.c + step, n), lax.rem(at.f + k, cores)
            return pltpu.make_async_remote_copy(
                src_ref=there(owner) if step else src.at[owner],
                dst_ref=there(owner),
                send_sem=pair_sems[0].at[owner, core],
                recv_sem=pair_sems[1].at[owner, at.f],
                device_id={"fsdp": core},
                device_id_type=MESH,
            )

        def link_copy(k):
            peer = lax.rem(at.c + k, n)
            return pltpu.make_async_remote_copy(
                src_ref=src.at[peer],
                dst_ref=there(at.c),
                send_sem=send_sem.at[peer],
                recv_sem=recv_sem.at[at.c],
                device_id={"ctx": peer},
                device_id_type=MESH,
            )

        def go(make):
            make().start()
            sent.append(make)

        def share(step):
            for k in range(1, cores):
                go(functools.partial(pair_copy, k, step))

        def begin():
            for k in range(1, n):
                go(functools.partial(link_copy, k))
            copy = pltpu.make_async_copy(src.at[at.c], there(at.c), own_sem.at[0])
            copy.start()
            kept.append(copy)
            if self.share:
                share(0)

        def arrive(k):
            owner = lax.rem(at.c + k, n)
            block = there(owner)
            pltpu.make_async_copy(block, block, recv_sem.at[owner]).wait()
            if self.share:
                share(k)

        def end():
            if self.share:
                for owner in range(n):
                    for k in range(1, cores):
                        core = lax.rem(at.f + k, cores)
                        block = out.at[owner, core]
                        pltpu.make_async_copy(block, block, pair_sems[1].at[owner, core]).wait()
            for make in sent:
                make().wait_send()
            for copy in kept:
                copy.wait()

        events.append((-1, begin))
        for k in range(1, n):
            events.append((100 + k, functools.partial(arrive, k)))
        events.append((1000, end))
        return events


def vmem_bytes(scratch):
    total = 0
    for s in scratch:
        if hasattr(s, "shape") and s.dtype in (jnp.bfloat16, jnp.float32):
            size = s.dtype.itemsize * -(-s.shape[-1] // 128) * 128
            for k in s.shape[:-1]:
                size *= k
            total += size
    return total


def communicate(name, number, n, cores, ops, arrays, work=None, work_arrays=()):
    everyone = any(op.peers == "all" for op in ops)
    spread = any(op.spread for op in ops)
    outs = [op.out for op in ops] + (work.outs if work else [])
    anywhere = pl.BlockSpec(memory_space=pl.ANY)

    def kernel(*refs):
        at = Place(n, cores)
        if ops:
            barrier = pltpu.get_barrier_semaphore()
        if not ops:
            pass
        elif everyone:
            for j in range(1, n):
                pl.semaphore_signal(
                    barrier, 1, device_id={"ctx": lax.rem(at.c + j, n)}, device_id_type=MESH
                )
            count = n - 1
        else:
            for peer, ok in at.peers.values():
                maybe(
                    ok,
                    lambda peer=peer: pl.semaphore_signal(
                        barrier, 1, device_id={"ctx": peer}, device_id_type=MESH
                    ),
                )
            count = 2 + (at.z > 0).astype(jnp.int32) + (at.z < at.lines - 1).astype(jnp.int32)
        if ops and spread:
            for j in range(1, cores):
                pl.semaphore_signal(
                    barrier, 1, device_id={"fsdp": lax.rem(at.f + j, cores)}, device_id_type=MESH
                )
            count = count + cores - 1
        if ops:
            pl.semaphore_wait(barrier, count)
        k, inputs = len(ops), len(ops) + len(work_arrays)
        events, first = [], inputs + len(outs)
        for j, op in enumerate(ops):
            mine = refs[first : first + len(op.scratch)]
            first += len(op.scratch)
            events += op.events(at, refs[j], refs[inputs + j], *mine)
        events = sorted(events, key=lambda e: e[0])
        if not work:
            for _, event in events:
                event()
            return
        for time, event in events:
            if time < 0:
                event()
        between = [event for time, event in events if 0 <= time < 1000]
        loops = work.loops(refs[k:inputs], refs[inputs + k : inputs + len(outs)], refs[first:])
        steps, done = sum(loop[1] for loop in loops), 0
        for before, turns, body, after in loops:
            before()

            def turn(i, carry, done=done, turns=turns, body=body):
                for j in range(turns):
                    low, high = ((done + j + d) * len(between) // steps for d in range(2))
                    if high > low:

                        @pl.when(i == j)
                        def _(low=low, high=high):
                            for event in between[low:high]:
                                event()

                body(i)
                return carry

            lax.fori_loop(0, turns, turn, 0)
            after()
            done += turns
        for time, event in events:
            if time >= 1000:
                event()

    return pl.pallas_call(
        kernel,
        out_shape=outs,
        in_specs=[anywhere] * (len(ops) + len(work_arrays)),
        out_specs=[op.out_spec for op in ops] + [anywhere] * (len(outs) - len(ops)),
        scratch_shapes=[s for op in ops for s in op.scratch] + (work.scratch if work else []),
        compiler_params=pltpu.CompilerParams(
            collective_id=number if ops else None,
            has_side_effects=bool(ops),
            vmem_limit_bytes=(60 if work else 48) << 20,
        ),
        name=name,
    )(*arrays, *work_arrays)


class Products:
    def __init__(self, arrays, jobs, shared):
        self.arrays, self.jobs, self.shared = arrays, jobs, shared
        self.outs, self.scratch = [], []
        for left, right, axis, width in jobs:
            shape = (arrays[left].shape[0], arrays[right].shape[1])
            self.outs.append(jax.ShapeDtypeStruct(shape, jnp.bfloat16))
            piece = (width, shape[1]) if axis == 0 else (shape[0], width)
            self.scratch.append(pltpu.VMEM((2,) + piece, jnp.bfloat16))
        self.scratch.append(pltpu.SemaphoreType.DMA((len(jobs), 2)))
        self.scratch.append(pltpu.SemaphoreType.DMA((len(arrays),)))
        later = [second for first, second in shared]
        self.held = [i for i in range(len(arrays)) if i not in later]
        self.scratch += [pltpu.VMEM(arrays[i].shape, arrays[i].dtype) for i in self.held]

    def loops(self, ins, outs, scratch):
        jobs = self.jobs
        stages, (out_sem, in_sem) = scratch[: len(jobs)], scratch[len(jobs) : len(jobs) + 2]
        kept = dict(zip(self.held, scratch[len(jobs) + 2 :]))
        for first, second in self.shared:
            kept[second] = kept[first]
        ready = set()
        follows = dict(self.shared)
        begun = set(self.held)

        def load(i):
            return pltpu.make_async_copy(ins[i], kept[i], in_sem.at[i])

        def make(number):
            left, right, axis, width = jobs[number]
            shape = self.outs[number].shape
            turns = shape[axis] // width
            stage = stages[number]

            def out_copy(i):
                slot = lax.rem(i, 2)
                at = pl.ds(pl.multiple_of(i * width, 128), width)
                there = outs[number].at[at] if axis == 0 else outs[number].at[:, at]
                return pltpu.make_async_copy(stage.at[slot], there, out_sem.at[number, slot])

            def before():
                if number == 0:
                    for i in self.held:
                        load(i).start()
                for i in (left, right):
                    if i not in ready:
                        load(i).wait()
                        ready.add(i)

            def body(i):
                @pl.when(i >= 2)
                def _():
                    out_copy(i - 2).wait()

                at = pl.ds(pl.multiple_of(i * width, 128), width)
                a = kept[left][at] if axis == 0 else kept[left][...]
                b = kept[right][...] if axis == 0 else kept[right][:, at]
                stage[lax.rem(i, 2)] = jnp.dot(a, b, preferred_element_type=jnp.float32).astype(
                    jnp.bfloat16
                )
                out_copy(i).start()

            def after():
                for i in range(max(0, turns - 2), turns):
                    out_copy(i).wait()
                for i in (left, right):
                    if i in follows:
                        load(follows.pop(i)).start()

            return before, turns, body, after

        return [make(number) for number in range(len(jobs))]


class Staged:
    def __init__(self):
        self.arrays, self.outs, self.scratch = [], [], []
        self.sem_rows = 0
        self.sems = self.add(pltpu.SemaphoreType.DMA((64, 2)))

    def add(self, scratch):
        self.scratch.append(scratch)
        return len(self.scratch) - 1

    def hold(self, shape, dtype):
        return self.add(pltpu.VMEM(shape, dtype))

    def take(self, array):
        self.arrays.append(array)
        return len(self.arrays) - 1

    def give(self, shape, dtype):
        self.outs.append(jax.ShapeDtypeStruct(shape, dtype))
        return len(self.outs) - 1

    def loops(self, ins, outs, scratch):
        self.ins, self.gives, self.refs = ins, outs, scratch
        self.sem_rows, self.first = 0, []
        found = self.build()
        start = found[0][0]

        def begin():
            for copy in self.first:
                copy.start()
            start()

        return [(begin,) + found[0][1:]] + found[1:]

    def new_sems(self, count):
        self.sem_rows += count
        return [self.refs[self.sems].at[self.sem_rows - count + k] for k in range(count)]

    def whole(self, number, held):
        (sem,) = self.new_sems(1)
        copy = pltpu.make_async_copy(self.ins[number], self.refs[held], sem.at[0])
        self.first.append(copy)
        return copy.wait

    def stage(self, turns, loads, stores, body, ready=()):
        load_sems, store_sems = self.new_sems(len(loads)), self.new_sems(len(stores))

        def load(k, i, slot):
            return pltpu.make_async_copy(*loads[k](i, slot), load_sems[k].at[slot])

        def store(k, i, slot):
            return pltpu.make_async_copy(*stores[k](i, slot), store_sems[k].at[slot])

        for k in range(len(loads)):
            self.first.append(load(k, 0, 0))

        def before():
            for wait in ready:
                wait()

        def turn(i):
            slot = lax.rem(i, 2)
            for k in range(len(loads)):
                load(k, i, slot).wait()

            @pl.when(i + 1 < turns)
            def _():
                for k in range(len(loads)):
                    load(k, i + 1, 1 - slot).start()

            @pl.when(i >= 2)
            def _():
                for k in range(len(stores)):
                    store(k, i - 2, slot).wait()

            body(i, slot)
            for k in range(len(stores)):
                store(k, i, slot).start()

        def after():
            for i in range(max(0, turns - 2), turns):
                for k in range(len(stores)):
                    store(k, i, i % 2).wait()

        return before, turns, turn, after


def span(i, width, unit=128):
    return pl.ds(pl.multiple_of(i * width, unit), width)


class ExpertForward(Staged):
    def __init__(self, arrived, gate, up, down, ffn, shared_in, shared_out, pick, row_gate):
        super().__init__()
        low, wide = jnp.bfloat16, jnp.float32
        self.rows, self.fe = arrived.shape[0], gate.shape[1]
        self.seq, self.wp = ffn.shape[0], shared_out.shape[0]
        rows, fe, seq, wp = self.rows, self.fe, self.seq, self.wp
        self.pairs, self.tokens, self.slots = pick.shape
        for a in (arrived, gate, up, down, ffn, shared_in, shared_out, pick, row_gate):
            self.take(a)
        self.give((rows, 2 * fe), wide)
        self.give((fe, rows), low)
        self.give((rows, D), low)
        self.give((D, rows), low)
        self.give((seq, 2 * wp), wide)
        self.give((wp, seq), low)
        self.give((seq, D), low)
        self.chunk = 512
        self.held = {
            "arrived": self.hold((rows, D), low),
            "tile": self.hold((2, D, 256), low),
            "hidden": self.hold((rows, fe), low),
            "pre": self.hold((2, rows, 256), wide),
            "hidden_t": self.hold((2, 128, rows), low),
            "down": self.hold((2, fe, 256), low),
            "y": self.hold((rows, D), low),
            "y_out": self.hold((2, rows, 256), low),
            "arrived_t": self.hold((2, 256, rows), low),
            "ffn": self.hold((2, self.chunk, D), low),
            "shared_in": self.hold((D, 2 * wp), low),
            "shared_hidden": self.hold((seq, wp), low),
            "shared_pre": self.hold((2, self.chunk, 2 * wp), wide),
            "shared_t": self.hold((2, wp, self.chunk), low),
            "shared_out": self.hold((wp, D), low),
            "pick": self.hold(pick.shape, low),
            "row_gate": self.hold((seq, 128), wide),
            "out": self.hold((2, self.tokens, D), low),
        }

    def build(self):
        low = jnp.bfloat16
        r = {name: self.refs[k] for name, k in self.held.items()}
        arrived, gate, up, down, ffn = self.ins[:5]
        pre, hidden_t, y, arrived_t, shared_pre, shared_t, out = self.gives
        fe, wp, chunk, tokens, slots = self.fe, self.wp, self.chunk, self.tokens, self.slots
        ready = {
            name: self.whole(k, self.held[name])
            for name, k in (
                ("arrived", 0),
                ("shared_in", 5),
                ("shared_out", 6),
                ("pick", 7),
                ("row_gate", 8),
            )
        }

        def expert_in(i, slot):
            both_ = jnp.dot(r["arrived"][...], r["tile"][slot], preferred_element_type=jnp.float32)
            r["pre"][slot] = both_
            first = both_[:, :128]
            value = (first * jax.nn.sigmoid(first) * both_[:, 128:]).astype(low)
            r["hidden"][:, span(i, 128)] = value
            r["hidden_t"][slot] = jnp.transpose(value.astype(jnp.float32)).astype(low)

        def expert_out(i, slot):
            value = jnp.dot(
                r["hidden"][...], r["down"][slot], preferred_element_type=jnp.float32
            ).astype(low)
            r["y"][:, span(i, 256)] = value
            r["y_out"][slot] = value
            rows = r["arrived"][:, span(i, 256)]
            r["arrived_t"][slot] = jnp.transpose(rows.astype(jnp.float32)).astype(low)

        def shared_in(i, slot):
            both_ = jnp.dot(r["ffn"][slot], r["shared_in"][...], preferred_element_type=jnp.float32)
            r["shared_pre"][slot] = both_
            first = both_[:, :wp]
            value = (first * jax.nn.sigmoid(first) * both_[:, wp:]).astype(low)
            r["shared_hidden"][span(i, chunk)] = value
            r["shared_t"][slot] = jnp.transpose(value.astype(jnp.float32)).astype(low)

        def result(i, slot):
            at = span(i, tokens)
            routed = jnp.dot(
                r["pick"][i], r["y"][span(i, slots, 16)], preferred_element_type=jnp.float32
            )
            more = jnp.dot(
                r["shared_hidden"][at], r["shared_out"][...], preferred_element_type=jnp.float32
            )
            r["out"][slot] = (r["row_gate"][at, 0:1] * routed + more).astype(low)

        return [
            self.stage(
                fe // 128,
                [
                    lambda i, s: (gate.at[:, span(i, 128)], r["tile"].at[s, :, pl.ds(0, 128)]),
                    lambda i, s: (up.at[:, span(i, 128)], r["tile"].at[s, :, pl.ds(128, 128)]),
                ],
                [
                    lambda i, s: (r["pre"].at[s], pre.at[:, span(i, 256)]),
                    lambda i, s: (r["hidden_t"].at[s], hidden_t.at[span(i, 128)]),
                ],
                expert_in,
                [ready["arrived"]],
            ),
            self.stage(
                D // 256,
                [lambda i, s: (down.at[:, span(i, 256)], r["down"].at[s])],
                [
                    lambda i, s: (r["y_out"].at[s], y.at[:, span(i, 256)]),
                    lambda i, s: (r["arrived_t"].at[s], arrived_t.at[span(i, 256)]),
                ],
                expert_out,
            ),
            self.stage(
                self.seq // chunk,
                [lambda i, s: (ffn.at[span(i, chunk)], r["ffn"].at[s])],
                [
                    lambda i, s: (r["shared_pre"].at[s], shared_pre.at[span(i, chunk)]),
                    lambda i, s: (r["shared_t"].at[s], shared_t.at[:, span(i, chunk)]),
                ],
                shared_in,
                [ready["shared_in"]],
            ),
            self.stage(
                self.pairs,
                [],
                [lambda i, s: (r["out"].at[s], out.at[span(i, tokens)])],
                result,
                [ready["shared_out"], ready["pick"], ready["row_gate"]],
            ),
        ]


class ExpertBackward(Staged):
    def __init__(self, grad_rows, pre, gate, up, down, grad, shared_pre, shared_in, shared_out, pick):
        super().__init__()
        low, wide = jnp.bfloat16, jnp.float32
        self.rows, self.fe = grad_rows.shape[0], gate.shape[1]
        self.seq, self.wp = grad.shape[0], shared_out.shape[1]
        rows, fe, seq, wp = self.rows, self.fe, self.seq, self.wp
        self.pairs, self.tokens, self.slots = pick.shape
        for a in (grad_rows, pre, gate, up, down, grad, shared_pre, shared_in, shared_out, pick):
            self.take(a)
        self.give((rows, fe), low)
        self.give((rows, fe), low)
        self.give((2 * wp, seq), low)
        self.give((seq, D), low)
        self.chunk = 512
        self.held = {
            "rows": self.hold((rows, D), low),
            "pre": self.hold((2, rows, 256), wide),
            "down": self.hold((2, 128, D), low),
            "d_gate": self.hold((rows, fe), low),
            "d_up": self.hold((rows, fe), low),
            "gate": self.hold((2, 256, fe), low),
            "up": self.hold((2, 256, fe), low),
            "grad": self.hold((2, self.chunk, D), low),
            "shared_pre": self.hold((2, self.chunk, 2 * wp), wide),
            "shared_out": self.hold((D, wp), low),
            "d_shared": self.hold((seq, 2 * wp), low),
            "shared_t": self.hold((2, 2 * wp, self.chunk), low),
            "shared_in": self.hold((2 * wp, D), low),
            "pick": self.hold(pick.shape, low),
            "out": self.hold((2, self.tokens, D), low),
        }

    def build(self):
        low = jnp.bfloat16
        r = {name: self.refs[k] for name, k in self.held.items()}
        grad_rows, pre, gate, up, down, grad, shared_pre = self.ins[:7]
        d_gate, d_up, shared_t, out = self.gives
        fe, wp, chunk, tokens, slots = self.fe, self.wp, self.chunk, self.tokens, self.slots
        ready = {
            name: self.whole(k, self.held[name])
            for name, k in (("rows", 0), ("shared_in", 7), ("shared_out", 8), ("pick", 9))
        }

        def across(left, right):
            return lax.dot_general(
                left, right, (((1,), (1,)), ((), ())), preferred_element_type=jnp.float32
            )

        def slopes(first, second, grads):
            sigmoid = jax.nn.sigmoid(first)
            act = first * sigmoid
            slope = sigmoid * (1.0 + first * (1.0 - sigmoid))
            return (grads * second * slope).astype(low), (grads * act).astype(low)

        def expert_hidden(i, slot):
            grads = across(r["rows"][...], r["down"][slot])
            values = r["pre"][slot]
            one, two = slopes(values[:, :128], values[:, 128:], grads)
            r["d_gate"][:, span(i, 128)] = one
            r["d_up"][:, span(i, 128)] = two

        def expert_rows(i, slot):
            value = across(r["d_gate"][...], r["gate"][slot])
            value = value + across(r["d_up"][...], r["up"][slot])
            r["rows"][:, span(i, 256)] = value.astype(low)

        def shared_hidden(i, slot):
            grads = jnp.dot(
                r["grad"][slot], r["shared_out"][...], preferred_element_type=jnp.float32
            )
            values = r["shared_pre"][slot]
            one, two = slopes(values[:, :wp], values[:, wp:], grads)
            value = jnp.concatenate([one, two], axis=1)
            r["d_shared"][span(i, chunk)] = value
            r["shared_t"][slot] = jnp.transpose(value.astype(jnp.float32)).astype(low)

        def result(i, slot):
            value = jnp.dot(
                r["pick"][i], r["rows"][span(i, slots, 16)], preferred_element_type=jnp.float32
            )
            value = value + jnp.dot(
                r["d_shared"][span(i, tokens)],
                r["shared_in"][...],
                preferred_element_type=jnp.float32,
            )
            r["out"][slot] = value.astype(low)

        return [
            self.stage(
                fe // 128,
                [
                    lambda i, s: (down.at[span(i, 128)], r["down"].at[s]),
                    lambda i, s: (pre.at[:, span(i, 256)], r["pre"].at[s]),
                ],
                [],
                expert_hidden,
                [ready["rows"]],
            ),
            self.stage(
                D // 256,
                [
                    lambda i, s: (gate.at[span(i, 256)], r["gate"].at[s]),
                    lambda i, s: (up.at[span(i, 256)], r["up"].at[s]),
                ],
                [],
                expert_rows,
            ),
            self.stage(
                self.seq // chunk,
                [
                    lambda i, s: (grad.at[span(i, chunk)], r["grad"].at[s]),
                    lambda i, s: (shared_pre.at[span(i, chunk)], r["shared_pre"].at[s]),
                ],
                [lambda i, s: (r["shared_t"].at[s], shared_t.at[:, span(i, chunk)])],
                shared_hidden,
                [ready["shared_out"]],
            ),
            self.stage(
                1,
                [],
                [
                    lambda i, s: (r["d_gate"], d_gate),
                    lambda i, s: (r["d_up"], d_up),
                ],
                lambda i, s: None,
            ),
            self.stage(
                self.pairs,
                [],
                [lambda i, s: (r["out"].at[s], out.at[span(i, tokens)])],
                result,
                [ready["shared_in"], ready["pick"]],
            ),
        ]


BLOCK = 256


def attend_kernel(causal, scale, query, key, value, bounds, attended, log_total):
    for start in range(0, query.shape[0], BLOCK):
        rows = pl.ds(start, BLOCK)
        reach = start + BLOCK if causal else key.shape[0]
        scores = lax.dot_general(
            query[rows], key[:reach], (((1,), (1,)), ((), ())), preferred_element_type=jnp.float32
        )
        column = lax.broadcasted_iota(jnp.int32, scores.shape, 1)
        seen = (column >= bounds[rows, 0:1]) & (column <= bounds[rows, 1:2])
        scores = jnp.where(seen, scores * scale, NEG)
        peak = jnp.max(scores, axis=-1, keepdims=True)
        shifted = jnp.exp(scores - peak)
        total = jnp.sum(shifted, axis=-1, keepdims=True)
        probs = (shifted * (1.0 / total)).astype(jnp.bfloat16)
        attended[rows] = jnp.dot(probs, value[:reach], preferred_element_type=jnp.float32)
        log_total[rows] = jnp.broadcast_to(peak + jnp.log(total), (BLOCK, 128))


def attend(query, key, value, bounds, causal, scale):
    whole = pl.BlockSpec(memory_space=pltpu.VMEM)
    return pl.pallas_call(
        functools.partial(attend_kernel, causal, scale),
        out_shape=[
            jax.ShapeDtypeStruct((query.shape[0], VDIM), jnp.float32),
            jax.ShapeDtypeStruct((query.shape[0], 128), jnp.float32),
        ],
        in_specs=[whole] * 4,
        out_specs=[whole] * 2,
        compiler_params=pltpu.CompilerParams(vmem_limit_bytes=48 << 20),
        name="attend",
    )(query, key, value, bounds)


def attend_back_kernel(
    causal, scale, query, key, value, bounds, log_total, attended, grad, d_query, d_key, d_value
):
    d_key[...] = jnp.zeros_like(d_key)
    d_value[...] = jnp.zeros_like(d_value)
    for start in range(0, query.shape[0], BLOCK):
        rows = pl.ds(start, BLOCK)
        reach = start + BLOCK if causal else key.shape[0]
        mine, grad_rows = query[rows], grad[rows]
        scores = lax.dot_general(
            mine, key[:reach], (((1,), (1,)), ((), ())), preferred_element_type=jnp.float32
        )
        column = lax.broadcasted_iota(jnp.int32, scores.shape, 1)
        seen = (column >= bounds[rows, 0:1]) & (column <= bounds[rows, 1:2])
        probs = jnp.where(seen, jnp.exp(scores * scale - log_total[rows, 0:1]), 0.0)
        delta = jnp.sum(grad_rows.astype(jnp.float32) * attended[rows], axis=-1, keepdims=True)
        d_probs = lax.dot_general(
            grad_rows, value[:reach], (((1,), (1,)), ((), ())), preferred_element_type=jnp.float32
        )
        d_scores = (probs * (d_probs - delta)).astype(jnp.bfloat16)
        d_query[rows] = (
            jnp.dot(d_scores, key[:reach], preferred_element_type=jnp.float32) * scale
        )
        d_key[:reach] += lax.dot_general(
            d_scores, mine, (((0,), (0,)), ((), ())), preferred_element_type=jnp.float32
        )
        d_value[:reach] += lax.dot_general(
            probs.astype(jnp.bfloat16),
            grad_rows,
            (((0,), (0,)), ((), ())),
            preferred_element_type=jnp.float32,
        )
    d_key[...] = d_key[...] * scale


def attend_back(query, key, value, bounds, log_total, attended, grad, causal, scale):
    whole = pl.BlockSpec(memory_space=pltpu.VMEM)
    return pl.pallas_call(
        functools.partial(attend_back_kernel, causal, scale),
        out_shape=[
            jax.ShapeDtypeStruct(query.shape, jnp.float32),
            jax.ShapeDtypeStruct(key.shape, jnp.float32),
            jax.ShapeDtypeStruct(value.shape, jnp.float32),
        ],
        in_specs=[whole] * 7,
        out_specs=[whole] * 3,
        compiler_params=pltpu.CompilerParams(vmem_limit_bytes=56 << 20),
        name="attend_back",
    )(query, key, value, bounds, log_total, attended, grad)


def doc_index(starts, positions):
    return jnp.sum((positions[:, None] >= starts[None, :]).astype(jnp.int32), axis=1) - 1


def rope_tables(positions):
    half = ROPE // 2
    frequency = THETA ** (-jnp.arange(half, dtype=jnp.float32) / half)
    angles = positions.astype(jnp.float32)[:, None] * frequency[None, :]
    return (jnp.cos(angles), jnp.sin(angles))


def rotate_pairs(values, cosines, sines):
    half = values.shape[-1] // 2
    first = values[..., :half]
    second = values[..., half:]
    return jnp.concatenate(
        [first * cosines - second * sines, second * cosines + first * sines], axis=-1
    )


def rms_forward(values, gain):
    factor = lax.rsqrt(jnp.mean(values * values, axis=-1, keepdims=True) + EPS)
    normal = values * factor
    return (normal * gain, normal, factor)


def rms_backward(grad_out, normal, factor, gain):
    scaled = grad_out * gain
    grad_in = factor * (scaled - normal * jnp.mean(scaled * normal, axis=-1, keepdims=True))
    return (grad_in, jnp.sum(grad_out * normal, axis=0))


def silu_parts(values):
    sigmoid = jax.nn.sigmoid(values)
    return (values * sigmoid, sigmoid * (1.0 + values * (1.0 - sigmoid)))


def dot(left, right):
    return jnp.dot(left, right, preferred_element_type=jnp.float32)


def dot_t(left, right):
    return lax.dot_general(left, right, (((1,), (1,)), ((), ())), preferred_element_type=jnp.float32)


def t_dot(left, right):
    return lax.dot_general(left, right, (((0,), (0,)), ((), ())), preferred_element_type=jnp.float32)


def two_parts(values):
    high = lax.reduce_precision(values, 8, 7)
    return high.astype(jnp.bfloat16), (values - high).astype(jnp.bfloat16)


def padded(values, columns):
    short = -values.shape[-1] % columns
    if not short:
        return values
    return jnp.pad(values, [(0, 0)] * (values.ndim - 1) + [(0, short)])


def shards(
    tokens,
    cotangent,
    doc_starts,
    routes,
    attn_gain,
    q_weight,
    kva_weight,
    kv_gain,
    kvb_weight,
    o_weight,
    ffn_gain,
    router_weight,
    shared_gate,
    shared_up,
    shared_down,
    expert_gate,
    expert_up,
    expert_down,
):
    low = jnp.bfloat16
    wide = jnp.float32
    n, cores = lax.axis_size("ctx"), lax.axis_size("fsdp")
    here = lax.axis_index("ctx")
    t = tokens.shape[1]
    half = t // 2
    seq = n * t
    ws = q_weight.shape[0]
    kr = kvb_weight.shape[0]
    copies = n // HEADS
    shared = shared_gate.shape[1]
    w = shared // n
    picks_count = routes.shape[2]
    capacity = 10 * t * picks_count // (7 * n)
    slots_count = -(-capacity // 8) * 8
    scale = HEAD ** (-0.5)
    starts = doc_starts[0]

    def run(name, number, ops, arrays, work=None):
        for op in ops:
            op.setup(n, cores)
        if work is None:
            return communicate(name, number, n, cores, ops, arrays)
        if vmem_bytes([s for op in ops for s in op.scratch] + work.scratch) < 54 << 20:
            return communicate(name, number, n, cores, ops, arrays, work, work.arrays)
        return list(communicate(name, number, n, cores, ops, arrays)) + list(
            communicate(name + "_work", None, n, cores, [], [], work, work.arrays)
        )

    def by_position(owner, start):
        if start < half:
            return pl.multiple_of(owner * half + start, 16)
        return pl.multiple_of((2 * n - 1 - owner) * half + start - half, 16)

    def by_row(rows):
        return lambda owner, start: pl.multiple_of(owner * rows + start, 16)

    def to_owners(values):
        columns = values.shape[-1]
        pair = values.reshape(2, n, half, columns)
        return jnp.concatenate([pair[0], pair[1][::-1]], axis=1)

    def to_positions(values):
        columns = values.shape[-1]
        return jnp.concatenate(
            [
                values[:, :half].reshape(n * half, columns),
                values[::-1, half:].reshape(n * half, columns),
            ]
        )

    small = jnp.concatenate(
        [
            kva_weight,
            router_weight,
            attn_gain[:, None],
            ffn_gain[:, None],
            jnp.pad(kv_gain, (0, ws - kr))[:, None],
        ],
        axis=1,
    ).astype(low)
    small = padded(small, 128)
    small_columns = small.shape[1]
    first = RANK + ROPE
    head_part = jnp.concatenate(
        [
            q_weight.astype(low).reshape(ws, HEADS, HEAD).transpose(1, 0, 2),
            kvb_weight.astype(low)
            .reshape(kr, HEADS, KV)
            .transpose(1, 0, 2)
            .reshape(HEADS, ws, kr * KV // ws),
        ],
        axis=-1,
    )
    if copies > 1:
        head_part = jnp.repeat(head_part, copies, axis=0)
    head_columns = head_part.shape[-1]
    shared_part = padded(
        jnp.concatenate(
            [
                v.astype(low).reshape(ws, n, w)
                for v in (shared_gate, shared_up, jnp.transpose(shared_down))
            ],
            axis=-1,
        ).transpose(1, 0, 2),
        128,
    )
    shared_columns = shared_part.shape[-1]

    pick_rows = -(-picks_count // 16) * 16
    pick_part = jnp.pad(jnp.transpose(routes[0]), ((0, pick_rows - picks_count), (0, 0))).astype(low)
    inputs_all, head_all, small, pick_blocks = run(
        "gather_tokens",
        0,
        [
            Gather(t, D, low, by_position),
            Exchange(ws, head_columns, low, True),
            Gather(ws, small_columns, low, by_row(ws), True),
            Gather(pick_rows, t, low, by_row(pick_rows)),
        ],
        [tokens[0], head_part, small, pick_part],
    )
    kva_full = small[:, :first]
    router_full = small[:, first : first + n]
    gain_one = small[:, first + n].astype(wide)
    gain_two = small[:, first + n + 1].astype(wide)
    gain_latent = small[:, first + n + 2].reshape(n * cores, ws)[:, :kr].reshape(-1).astype(wide)
    picks_all = pick_blocks.reshape(n, pick_rows, t)[:, :picks_count].astype(jnp.int32)

    def after(value, *others):
        return lax.optimization_barrier((value,) + others)[0]

    grad_low = cotangent[0]
    grad = grad_low.astype(wide)
    expert_parts = [
        after(v[0], inputs_all).astype(low) for v in (expert_gate, expert_up, expert_down)
    ]
    experts = (
        lax.all_gather(expert_parts[0], "fsdp", axis=0, tiled=True),
        lax.all_gather(expert_parts[1], "fsdp", axis=0, tiled=True),
        lax.all_gather(expert_parts[2], "fsdp", axis=1, tiled=True),
    )

    head_all = head_all.reshape(D, head_columns)
    q_head = head_all[:, :HEAD]
    kvb_head = head_all[:, HEAD:].reshape(RANK, KV)

    positions = jnp.arange(seq, dtype=jnp.int32)
    cosines, sines = rope_tables(positions)
    normed_all = rms_forward(inputs_all.astype(wide), gain_one)[0].astype(low)
    query_raw = dot(normed_all, q_head)
    blank = jnp.zeros((seq, 2 * NOPE - HEAD), low)
    queries = jnp.concatenate(
        [
            query_raw[:, :NOPE].astype(low),
            rotate_pairs(query_raw[:, NOPE:], cosines, sines).astype(low),
            blank,
        ],
        axis=-1,
    )
    compressed = dot(normed_all, kva_full)
    latent_all = rms_forward(compressed[:, :RANK], gain_latent)[0].astype(low)
    rope_all = rotate_pairs(compressed[:, RANK:], cosines, sines).astype(low)
    kv_head = dot(latent_all, kvb_head).astype(low)
    keys = jnp.concatenate([kv_head[:, :NOPE], rope_all, blank], axis=-1)
    values = kv_head[:, NOPE:]
    opening = jnp.max(jnp.where(starts[None, :] <= positions[:, None], starts[None, :], 0), axis=1)

    def queries_here(rows):
        if copies == 1:
            return rows
        if rows.ndim == 1:
            return queries_here(rows[:, None])[:, 0]
        blocks = to_owners(rows).reshape(n // copies, copies, t, rows.shape[-1])
        return lax.dynamic_index_in_dim(blocks, here % copies, 1, False).reshape(-1, rows.shape[-1])

    def queries_back(rows):
        if copies == 1:
            return to_owners(rows)
        blocks = rows.reshape(n // copies, 1, t, rows.shape[-1])
        mine = (jnp.arange(copies) == here % copies)[None, :, None, None]
        return jnp.where(mine, blocks, jnp.zeros((), rows.dtype)).reshape(n, t, rows.shape[-1])

    def of_heads(blocks):
        columns = blocks.shape[-1]
        if copies > 1:
            blocks = blocks.reshape(HEADS, copies, t, columns)
            blocks = jnp.sum(blocks.astype(wide), axis=1).astype(blocks.dtype)
        return blocks.transpose(1, 0, 2).reshape(t, HEADS * columns)

    queries, query_cos, query_sin = (queries_here(v) for v in (queries, cosines, sines))
    bounds = queries_here(jnp.pad(jnp.stack([opening, positions], axis=1), ((0, 0), (0, 126))))
    attended, log_total = attend(queries, keys, values, bounds, copies == 1, scale)

    attn_blocks, shared_all, out_proj = run(
        "attended",
        1,
        [
            Exchange(t, VDIM, low),
            Exchange(ws, shared_columns, low, True),
            Gather(ws, D, low, by_row(ws), True),
        ],
        [
            queries_back(attended.astype(low)),
            shared_part,
            jnp.transpose(o_weight).astype(low),
        ],
    )
    shared_all = shared_all.reshape(D, shared_columns)
    gate_cols, up_cols, down_rows = (shared_all[:, i * w : (i + 1) * w] for i in range(3))
    attn_values = of_heads(attn_blocks)

    inputs = tokens[0].astype(wide)
    normed_one, normal_one, factor_one = rms_forward(inputs, gain_one)
    normed_low = normed_one.astype(low)
    resid = inputs + dot_t(attn_values, out_proj)
    normed_two, normal_two, factor_two = rms_forward(resid, gain_two)
    ffn_in = normed_two.astype(low)

    (ffn_all,) = run("gather_ffn", 2, [Gather(t, D, low, by_row(t))], [ffn_in])

    chosen = jnp.any(
        picks_all[:, :, :, None] == jnp.arange(n, dtype=jnp.int32)[None, None, None, :], axis=1
    ).reshape(seq, n)
    logits = jnp.where(chosen, dot(ffn_all, router_full), NEG)
    shifted = jnp.where(chosen, jnp.exp(logits - jnp.max(logits, axis=-1, keepdims=True)), 0.0)
    gates_all = shifted / jnp.sum(shifted, axis=-1, keepdims=True)
    gate_here = lax.dynamic_index_in_dim(gates_all, here, 1, False).reshape(n, t)
    taken = lax.dynamic_index_in_dim(chosen, here, 1, False).reshape(n, t)
    slots = jnp.where(taken, jnp.cumsum(taken.astype(jnp.int32), axis=1) - 1, -1)
    onehot = slots[:, None, :] == jnp.arange(slots_count, dtype=jnp.int32)[None, :, None]
    onehot_low = onehot.astype(low)
    rows = n * slots_count

    def to_slots(values):
        return (
            jnp.einsum(
                "nst,ntd->nsd", onehot_low, values.reshape(n, t, D), preferred_element_type=wide
            )
            .astype(low)
            .reshape(rows, D)
        )

    pick = (
        jnp.transpose(onehot_low, (0, 2, 1)).reshape(n // 2, 2, t, 1, slots_count)
        * jnp.eye(2, dtype=low)[None, :, None, :, None]
    ).reshape(n // 2, 2 * t, 2 * slots_count)
    shared_rows = -(-w // 128) * 128

    def wider(values):
        return jnp.pad(values, ((0, 0), (0, shared_rows - w)))

    shared_in = jnp.concatenate([wider(gate_cols), wider(up_cols)], axis=1)
    shared_out = wider(down_rows)
    arrived = to_slots(ffn_all)
    (
        grad_all,
        query_proj,
        pre,
        hidden_t,
        expert_result,
        arrived_t,
        shared_pre,
        shared_t,
        out_part,
    ) = run(
        "gather_grad",
        6,
        [Gather(t, D, low, by_row(t)), Gather(ws, HEADS * HEAD, low, by_row(ws), True)],
        [grad_low, q_weight.astype(low)],
        ExpertForward(
            arrived,
            experts[0],
            experts[1],
            experts[2],
            ffn_all,
            shared_in,
            jnp.transpose(shared_out),
            pick,
            jnp.broadcast_to(gate_here.reshape(seq, 1), (seq, 128)),
        ),
    )
    row_gate = jnp.sum(jnp.where(onehot, gate_here[:, None, :], 0.0), axis=2).reshape(rows, 1)
    arrived_grad = to_slots(grad_all)
    pick_grad = (row_gate * arrived_grad.astype(wide)).astype(low)
    routed, pre_gate_grad, pre_up_grad, shared_grad_t, ffn_part = run(
        "reduce_out",
        7,
        [Reduce(t, D, by_row(t))],
        [out_part],
        ExpertBackward(
            pick_grad,
            pre,
            experts[0],
            experts[1],
            experts[2],
            grad_all,
            shared_pre,
            jnp.transpose(shared_in),
            shared_out,
            pick,
        ),
    )
    output = (resid + routed).astype(low)
    row_gate_grad = jnp.sum(expert_result.astype(wide) * arrived_grad.astype(wide), axis=-1)
    gate_grad_here = jnp.sum(
        jnp.where(onehot, row_gate_grad.reshape(n, slots_count, 1), 0.0), axis=1
    )

    results = run(
        "reduce_ffn",
        3,
        [Reduce(t, D, by_row(t)), Exchange(8, t, wide)],
        [ffn_part, jnp.pad(gate_grad_here[:, None, :], ((0, 0), (0, 7), (0, 0)))],
        Products(
            [
                shared_grad_t,
                ffn_all,
                hidden_t,
                pick_grad,
                arrived_t,
                pre_gate_grad,
                pre_up_grad,
                shared_t,
                grad_all,
            ],
            [(0, 1, 1, 512), (2, 3, 1, 256), (4, 5, 0, 256), (4, 6, 0, 256), (7, 8, 1, 512)],
            [(1, 8)],
        ),
    )
    ffn_in_grad, gate_blocks, shared_in_grad, out_w_grad, in_gate_grad, in_up_grad, shared_out_grad = (
        results
    )
    expert_grads = (
        lax.psum_scatter(in_gate_grad, "fsdp", scatter_dimension=0, tiled=True),
        lax.psum_scatter(in_up_grad, "fsdp", scatter_dimension=0, tiled=True),
        lax.psum_scatter(out_w_grad, "fsdp", scatter_dimension=1, tiled=True),
    )
    shared_grads = jnp.concatenate(
        [shared_in_grad[:w], shared_in_grad[shared_rows : shared_rows + w], shared_out_grad[:w]]
    )
    shared_grads = padded(jnp.transpose(shared_grads), 128).reshape(n, cores, ws, shared_columns)

    gates = lax.dynamic_slice_in_dim(gates_all, here * t, t, 0)
    gate_grad = jnp.transpose(gate_blocks[:, 0, :])
    mixed = jnp.sum(gates * gate_grad, axis=-1, keepdims=True)
    logit_grad = (gates * (gate_grad - mixed)).astype(low)
    router_grad = t_dot(ffn_in, logit_grad)
    ffn_in_grad = ffn_in_grad + dot_t(logit_grad, router_full)
    resid_part, gain_two_grad = rms_backward(ffn_in_grad, normal_two, factor_two, gain_two)
    resid_grad = grad + resid_part
    attn_grad_low = resid_grad.astype(low)
    grad_attended = dot(attn_grad_low, out_proj).astype(low)
    grad_blocks = grad_attended.reshape(t, HEADS, VDIM).transpose(1, 0, 2)
    if copies > 1:
        grad_blocks = jnp.repeat(grad_blocks, copies, axis=0)
    (grad_att_blocks,) = run("grad_attended", 4, [Exchange(t, VDIM, low)], [grad_blocks])
    out_proj_grad = t_dot(attn_grad_low, attn_values).astype(low).reshape(n, cores, ws, D)

    grad_att = queries_here(to_positions(grad_att_blocks))
    query_grad, key_grad, value_grad = attend_back(
        queries, keys, values, bounds, log_total, attended, grad_att, copies == 1, scale
    )
    query_grad = query_grad.astype(low).astype(wide)
    raw_grad = jnp.concatenate(
        [query_grad[:, :NOPE], rotate_pairs(query_grad[:, NOPE:HEAD], query_cos, -query_sin)], axis=-1
    ).astype(low)
    kv_grad = jnp.concatenate([key_grad[:, :NOPE], value_grad], axis=-1)
    kv_high, kv_rest = two_parts(kv_grad)
    latent_part = dot_t(kv_high, kvb_head) + dot_t(kv_rest, kvb_head)
    latent_part = padded(jnp.concatenate([latent_part, key_grad[:, NOPE:HEAD]], axis=1).astype(low), 128)
    query_blocks, latent_sum, shared_blocks, out_proj_sum = run(
        "reduce_latent",
        5,
        [
            Exchange(t, 2 * NOPE, low),
            Reduce(t, latent_part.shape[1], by_position),
            Exchange(ws, shared_columns, low, fold=True),
            Reduce(ws, D, by_row(ws), True),
        ],
        [padded(queries_back(raw_grad), 2 * NOPE), latent_part, shared_grads, out_proj_grad],
    )
    up_latent_grad = t_dot(latent_all, kv_high) + t_dot(latent_all, kv_rest)
    query_proj_grad = t_dot(queries_here(normed_all), raw_grad)
    head_grads = jnp.concatenate(
        [query_proj_grad, up_latent_grad.reshape(D, head_columns - HEAD)], axis=1
    ).astype(low).reshape(n, cores, ws, head_columns)

    compressed_here = dot(normed_low, kva_full)
    unused, latent_normal, latent_factor = rms_forward(compressed_here[:, :RANK], gain_latent)
    my_rows = jnp.arange(t, dtype=jnp.int32)
    my_positions = jnp.where(
        my_rows < half, here * half + my_rows, (2 * n - 1 - here) * half + my_rows - half
    )
    my_cosines, my_sines = rope_tables(my_positions)
    comp_latent_grad, gain_latent_grad = rms_backward(
        latent_sum[:, :RANK], latent_normal, latent_factor, gain_latent
    )
    rope_sum = latent_sum[:, RANK : RANK + ROPE].astype(low).astype(wide)
    rope_back = rotate_pairs(rope_sum, my_cosines, -my_sines)
    comp_grad = jnp.concatenate([comp_latent_grad, rope_back], axis=-1).astype(low)
    raw_here = of_heads(query_blocks[:, :, :HEAD])
    normed_grad = dot_t(raw_here, query_proj) + dot_t(comp_grad, kva_full)
    input_part, gain_one_grad = rms_backward(normed_grad, normal_one, factor_one, gain_one)
    input_grad = (resid_grad + input_part).astype(low)

    down_latent_grad = t_dot(normed_low, comp_grad)
    latent_column = jnp.pad(gain_latent_grad.reshape(n * cores, kr), ((0, 0), (0, ws - kr)))
    small_grads = padded(
        jnp.concatenate(
            [
                down_latent_grad,
                router_grad,
                gain_one_grad[:, None],
                gain_two_grad[:, None],
                latent_column.reshape(D, 1),
            ],
            axis=1,
        ).astype(low),
        128,
    ).reshape(n, cores, ws, small_columns)
    head_blocks, small_sum = run(
        "weight_grads",
        8,
        [
            Exchange(ws, head_columns, low, fold=True),
            Reduce(ws, small_columns, by_row(ws), True),
        ],
        [head_grads, small_grads],
    )
    head_sum = jnp.sum(
        head_blocks.astype(wide).reshape(HEADS, copies, ws, head_columns), axis=1
    )
    q_weight_grad = head_sum[:, :, :HEAD].transpose(1, 0, 2).reshape(ws, HEADS * HEAD)
    kvb_weight_grad = (
        head_sum[:, :, HEAD:].reshape(HEADS, kr, KV).transpose(1, 0, 2).reshape(kr, HEADS * KV)
    )
    shared_sums = [
        shared_blocks[:, :, i * w : (i + 1) * w]
        .transpose(1, 0, 2)
        .reshape(ws, shared)
        .astype(wide)
        for i in range(3)
    ]
    return (
        output[None],
        input_grad[None],
        small_sum[:, first + n],
        q_weight_grad,
        small_sum[:, :first],
        small_sum[:kr, first + n + 2],
        kvb_weight_grad,
        jnp.transpose(out_proj_sum),
        small_sum[:, first + n + 1],
        small_sum[:, first : first + n],
        shared_sums[0],
        shared_sums[1],
        jnp.transpose(shared_sums[2]),
        expert_grads[0][None].astype(wide),
        expert_grads[1][None].astype(wide),
        expert_grads[2][None].astype(wide),
    )


def solution(mesh):
    return jax.shard_map(
        shards,
        mesh=mesh,
        in_specs=(
            P("fsdp", "ctx", None),
            P("fsdp", "ctx", None),
            P("fsdp", None),
            P("fsdp", "ctx", None),
            P(("ctx", "fsdp")),
            P(("ctx", "fsdp"), None),
            P(("ctx", "fsdp"), None),
            P(("ctx", "fsdp")),
            P(("ctx", "fsdp"), None),
            P(None, ("ctx", "fsdp")),
            P(("ctx", "fsdp")),
            P(("ctx", "fsdp"), None),
            P(("ctx", "fsdp"), None),
            P(("ctx", "fsdp"), None),
            P(None, ("ctx", "fsdp")),
            P("ctx", "fsdp", None),
            P("ctx", "fsdp", None),
            P("ctx", None, "fsdp"),
        ),
        out_specs=(
            P("fsdp", "ctx", None),
            P("fsdp", "ctx", None),
            P(("ctx", "fsdp")),
            P(("ctx", "fsdp"), None),
            P(("ctx", "fsdp"), None),
            P(("ctx", "fsdp")),
            P(("ctx", "fsdp"), None),
            P(None, ("ctx", "fsdp")),
            P(("ctx", "fsdp")),
            P(("ctx", "fsdp"), None),
            P(("ctx", "fsdp"), None),
            P(("ctx", "fsdp"), None),
            P(None, ("ctx", "fsdp")),
            P("ctx", "fsdp", None),
            P("ctx", "fsdp", None),
            P("ctx", None, "fsdp"),
        ),
        check_vma=False,
    )
```

```python
import functools

import jax
import jax.numpy as jnp
from jax import lax
from jax.experimental import pallas as pl
from jax.experimental.pallas import tpu as pltpu
from jax.sharding import PartitionSpec as P

D = 2048
HEADS = 16
NOPE = 128
ROPE = 64
VDIM = 128
RANK = 512
HEAD = NOPE + ROPE
KV = NOPE + VDIM

EPS = 1e-06
THETA = 10000.0
NEG = -1e30
MESH = pl.DeviceIdType.MESH
BLOCK = 256

ZXY, ZYX = ("z", "x", "y"), ("z", "y", "x")
XYZ, YXZ = ("x", "y", "z"), ("y", "x", "z")


def pieces(rows, light=False):
    if rows == 128 and not light:
        return (
            (0, 32, ZXY),
            (32, 32, ZYX),
            (64, 16, ZXY),
            (80, 16, ZYX),
            (96, 16, XYZ),
            (112, 16, YXZ),
        )
    if rows == 128:
        return ((0, 32, ZXY), (32, 32, ZYX), (64, 32, ZXY), (96, 32, ZYX))
    if rows == 64 and not light:
        return ((0, 32, ZXY), (32, 16, ZYX), (48, 16, YXZ))
    if rows % 32 == 0:
        return ((0, rows // 2, ZXY), (rows // 2, rows // 2, ZYX))
    return ((0, rows, ZXY),)


def maybe(cond, fn):
    if cond is None:
        fn()
    else:
        pl.when(cond)(fn)


def both(first, second):
    if first is None:
        return second
    if second is None:
        return first
    return jnp.logical_and(first, second)


class Place:
    def __init__(self, n, cores):
        self.n, self.cores, self.lines = n, cores, n // 4
        self.c, self.f = lax.axis_index("ctx"), lax.axis_index("fsdp")
        self.z, self.y, self.x = self.split(self.c)
        z, y, x, top = self.z, self.y, self.x, self.lines - 1
        self.peers = {
            ("z", 1): (self.index(jnp.minimum(z + 1, top), y, x), z < top),
            ("z", -1): (self.index(jnp.maximum(z - 1, 0), y, x), z > 0),
            ("y", 1): (self.index(z, 1 - y, x), None),
            ("x", 1): (self.index(z, y, 1 - x), None),
        }

    @staticmethod
    def split(c):
        return c // 4, (c // 2) % 2, c % 2

    @staticmethod
    def index(z, y, x):
        return z * 4 + y * 2 + x

    def owner(self, rel):
        oz = self.z + rel["z"]
        cond = None if rel["z"] == 0 else (oz >= 0) & (oz < self.lines)
        oz = jnp.clip(oz, 0, self.lines - 1)
        oy = 1 - self.y if rel["y"] else self.y
        ox = 1 - self.x if rel["x"] else self.x
        return cond, self.index(oz, oy, ox)


SLOT = {("z", 1): 0, ("z", -1): 1, ("y", 1): 2, ("x", 1): 3}


def offsets(n, order):
    lines = n // 4
    found = []
    for a in range(1 - lines, lines):
        for y in range(2):
            for x in range(2):
                rel = {"z": a, "y": y, "x": x}
                used = [k for k, d in enumerate(order) if rel[d] != 0]
                found.append((rel, used[-1] if used else -1, abs(a) + y + x))
    return found


class Gather:
    peers = "near"

    def __init__(self, rows, cols, dtype, place, spread=False, light=False):
        self.rows, self.cols, self.dtype, self.place = rows, cols, dtype, place
        self.spread, self.light = spread, light

    def setup(self, n, cores):
        self.n, self.cores, self.parts = n, cores, pieces(self.rows, self.light)
        k = len(self.parts)
        count = n * cores if self.spread else n
        self.out = jax.ShapeDtypeStruct((count * self.rows, self.cols), self.dtype)
        self.out_spec = pl.BlockSpec(memory_space=pl.ANY)
        self.scratch = [
            pltpu.SemaphoreType.DMA((k, 4, n)),
            pltpu.SemaphoreType.DMA((k, n)),
            pltpu.SemaphoreType.DMA((k,)),
        ]
        if self.spread:
            self.scratch += [pltpu.SemaphoreType.DMA((k, n, cores))] * 2

    def events(self, at, src, out, send_sem, recv_sem, own_sem, *pair_sems):
        n, cores, parts = self.n, self.cores, self.parts
        sent, kept, events = [], [], []

        def rows_of(i, owner, core=None):
            if self.spread:
                owner = owner * cores + (at.f if core is None else core)
            return pl.ds(self.place(owner, parts[i][0]), parts[i][1])

        def pair_copy(i, rel, k):
            cond, owner = at.owner(rel)
            core = lax.rem(at.f + k, cores)
            there = out.at[rows_of(i, owner)]
            here = src.at[pl.ds(parts[i][0], parts[i][1])]
            return cond, pltpu.make_async_remote_copy(
                src_ref=there if any(rel.values()) else here,
                dst_ref=there,
                send_sem=pair_sems[0].at[i, owner, core],
                recv_sem=pair_sems[1].at[i, owner, at.f],
                device_id={"fsdp": core},
                device_id_type=MESH,
            )

        def go(make):
            cond, copy = make()
            maybe(cond, copy.start)
            sent.append(make)

        def share(i, rel):
            for k in range(1, cores):
                go(functools.partial(pair_copy, i, rel, k))

        def link_copy(i, rel, key):
            cond, owner = at.owner(rel)
            peer, ok = at.peers[key]
            there = out.at[rows_of(i, owner)]
            here = src.at[pl.ds(parts[i][0], parts[i][1])]
            return both(cond, ok), pltpu.make_async_remote_copy(
                src_ref=there if any(rel.values()) else here,
                dst_ref=there,
                send_sem=send_sem.at[i, SLOT[key], owner],
                recv_sem=recv_sem.at[i, owner],
                device_id={"ctx": peer},
                device_id_type=MESH,
            )

        def onward(i, rel, last):
            order = parts[i][2]
            keys = []
            if last >= 0 and order[last] == "z":
                keys.append(("z", 1 if rel["z"] < 0 else -1))
            for d in order[last + 1 :]:
                keys += [("z", 1), ("z", -1)] if d == "z" else [(d, 1)]
            for key in keys:
                go(functools.partial(link_copy, i, rel, key))

        def begin():
            still = {"z": 0, "y": 0, "x": 0}
            for i in range(len(parts)):
                onward(i, still, -1)
            for i, (start, rows, order) in enumerate(parts):
                copy = pltpu.make_async_copy(
                    src.at[pl.ds(start, rows)], out.at[rows_of(i, at.c)], own_sem.at[i]
                )
                copy.start()
                kept.append(copy)
                if self.spread:
                    share(i, still)

        def arrive(i, rel, last):
            cond, owner = at.owner(rel)
            there = out.at[rows_of(i, owner)]
            maybe(
                cond,
                lambda: pltpu.make_async_copy(there, there, recv_sem.at[i, owner]).wait(),
            )
            onward(i, rel, last)
            if self.spread:
                share(i, rel)

        def end():
            if self.spread:
                for i in range(len(parts)):
                    for owner in range(n):
                        for k in range(1, cores):
                            core = lax.rem(at.f + k, cores)
                            there = out.at[rows_of(i, owner, core)]
                            pltpu.make_async_copy(
                                there, there, pair_sems[1].at[i, owner, core]
                            ).wait()
            for make in sent:
                cond, copy = make()
                maybe(cond, copy.wait_send)
            for copy in kept:
                copy.wait()

        events.append((-1, begin))
        for i, part in enumerate(parts):
            for rel, last, hops in offsets(n, part[2]):
                if last >= 0:
                    events.append((hops, functools.partial(arrive, i, rel, last)))
        events.append((1000, end))
        return events


class Fold:
    def __init__(self, n, cores, rows, cols, dtype):
        self.n, self.cores, self.rows, self.cols, self.dtype = n, cores, rows, cols, dtype
        self.scratch = [
            pltpu.VMEM((cores - 1, n, rows, cols), dtype),
            pltpu.VMEM((n, rows, cols), dtype),
            pltpu.SemaphoreType.DMA((cores,)),
            pltpu.SemaphoreType.DMA((cores,)),
            pltpu.SemaphoreType.DMA((1,)),
        ]

    def events(self, at, src, held, total, send_sem, recv_sem, own_sem):
        cores, sent = self.cores, []

        def begin():
            for k in range(1, cores):
                core = lax.rem(at.f + k, cores)
                copy = pltpu.make_async_remote_copy(
                    src_ref=src.at[:, core],
                    dst_ref=held.at[cores - 1 - k],
                    send_sem=send_sem.at[k],
                    recv_sem=recv_sem.at[cores - k],
                    device_id={"fsdp": core},
                    device_id_type=MESH,
                )
                copy.start()
                sent.append(copy)
            pltpu.make_async_copy(src.at[:, at.f], total, own_sem.at[0]).start()

        def work():
            pltpu.make_async_copy(src.at[:, at.f], total, own_sem.at[0]).wait()
            for k in range(1, cores):
                pltpu.make_async_copy(held.at[k - 1], held.at[k - 1], recv_sem.at[k]).wait()
            tiles = self.rows // 16

            def step(j, carry):
                owner, to = j // tiles, pl.ds(pl.multiple_of(lax.rem(j, tiles) * 16, 16), 16)
                value = total[owner, to].astype(jnp.float32)
                for k in range(cores - 1):
                    value = value + held[k, owner, to].astype(jnp.float32)
                total[owner, to] = value.astype(self.dtype)
                return carry

            lax.fori_loop(0, self.n * tiles, step, 0)
            for copy in sent:
                copy.wait_send()

        return [(-3, begin), (-2, work)]


class Halves:
    peers, spread = "near", True

    def __init__(self, shape, dtype, axis):
        self.shape, self.dtype, self.axis = shape, dtype, axis

    def setup(self, n, cores):
        self.cores, self.part = cores, list(self.shape)
        self.part[self.axis] //= cores
        self.out = jax.ShapeDtypeStruct((cores - 1,) + tuple(self.part), self.dtype)
        self.out_spec = pl.BlockSpec(memory_space=pl.ANY)
        self.scratch = [pltpu.SemaphoreType.DMA((2, cores))]

    def events(self, at, src, out, sems):
        cores, size = self.cores, self.part[self.axis]

        def copy(k):
            other = lax.rem(at.f + k, cores)
            place = pl.ds(pl.multiple_of(other * size, 128), size)
            return pltpu.make_async_remote_copy(
                src_ref=src.at[place] if self.axis == 0 else src.at[:, place],
                dst_ref=out.at[cores - 1 - k],
                send_sem=sems.at[0, k],
                recv_sem=sems.at[1, cores - k],
                device_id={"fsdp": other},
                device_id_type=MESH,
            )

        def begin():
            for k in range(1, cores):
                copy(k).start()

        def end():
            for k in range(1, cores):
                there = out.at[k - 1]
                pltpu.make_async_copy(there, there, sems.at[1, k]).wait()
                copy(k).wait_send()

        return [(-1, begin), (1000, end)]


class Reduce:
    peers = "near"

    def __init__(self, rows, cols, place, fold=False, light=False):
        self.rows, self.cols, self.place, self.light = rows, cols, place, light
        self.dtype = jnp.bfloat16
        self.spread = fold

    def setup(self, n, cores):
        self.n, self.parts = n, pieces(self.rows, self.light)
        lines, k = n // 4, len(self.parts)
        self.size = {"z": lines, "y": 2, "x": 2}
        self.table, total = [], 0
        for start, rows, order in self.parts:
            entry, ahead = {}, 1
            for d in order:
                entry[d] = total
                total += rows * ahead * (lines + 1 if d == "z" else 1)
                ahead *= self.size[d]
            self.table.append(entry)
        self.out = jax.ShapeDtypeStruct((self.rows, self.cols), jnp.float32)
        self.out_spec = pl.BlockSpec(memory_space=pltpu.VMEM)
        self.scratch = [
            pltpu.VMEM((total, self.cols), self.dtype),
            pltpu.SemaphoreType.DMA((k, 4, n)),
            pltpu.SemaphoreType.DMA((k, 4, n)),
        ]
        if self.spread:
            self.fold = Fold(n, cores, self.rows, self.cols, self.dtype)
            self.scratch += self.fold.scratch
        else:
            self.own_first, own_total = [], 0
            for start, rows, order in self.parts:
                self.own_first.append(own_total)
                own_total += rows * (n if order[2] == "z" else n // 2)
            self.scratch += [
                pltpu.VMEM((own_total, self.cols), self.dtype),
                pltpu.SemaphoreType.DMA((k, n)),
            ]

    def own_rows(self, i, owner, first, count):
        start, rows, order = self.parts[i]
        if self.spread:
            return owner, pl.ds(pl.multiple_of(start + first, 16), count)
        oz, oy, ox = Place.split(owner)
        number = {"z": owner, "y": oz * 2 + ox, "x": oz * 2 + oy}[order[2]]
        at = self.own_first[i] + number * rows + first
        return (pl.ds(pl.multiple_of(at, 16), count),)

    def held_rows(self, i, d, owner, line, up):
        start, rows, order = self.parts[i]
        oz, oy, ox = Place.split(owner)
        have = {"z": oz, "y": oy, "x": ox}
        number = 0
        for e in order[: order.index(d)]:
            number = number * self.size[e] + have[e]
        if d == "z":
            lines = self.size["z"]
            number = number * (lines + 1) + (oz if up else jnp.where(oz == line, lines, oz))
        return pl.ds(pl.multiple_of(self.table[i][d] + number * rows, 16), rows)

    def events(self, at, src, out, held, send_sem, recv_sem, *more):
        n, parts, lines = self.n, self.parts, self.n // 4
        sent, events = [], []
        if self.spread:
            events += self.fold.events(at, src, *more)
            own = more[1]
        else:
            own, own_sem = more

        def coming(i, rel, last):
            order = parts[i][2]
            come = []
            if last >= 0 and order[last] == "z":
                come.append(("z", 1 if rel["z"] < 0 else -1))
            for d in order[last + 1 :]:
                come += [("z", 1), ("z", -1)] if d == "z" else [(d, 1)]
            return come

        def fetch(i, owner):
            start, rows, order = parts[i]
            return pltpu.make_async_copy(
                src.at[pl.ds(self.place(owner, start), rows)],
                own.at[self.own_rows(i, owner, 0, rows)],
                own_sem.at[i, owner],
            )

        def begin(i, rel, last):
            if coming(i, rel, last):
                cond, owner = at.owner(rel)
                maybe(cond, fetch(i, owner).start)

        def tiles(rows, body):
            def step(r, carry):
                body(r * 16)
                return carry

            lax.fori_loop(0, rows // 16, step, 0)

        def tile(start, r):
            return pl.ds(pl.multiple_of(start + r, 16), 16)

        def work(i, rel, last):
            start, rows, order = parts[i]
            cond, owner = at.owner(rel)
            come = coming(i, rel, last)

            def arrived(d, way, add):
                ok = at.peers[(d, way)][1]
                got = self.held_rows(i, d, owner, at.z, way < 0)

                def take():
                    there = held.at[got]
                    pltpu.make_async_copy(there, there, recv_sem.at[i, SLOT[(d, way)], owner]).wait()
                    tiles(rows, lambda r: add(r, tile(got.start, r)))

                maybe(ok, take)

            def add_on(r, got):
                to = self.own_rows(i, owner, r, 16)
                own[to] = (own[to].astype(jnp.float32) + held[got].astype(jnp.float32)).astype(
                    self.dtype
                )

            def add_last(r, got):
                to = tile(start, r)
                out[to] = out[to] + held[got].astype(jnp.float32)

            def keep(r):
                out[tile(start, r)] = own[self.own_rows(i, owner, r, 16)].astype(jnp.float32)

            def take_all():
                if not self.spread:
                    fetch(i, owner).wait()
                if last < 0:
                    tiles(rows, keep)
                for d, way in come:
                    arrived(d, way, add_last if last < 0 else add_on)

            if come:
                maybe(cond, take_all)
            if last >= 0:
                make = functools.partial(link_copy, i, rel, last)
                cond, copy = make()
                maybe(cond, copy.start)
                sent.append(make)

        def link_copy(i, rel, last):
            start, rows, order = parts[i]
            cond, owner = at.owner(rel)
            d = order[last]
            way = 1 if d != "z" or rel["z"] > 0 else -1
            peer, ok = at.peers[(d, way)]
            there = self.held_rows(i, d, owner, at.z + (way if d == "z" else 0), way > 0)
            if coming(i, rel, last) or self.spread:
                mine = own.at[self.own_rows(i, owner, 0, rows)]
            else:
                mine = src.at[pl.ds(self.place(owner, start), rows)]
            return cond, pltpu.make_async_remote_copy(
                src_ref=mine,
                dst_ref=held.at[there],
                send_sem=send_sem.at[i, SLOT[(d, way)], owner],
                recv_sem=recv_sem.at[i, SLOT[(d, -way if d == "z" else 1)], owner],
                device_id={"ctx": peer},
                device_id_type=MESH,
            )

        def end():
            for make in sent:
                cond, copy = make()
                maybe(cond, copy.wait_send)

        for i, part in enumerate(parts):
            for rel, last, hops in offsets(n, part[2]):
                if not self.spread:
                    events.append((-1, functools.partial(begin, i, rel, last)))
                events.append((lines + 2 - hops, functools.partial(work, i, rel, last)))
        events.append((1000, end))
        return events


class Exchange:
    peers = "all"

    def __init__(self, rows, cols, dtype, spread=False, fold=False):
        self.rows, self.cols, self.dtype = rows, cols, dtype
        self.share, self.spread, self.folds = spread, spread or fold, fold

    def setup(self, n, cores):
        self.n, self.cores = n, cores
        shape = (n, cores, self.rows, self.cols) if self.share else (n, self.rows, self.cols)
        self.out = jax.ShapeDtypeStruct(shape, self.dtype)
        self.out_spec = pl.BlockSpec(memory_space=pl.ANY)
        self.scratch = [
            pltpu.SemaphoreType.DMA((n,)),
            pltpu.SemaphoreType.DMA((n,)),
            pltpu.SemaphoreType.DMA((1,)),
        ]
        if self.share:
            self.scratch += [pltpu.SemaphoreType.DMA((n, cores))] * 2
        if self.folds:
            self.fold = Fold(n, cores, self.rows, self.cols, self.dtype)
            self.scratch += self.fold.scratch

    def events(self, at, src, out, send_sem, recv_sem, own_sem, *more):
        n, cores = self.n, self.cores
        sent, kept, events = [], [], []
        pair_sems = more[:2]
        if self.folds:
            events += self.fold.events(at, src, *more)
            src = more[1]

        def there(owner):
            return out.at[owner, at.f] if self.share else out.at[owner]

        def pair_copy(k, step):
            owner, core = lax.rem(at.c + step, n), lax.rem(at.f + k, cores)
            return pltpu.make_async_remote_copy(
                src_ref=there(owner) if step else src.at[owner],
                dst_ref=there(owner),
                send_sem=pair_sems[0].at[owner, core],
                recv_sem=pair_sems[1].at[owner, at.f],
                device_id={"fsdp": core},
                device_id_type=MESH,
            )

        def link_copy(k):
            peer = lax.rem(at.c + k, n)
            return pltpu.make_async_remote_copy(
                src_ref=src.at[peer],
                dst_ref=there(at.c),
                send_sem=send_sem.at[peer],
                recv_sem=recv_sem.at[at.c],
                device_id={"ctx": peer},
                device_id_type=MESH,
            )

        def go(make):
            make().start()
            sent.append(make)

        def share(step):
            for k in range(1, cores):
                go(functools.partial(pair_copy, k, step))

        def begin():
            for k in range(1, n):
                go(functools.partial(link_copy, k))
            copy = pltpu.make_async_copy(src.at[at.c], there(at.c), own_sem.at[0])
            copy.start()
            kept.append(copy)
            if self.share:
                share(0)

        def arrive(k):
            owner = lax.rem(at.c + k, n)
            block = there(owner)
            pltpu.make_async_copy(block, block, recv_sem.at[owner]).wait()
            if self.share:
                share(k)

        def end():
            if self.share:
                for owner in range(n):
                    for k in range(1, cores):
                        core = lax.rem(at.f + k, cores)
                        block = out.at[owner, core]
                        pltpu.make_async_copy(block, block, pair_sems[1].at[owner, core]).wait()
            for make in sent:
                make().wait_send()
            for copy in kept:
                copy.wait()

        events.append((-1, begin))
        for k in range(1, n):
            events.append((100 + k, functools.partial(arrive, k)))
        events.append((1000, end))
        return events


def vmem_bytes(scratch):
    total = 0
    for s in scratch:
        if hasattr(s, "shape") and s.dtype in (jnp.bfloat16, jnp.float32, jnp.int32):
            size = s.dtype.itemsize * -(-s.shape[-1] // 128) * 128
            for k in s.shape[:-1]:
                size *= k
            total += size
    return total


def communicate(name, number, n, cores, ops, arrays, work=None, work_arrays=()):
    everyone = any(op.peers == "all" for op in ops)
    spread = any(op.spread for op in ops)
    outs = [op.out for op in ops] + (work.outs if work else [])
    anywhere = pl.BlockSpec(memory_space=pl.ANY)

    def kernel(*refs):
        at = Place(n, cores)
        if ops:
            barrier = pltpu.get_barrier_semaphore()
        if not ops:
            pass
        elif everyone:
            for j in range(1, n):
                pl.semaphore_signal(
                    barrier, 1, device_id={"ctx": lax.rem(at.c + j, n)}, device_id_type=MESH
                )
            count = n - 1
        else:
            for peer, ok in at.peers.values():
                maybe(
                    ok,
                    lambda peer=peer: pl.semaphore_signal(
                        barrier, 1, device_id={"ctx": peer}, device_id_type=MESH
                    ),
                )
            count = 2 + (at.z > 0).astype(jnp.int32) + (at.z < at.lines - 1).astype(jnp.int32)
        if ops and spread:
            for j in range(1, cores):
                pl.semaphore_signal(
                    barrier, 1, device_id={"fsdp": lax.rem(at.f + j, cores)}, device_id_type=MESH
                )
            count = count + cores - 1
        if ops:
            pl.semaphore_wait(barrier, count)
        k, inputs = len(ops), len(ops) + len(work_arrays)
        events, first = [], inputs + len(outs)
        for j, op in enumerate(ops):
            mine = refs[first : first + len(op.scratch)]
            first += len(op.scratch)
            events += op.events(at, refs[j], refs[inputs + j], *mine)
        events = sorted(events, key=lambda e: e[0])
        if not work:
            for _, event in events:
                event()
            return
        for time, event in events:
            if time < 0:
                event()
        between = [event for time, event in events if 0 <= time < 1000]
        loops = work.loops(refs[k:inputs], refs[inputs + k : inputs + len(outs)], refs[first:])
        steps, done = sum(loop[1] for loop in loops), 0
        for before, turns, body, after in loops:
            before()

            def turn(i, carry, done=done, turns=turns, body=body):
                for j in range(turns):
                    low, high = ((done + j + d) * len(between) // steps for d in range(2))
                    if high > low:

                        @pl.when(i == j)
                        def _(low=low, high=high):
                            for event in between[low:high]:
                                event()

                body(i)
                return carry

            lax.fori_loop(0, turns, turn, 0)
            after()
            done += turns
        for time, event in events:
            if time >= 1000:
                event()

    return pl.pallas_call(
        kernel,
        out_shape=outs,
        in_specs=[anywhere] * (len(ops) + len(work_arrays)),
        out_specs=[op.out_spec for op in ops] + [anywhere] * (len(outs) - len(ops)),
        scratch_shapes=[s for op in ops for s in op.scratch] + (work.scratch if work else []),
        compiler_params=pltpu.CompilerParams(
            collective_id=number if ops else None,
            has_side_effects=bool(ops),
            vmem_limit_bytes=(60 if work else 48) << 20,
        ),
        name=name,
    )(*arrays, *work_arrays)


class Products:
    def __init__(self, arrays, jobs, shared):
        self.arrays, self.jobs, self.shared = arrays, jobs, shared
        self.outs, self.scratch = [], []
        for left, right, axis, width in jobs:
            shape = (arrays[left].shape[0], arrays[right].shape[1])
            self.outs.append(jax.ShapeDtypeStruct(shape, jnp.bfloat16))
            piece = (width, shape[1]) if axis == 0 else (shape[0], width)
            self.scratch.append(pltpu.VMEM((2,) + piece, jnp.bfloat16))
        self.scratch.append(pltpu.SemaphoreType.DMA((len(jobs), 2)))
        self.scratch.append(pltpu.SemaphoreType.DMA((len(arrays),)))
        later = [second for first, second in shared]
        self.held = [i for i in range(len(arrays)) if i not in later]
        self.scratch += [pltpu.VMEM(arrays[i].shape, arrays[i].dtype) for i in self.held]

    def loops(self, ins, outs, scratch):
        jobs = self.jobs
        stages, (out_sem, in_sem) = scratch[: len(jobs)], scratch[len(jobs) : len(jobs) + 2]
        kept = dict(zip(self.held, scratch[len(jobs) + 2 :]))
        for first, second in self.shared:
            kept[second] = kept[first]
        ready = set()
        follows = dict(self.shared)
        begun = set(self.held)

        def load(i):
            return pltpu.make_async_copy(ins[i], kept[i], in_sem.at[i])

        def make(number):
            left, right, axis, width = jobs[number]
            shape = self.outs[number].shape
            turns = shape[axis] // width
            stage = stages[number]

            def out_copy(i):
                slot = lax.rem(i, 2)
                at = pl.ds(pl.multiple_of(i * width, 128), width)
                there = outs[number].at[at] if axis == 0 else outs[number].at[:, at]
                return pltpu.make_async_copy(stage.at[slot], there, out_sem.at[number, slot])

            def before():
                if number == 0:
                    for i in self.held:
                        load(i).start()
                for i in (left, right):
                    if i not in ready:
                        load(i).wait()
                        ready.add(i)

            def body(i):
                @pl.when(i >= 2)
                def _():
                    out_copy(i - 2).wait()

                at = pl.ds(pl.multiple_of(i * width, 128), width)
                a = kept[left][at] if axis == 0 else kept[left][...]
                b = kept[right][...] if axis == 0 else kept[right][:, at]
                stage[lax.rem(i, 2)] = jnp.dot(a, b, preferred_element_type=jnp.float32).astype(
                    jnp.bfloat16
                )
                out_copy(i).start()

            def after():
                for i in range(max(0, turns - 2), turns):
                    out_copy(i).wait()
                for i in (left, right):
                    if i in follows:
                        load(follows.pop(i)).start()

            return before, turns, body, after

        return [make(number) for number in range(len(jobs))]


class Staged:
    def __init__(self):
        self.arrays, self.outs, self.scratch = [], [], []
        self.sem_rows = 0
        self.sems = self.add(pltpu.SemaphoreType.DMA((128, 2)))

    def add(self, scratch):
        self.scratch.append(scratch)
        return len(self.scratch) - 1

    def hold(self, shape, dtype):
        return self.add(pltpu.VMEM(shape, dtype))

    def take(self, array):
        self.arrays.append(array)
        return len(self.arrays) - 1

    def give(self, shape, dtype):
        self.outs.append(jax.ShapeDtypeStruct(shape, dtype))
        return len(self.outs) - 1

    def loops(self, ins, outs, scratch):
        self.ins, self.gives, self.refs = ins, outs, scratch
        self.sem_rows, self.first = 0, []
        found = self.build()
        start = found[0][0]

        def begin():
            for copy in self.first:
                copy.start()
            start()

        return [(begin,) + found[0][1:]] + found[1:]

    def new_sems(self, count):
        self.sem_rows += count
        return [self.refs[self.sems].at[self.sem_rows - count + k] for k in range(count)]

    def whole(self, number, held):
        (sem,) = self.new_sems(1)
        copy = pltpu.make_async_copy(self.ins[number], self.refs[held], sem.at[0])
        self.first.append(copy)
        return copy.wait

    def stage(self, turns, loads, stores, body, ready=(), late=False):
        load_sems, store_sems = self.new_sems(len(loads)), self.new_sems(len(stores))

        def load(k, i, slot):
            return pltpu.make_async_copy(*loads[k](i, slot), load_sems[k].at[slot])

        def store(k, i, slot):
            return pltpu.make_async_copy(*stores[k](i, slot), store_sems[k].at[slot])

        if not late:
            for k in range(len(loads)):
                self.first.append(load(k, 0, 0))

        def before():
            for wait in ready:
                wait()
            if late:
                for k in range(len(loads)):
                    load(k, 0, 0).start()

        def turn(i):
            slot = lax.rem(i, 2)
            for k in range(len(loads)):
                load(k, i, slot).wait()

            @pl.when(i + 1 < turns)
            def _():
                for k in range(len(loads)):
                    load(k, i + 1, 1 - slot).start()

            @pl.when(i >= 2)
            def _():
                for k in range(len(stores)):
                    store(k, i - 2, slot).wait()

            body(i, slot)
            for k in range(len(stores)):
                store(k, i, slot).start()

        def after():
            for i in range(max(0, turns - 2), turns):
                for k in range(len(stores)):
                    store(k, i, i % 2).wait()

        return before, turns, turn, after


def span(i, width, unit=128):
    return pl.ds(pl.multiple_of(i * width, unit), width)


class Cast(Staged):
    def __init__(self, arrays):
        super().__init__()
        self.held = []
        for a in arrays:
            self.take(a)
            self.give(a.shape, jnp.bfloat16)
            self.held.append(
                (
                    self.hold((2, 128, a.shape[1]), jnp.float32),
                    self.hold((2, 128, a.shape[1]), jnp.bfloat16),
                )
            )

    def build(self):
        def one(k):
            wide, low = (self.refs[j] for j in self.held[k])
            src, out = self.ins[k], self.gives[k]

            def body(i, slot):
                low[slot] = wide[slot].astype(jnp.bfloat16)

            return self.stage(
                src.shape[0] // 128,
                [lambda i, s: (src.at[span(i, 128)], wide.at[s])],
                [lambda i, s: (low.at[s], out.at[span(i, 128)])],
                body,
            )

        return [one(k) for k in range(len(self.held))]


def wide_dot(left, right):
    return jnp.dot(left, right, preferred_element_type=jnp.float32)


def across(left, right):
    return lax.dot_general(
        left, right, (((1,), (1,)), ((), ())), preferred_element_type=jnp.float32
    )


def norm_rows(values):
    return values * lax.rsqrt(jnp.mean(values * values, axis=-1, keepdims=True) + EPS)


def turned(values):
    return jnp.transpose(values.astype(jnp.float32)).astype(values.dtype)


def select(slots, column):
    place = lax.broadcasted_iota(jnp.int32, (column.shape[0], slots), 1).astype(jnp.float32)
    return jnp.where(place == column, 1.0, 0.0).astype(jnp.bfloat16)


def select_t(slots, row):
    place = lax.broadcasted_iota(jnp.int32, (slots, row.shape[1]), 0).astype(jnp.float32)
    return jnp.where(place == row, 1.0, 0.0).astype(jnp.bfloat16)


class ExpertForward(Staged):
    def __init__(self, gate, up, down, ffn, shared_in, shared_out, router, chosen, column, row, lane):
        super().__init__()
        low, wide = jnp.bfloat16, jnp.float32
        self.pairs, self.slots, self.tokens = row.shape[0], row.slots, row.shape[2]
        rows, fe, seq = self.pairs * self.slots, gate.shape[1], ffn.shape[0]
        wp = shared_out.shape[1]
        self.fe, self.wp, self.lane = fe, wp, lane
        for a in (gate, up, down, ffn, shared_in, shared_out, router, chosen, column, row.array):
            self.take(a)
        self.give((rows, 2 * fe), wide)
        self.give((fe, rows), low)
        self.give((rows, D), low)
        self.give((D, rows), low)
        self.give((seq, 2 * wp), wide)
        self.give((wp, seq), low)
        self.give((seq, D), low)
        self.give((seq, 128), wide)
        self.give((seq, 128), wide)
        self.held = {
            "arrived": self.hold((rows, D), low),
            "tile": self.hold((2, D, 256), low),
            "hidden": self.hold((rows, fe), low),
            "pre": self.hold((2, rows, 256), wide),
            "hidden_t": self.hold((2, 128, rows), low),
            "down": self.hold((2, fe, 256), low),
            "y": self.hold((rows, D), low),
            "y_out": self.hold((2, rows, 256), low),
            "arrived_t": self.hold((2, 256, rows), low),
            "ffn": self.hold((2, self.tokens, D), low),
            "chosen": self.hold((2, self.tokens, 128), low),
            "gates": self.hold((2, self.tokens, 128), wide),
            "gate_out": self.hold((2, self.tokens, 128), wide),
            "gate": self.hold((seq, 128), wide),
            "shared_in": self.hold((D, 2 * wp), low),
            "shared_hidden": self.hold((seq, wp), low),
            "shared_pre": self.hold((2, self.tokens, 2 * wp), wide),
            "shared_t": self.hold((2, wp, self.tokens), low),
            "shared_out": self.hold((D, wp), low),
            "router": self.hold((D, 128), low),
            "column": self.hold((seq, 128), wide),
            "row": self.hold(row.shape, wide),
            "out": self.hold((2, self.tokens, D), low),
        }

    def build(self):
        low = jnp.bfloat16
        r = {name: self.refs[k] for name, k in self.held.items()}
        gate, up, down, ffn = self.ins[:4]
        chosen = self.ins[7]
        pre, hidden_t, y, arrived_t, shared_pre, shared_t, out, gates, gate_out = self.gives
        fe, wp, tokens, slots = self.fe, self.wp, self.tokens, self.slots
        mine = self.lane + lax.axis_index("ctx")
        ready = {
            name: self.whole(k, self.held[name])
            for name, k in (
                ("shared_in", 4),
                ("shared_out", 5),
                ("router", 6),
                ("column", 8),
                ("row", 9),
            )
        }

        def rows_in(i, slot):
            at = span(i, tokens)
            rows = r["ffn"][slot]
            marks = r["chosen"][slot].astype(jnp.float32) > 0.5
            logits = jnp.where(marks, wide_dot(rows, r["router"][...]), NEG)
            shifted = jnp.exp(logits - jnp.max(logits, axis=-1, keepdims=True))
            shifted = jnp.where(marks, shifted, 0.0)
            parts = shifted / jnp.sum(shifted, axis=-1, keepdims=True)
            r["gates"][slot] = parts
            lanes = lax.broadcasted_iota(jnp.int32, parts.shape, 1)
            part = jnp.sum(jnp.where(lanes == mine, parts, 0.0), axis=-1, keepdims=True)
            part = jnp.broadcast_to(part, parts.shape)
            r["gate"][at] = part
            r["gate_out"][slot] = part
            r["arrived"][span(i, slots, 16)] = wide_dot(select_t(slots, r["row"][i]), rows).astype(
                low
            )
            both_ = wide_dot(rows, r["shared_in"][...])
            r["shared_pre"][slot] = both_
            first = both_[:, :wp]
            value = (first * jax.nn.sigmoid(first) * both_[:, wp:]).astype(low)
            r["shared_hidden"][at] = value
            r["shared_t"][slot] = turned(value)

        def expert_in(i, slot):
            both_ = wide_dot(r["arrived"][...], r["tile"][slot])
            r["pre"][slot] = both_
            first = both_[:, :128]
            value = (first * jax.nn.sigmoid(first) * both_[:, 128:]).astype(low)
            r["hidden"][:, span(i, 128)] = value
            r["hidden_t"][slot] = turned(value)

        def expert_out(i, slot):
            value = wide_dot(r["hidden"][...], r["down"][slot]).astype(low)
            r["y"][:, span(i, 256)] = value
            r["y_out"][slot] = value
            r["arrived_t"][slot] = turned(r["arrived"][:, span(i, 256)])

        def result(i, slot):
            at = span(i, tokens)
            routed = wide_dot(select(slots, r["column"][at, 0:1]), r["y"][span(i, slots, 16)])
            more = across(r["shared_hidden"][at], r["shared_out"][...])
            r["out"][slot] = (r["gate"][at, 0:1] * routed + more).astype(low)

        return [
            self.stage(
                self.pairs,
                [
                    lambda i, s: (ffn.at[span(i, tokens)], r["ffn"].at[s]),
                    lambda i, s: (chosen.at[span(i, tokens)], r["chosen"].at[s]),
                ],
                [
                    lambda i, s: (r["shared_pre"].at[s], shared_pre.at[span(i, tokens)]),
                    lambda i, s: (r["shared_t"].at[s], shared_t.at[:, span(i, tokens)]),
                    lambda i, s: (r["gates"].at[s], gates.at[span(i, tokens)]),
                    lambda i, s: (r["gate_out"].at[s], gate_out.at[span(i, tokens)]),
                ],
                rows_in,
                [ready["shared_in"], ready["router"], ready["row"]],
            ),
            self.stage(
                fe // 128,
                [
                    lambda i, s: (gate.at[:, span(i, 128)], r["tile"].at[s, :, pl.ds(0, 128)]),
                    lambda i, s: (up.at[:, span(i, 128)], r["tile"].at[s, :, pl.ds(128, 128)]),
                ],
                [
                    lambda i, s: (r["pre"].at[s], pre.at[:, span(i, 256)]),
                    lambda i, s: (r["hidden_t"].at[s], hidden_t.at[span(i, 128)]),
                ],
                expert_in,
            ),
            self.stage(
                D // 256,
                [lambda i, s: (down.at[:, span(i, 256)], r["down"].at[s])],
                [
                    lambda i, s: (r["y_out"].at[s], y.at[:, span(i, 256)]),
                    lambda i, s: (r["arrived_t"].at[s], arrived_t.at[span(i, 256)]),
                ],
                expert_out,
            ),
            self.stage(
                self.pairs,
                [],
                [lambda i, s: (r["out"].at[s], out.at[span(i, tokens)])],
                result,
                [ready["shared_out"], ready["column"]],
            ),
        ]


class Slots:
    def __init__(self, array, slots):
        self.array, self.shape, self.slots = array, array.shape, slots


class ExpertBackward(Staged):
    def __init__(
        self, gate, up, down, grad, y, row_gate, pre, shared_pre, shared_in, shared_out, column, row
    ):
        super().__init__()
        low, wide = jnp.bfloat16, jnp.float32
        self.pairs, self.slots, self.tokens = row.shape[0], row.slots, row.shape[2]
        rows, fe, seq = self.pairs * self.slots, gate.shape[1], grad.shape[0]
        wp = shared_out.shape[1]
        self.fe, self.wp = fe, wp
        for a in (gate, up, down, grad, y, row_gate, pre, shared_pre, shared_in, shared_out, column):
            self.take(a)
        self.take(row.array)
        self.give((rows, D), low)
        self.give((rows, fe), low)
        self.give((rows, fe), low)
        self.give((2 * wp, seq), low)
        self.give((2 * self.pairs, 8, self.tokens // 2), wide)
        self.give((seq, D), low)
        self.held = {
            "rows": self.hold((rows, D), low),
            "pre": self.hold((2, rows, 512), wide),
            "down": self.hold((2, 256, D), low),
            "pre_last": self.hold((2, rows, 256), wide),
            "down_last": self.hold((2, 128, D), low),
            "d_gate": self.hold((rows, fe), low),
            "d_up": self.hold((rows, fe), low),
            "gate": self.hold((2, 256, fe), low),
            "up": self.hold((2, 256, fe), low),
            "grad": self.hold((2, self.tokens, D), low),
            "y": self.hold((2, self.slots, D), low),
            "row_gate": self.hold((2, self.tokens, 128), wide),
            "gate_grad": self.hold((2, 2, 8, self.tokens // 2), wide),
            "shared_pre": self.hold((2, self.tokens, 2 * wp), wide),
            "shared_out": self.hold((D, wp), low),
            "d_shared": self.hold((seq, 2 * wp), low),
            "shared_t": self.hold((2, 2 * wp, self.tokens), low),
            "shared_in": self.hold((D, 2 * wp), low),
            "column": self.hold((seq, 128), wide),
            "row": self.hold(row.shape, wide),
            "out": self.hold((2, self.tokens, D), low),
        }

    def build(self):
        low, wide = jnp.bfloat16, jnp.float32
        r = {name: self.refs[k] for name, k in self.held.items()}
        gate, up, down, grad, y, row_gate, pre, shared_pre = self.ins[:8]
        grad_rows, d_gate, d_up, shared_t, gate_grad, out = self.gives
        fe, wp, tokens, slots = self.fe, self.wp, self.tokens, self.slots
        ready = {
            name: self.whole(k, self.held[name])
            for name, k in (("shared_in", 8), ("shared_out", 9), ("column", 10), ("row", 11))
        }

        def slopes(first, second, grads):
            sigmoid = jax.nn.sigmoid(first)
            act = first * sigmoid
            slope = sigmoid * (1.0 + first * (1.0 - sigmoid))
            return (grads * second * slope).astype(low), (grads * act).astype(low)

        def rows_in(i, slot):
            at = span(i, tokens)
            grads = r["grad"][slot]
            exact = grads.astype(wide)
            weighted = (r["row_gate"][slot, :, 0:1] * exact).astype(low)
            r["rows"][span(i, slots, 16)] = wide_dot(
                select_t(slots, r["row"][i]), weighted
            ).astype(low)
            results = wide_dot(select(slots, r["column"][at, 0:1]), r["y"][slot])
            gained = jnp.sum(results * exact, axis=-1, keepdims=True)
            gained = jnp.transpose(jnp.broadcast_to(gained, (tokens, 128)))
            for k in range(2):
                r["gate_grad"][slot, k] = gained[:8, k * (tokens // 2) : (k + 1) * (tokens // 2)]
            hidden_grads = wide_dot(grads, r["shared_out"][...])
            values = r["shared_pre"][slot]
            one, two = slopes(values[:, :wp], values[:, wp:], hidden_grads)
            value = jnp.concatenate([one, two], axis=1)
            r["d_shared"][at] = value
            r["shared_t"][slot] = turned(value)

        def expert_hidden(i, slot):
            grads = across(r["rows"][...], r["down"][slot])
            values = r["pre"][slot]
            first = jnp.concatenate([values[:, :128], values[:, 256:384]], axis=1)
            second = jnp.concatenate([values[:, 128:256], values[:, 384:]], axis=1)
            one, two = slopes(first, second, grads)
            r["d_gate"][:, span(i, 256)] = one
            r["d_up"][:, span(i, 256)] = two

        def expert_hidden_last(i, slot):
            grads = across(r["rows"][...], r["down_last"][slot])
            values = r["pre_last"][slot]
            one, two = slopes(values[:, :128], values[:, 128:], grads)
            at = pl.ds(even, 128)
            r["d_gate"][:, at] = one
            r["d_up"][:, at] = two

        def expert_rows(i, slot):
            value = across(r["d_gate"][...], r["gate"][slot])
            value = value + across(r["d_up"][...], r["up"][slot])
            r["rows"][:, span(i, 256)] = value.astype(low)

        def result(i, slot):
            at = span(i, tokens)
            value = wide_dot(select(slots, r["column"][at, 0:1]), r["rows"][span(i, slots, 16)])
            value = value + across(r["d_shared"][at], r["shared_in"][...])
            r["out"][slot] = value.astype(low)

        even = fe // 256 * 256
        found = [
            self.stage(
                self.pairs,
                [
                    lambda i, s: (grad.at[span(i, tokens)], r["grad"].at[s]),
                    lambda i, s: (y.at[span(i, slots, 16)], r["y"].at[s]),
                    lambda i, s: (row_gate.at[span(i, tokens)], r["row_gate"].at[s]),
                    lambda i, s: (shared_pre.at[span(i, tokens)], r["shared_pre"].at[s]),
                ],
                [
                    lambda i, s: (r["shared_t"].at[s], shared_t.at[:, span(i, tokens)]),
                    lambda i, s: (r["gate_grad"].at[s], gate_grad.at[pl.ds(2 * i, 2)]),
                    lambda i, s: (
                        r["rows"].at[span(i, slots, 16)],
                        grad_rows.at[span(i, slots, 16)],
                    ),
                ],
                rows_in,
                [ready["shared_out"], ready["column"], ready["row"]],
            ),
            self.stage(
                even // 256,
                [
                    lambda i, s: (down.at[span(i, 256)], r["down"].at[s]),
                    lambda i, s: (pre.at[:, span(i, 512)], r["pre"].at[s]),
                ],
                [],
                expert_hidden,
            ),
        ]
        if even < fe:
            found.append(
                self.stage(
                    1,
                    [
                        lambda i, s: (down.at[pl.ds(even, 128)], r["down_last"].at[s]),
                        lambda i, s: (pre.at[:, pl.ds(2 * even, 256)], r["pre_last"].at[s]),
                    ],
                    [],
                    expert_hidden_last,
                )
            )
        return found + [
            self.stage(
                D // 256,
                [
                    lambda i, s: (gate.at[span(i, 256)], r["gate"].at[s]),
                    lambda i, s: (up.at[span(i, 256)], r["up"].at[s]),
                ],
                [],
                expert_rows,
            ),
            self.stage(
                1,
                [],
                [lambda i, s: (r["d_gate"], d_gate), lambda i, s: (r["d_up"], d_up)],
                lambda i, s: None,
            ),
            self.stage(
                self.pairs,
                [],
                [lambda i, s: (r["out"].at[s], out.at[span(i, tokens)])],
                result,
                [ready["shared_in"]],
            ),
        ]


class Heads(Staged):
    def __init__(self, inputs, gain, head, small, kvb, gain_latent, turns, starts, scale):
        super().__init__()
        low, wide = jnp.bfloat16, jnp.float32
        seq = inputs.shape[0]
        self.seq, self.scale, self.n = seq, scale, seq // 128
        for a in (inputs, gain, head, small, kvb, gain_latent, turns, starts):
            self.take(a)
        self.give((seq, D), low)
        self.give((seq, RANK), low)
        self.give((seq, 256), low)
        self.give((seq, 256), low)
        self.give((seq, VDIM), low)
        self.give((seq, VDIM), wide)
        self.give((seq, 128), wide)
        self.give((self.n, 128, VDIM), low)
        self.held = {
            "inputs": self.hold((2, BLOCK, D), low),
            "normed": self.hold((2, BLOCK, D), low),
            "latent": self.hold((2, BLOCK, RANK), low),
            "turns": self.hold((2, BLOCK, 256), wide),
            "gain": self.hold((8, D), wide),
            "head": self.hold(head.shape, low),
            "small": self.hold(small.shape, low),
            "kvb": self.hold(kvb.shape, low),
            "gain_latent": self.hold((8, RANK), wide),
            "starts": self.hold(starts.shape, jnp.int32),
            "query": self.hold((seq, 256), low),
            "key": self.hold((seq, 256), low),
            "value": self.hold((seq, VDIM), low),
            "attended": self.hold((seq, VDIM), wide),
            "log_total": self.hold((seq, 128), wide),
            "result": self.hold((seq, VDIM), low),
        }

    def build(self):
        low, wide = jnp.bfloat16, jnp.float32
        r = {name: self.refs[k] for name, k in self.held.items()}
        inputs, turns = self.ins[0], self.ins[6]
        normed, latent, query, key, value, attended, log_total, blocks = self.gives
        n = self.n
        ready = [
            self.whole(k, self.held[name])
            for name, k in (
                ("gain", 1),
                ("head", 2),
                ("small", 3),
                ("kvb", 4),
                ("gain_latent", 5),
                ("starts", 7),
            )
        ]

        def rope(values, slot):
            lanes = lax.broadcasted_iota(jnp.int32, values.shape, 1)
            half = ROPE // 2
            partner = jnp.where(
                lanes < half, pltpu.roll(values, 128 - half, 1), pltpu.roll(values, half, 1)
            )
            turned_ = values * r["turns"][slot, :, :128] + partner * r["turns"][slot, :, 128:]
            return jnp.where(lanes < ROPE, turned_, 0.0).astype(low)

        def project(i, slot):
            at = span(i, BLOCK)
            rows = norm_rows(r["inputs"][slot].astype(wide)) * r["gain"][0:1]
            rows = rows.astype(low)
            r["normed"][slot] = rows
            raw = wide_dot(rows, r["head"][...])
            r["query"][at, pl.ds(0, 128)] = raw[:, :128].astype(low)
            r["query"][at, pl.ds(128, 128)] = rope(raw[:, 128:256], slot)
            packed = wide_dot(rows, r["small"][...])
            rows = (norm_rows(packed[:, :RANK]) * r["gain_latent"][0:1]).astype(low)
            r["latent"][slot] = rows
            pair = wide_dot(rows, r["kvb"][...]).astype(low)
            r["key"][at, pl.ds(0, 128)] = pair[:, :128]
            r["key"][at, pl.ds(128, 128)] = rope(packed[:, RANK : RANK + 128], slot)
            r["value"][at] = pair[:, 128:]

        def block(start):
            def body(i, slot):
                rows, reach = pl.ds(start, BLOCK), start + BLOCK
                scores = across(r["query"][rows], r["key"][:reach])
                seen = visible(r["starts"], start, scores.shape)
                scores = jnp.where(seen, scores * self.scale, NEG)
                peak = jnp.max(scores, axis=-1, keepdims=True)
                shifted = jnp.exp(scores - peak)
                total = jnp.sum(shifted, axis=-1, keepdims=True)
                probs = (shifted * (1.0 / total)).astype(low)
                found = wide_dot(probs, r["value"][:reach])
                r["attended"][rows] = found
                r["result"][rows] = found.astype(low)
                r["log_total"][rows] = jnp.broadcast_to(peak + jnp.log(total), (BLOCK, 128))

            def piece(k):
                owner, first = (k, 0) if k < n else (2 * n - 1 - k, 64)
                return lambda i, s: (
                    r["result"].at[pl.ds(64 * k, 64)],
                    blocks.at[owner, pl.ds(first, 64)],
                )

            first = start // 64
            return self.stage(1, [], [piece(first + k) for k in range(BLOCK // 64)], body)

        def whole_out(name, there):
            return lambda i, s: (r[name], there)

        return (
            [
                self.stage(
                    self.seq // BLOCK,
                    [
                        lambda i, s: (inputs.at[span(i, BLOCK)], r["inputs"].at[s]),
                        lambda i, s: (turns.at[span(i, BLOCK)], r["turns"].at[s]),
                    ],
                    [
                        lambda i, s: (r["normed"].at[s], normed.at[span(i, BLOCK)]),
                        lambda i, s: (r["latent"].at[s], latent.at[span(i, BLOCK)]),
                    ],
                    project,
                    ready,
                )
            ]
            + [block(start) for start in range(0, self.seq, BLOCK)]
            + [
                self.stage(
                    1,
                    [],
                    [
                        whole_out("query", query),
                        whole_out("key", key),
                        whole_out("value", value),
                        whole_out("attended", attended),
                        whole_out("log_total", log_total),
                    ],
                    lambda i, s: None,
                )
            ]
        )


class HeadsBack(Staged):
    def __init__(
        self, grads, query, key, value, attended, log_total, starts, turns, kvb, normed, latent, scale
    ):
        super().__init__()
        low, wide = jnp.bfloat16, jnp.float32
        seq = query.shape[0]
        self.seq, self.scale, self.n, self.columns = seq, scale, seq // 128, RANK + 128
        for a in (grads, query, key, value, attended, log_total, starts, turns, kvb, normed, latent):
            self.take(a)
        self.give((self.n, 128, 256), low)
        self.give((seq, self.columns), low)
        self.give((D, 256), low)
        self.give((RANK, KV), low)
        self.held = {
            "grad": self.hold((seq, VDIM), low),
            "query": self.hold((seq, 256), low),
            "key": self.hold((seq, 256), low),
            "value": self.hold((seq, VDIM), low),
            "attended": self.hold((seq, VDIM), wide),
            "log_total": self.hold((seq, 128), wide),
            "starts": self.hold(starts.shape, jnp.int32),
            "turns": self.hold((seq, 256), wide),
            "kvb": self.hold(kvb.shape, low),
            "normed": self.hold((2, BLOCK, D), low),
            "latent": self.hold((2, BLOCK, RANK), low),
            "d_query": self.hold((seq, 256), low),
            "d_key": self.hold((seq, 256), wide),
            "d_value": self.hold((seq, VDIM), wide),
            "part": self.hold((2, BLOCK, self.columns), low),
            "q_sum": self.hold((256, D), wide),
            "kvb_sum": self.hold((KV, RANK), wide),
            "q_grad": self.hold((D, 256), low),
            "kvb_grad": self.hold((RANK, KV), low),
        }

    def build(self):
        low, wide = jnp.bfloat16, jnp.float32
        r = {name: self.refs[k] for name, k in self.held.items()}
        grads, normed, latent = self.ins[0], self.ins[9], self.ins[10]
        blocks, part, q_grad, kvb_grad = self.gives
        n, scale = self.n, self.scale
        ready = [
            self.whole(k, self.held[name])
            for name, k in (
                ("query", 1),
                ("key", 2),
                ("value", 3),
                ("attended", 4),
                ("log_total", 5),
                ("starts", 6),
                ("turns", 7),
                ("kvb", 8),
            )
        ]

        def owned(there, k):
            owner, first = (k, 0) if k < n else (2 * n - 1 - k, 64)
            return there.at[owner, pl.ds(first, 64)]

        for k in range(2 * n):
            (sem,) = self.new_sems(1)
            copy = pltpu.make_async_copy(
                owned(grads, k), r["grad"].at[pl.ds(64 * k, 64)], sem.at[0]
            )
            self.first.append(copy)
            ready.append(copy.wait)

        def clear():
            r["d_key"][...] = jnp.zeros_like(r["d_key"])
            r["d_value"][...] = jnp.zeros_like(r["d_value"])
            r["q_sum"][...] = jnp.zeros_like(r["q_sum"])
            r["kvb_sum"][...] = jnp.zeros_like(r["kvb_sum"])

        def rope_back(values, rows):
            lanes = lax.broadcasted_iota(jnp.int32, values.shape, 1)
            half = ROPE // 2
            partner = jnp.where(
                lanes < half, pltpu.roll(values, 128 - half, 1), pltpu.roll(values, half, 1)
            )
            turned_ = values * r["turns"][rows, 0:128] - partner * r["turns"][rows, 128:256]
            return jnp.where(lanes < ROPE, turned_, 0.0).astype(low)

        def t_dot(left, right):
            return lax.dot_general(
                left, right, (((0,), (0,)), ((), ())), preferred_element_type=wide
            )

        def block(start):
            def body(i, slot):
                rows, reach = pl.ds(start, BLOCK), start + BLOCK
                mine, grad_rows = r["query"][rows], r["grad"][rows]
                scores = across(mine, r["key"][:reach])
                seen = visible(r["starts"], start, scores.shape)
                probs = jnp.exp(scores * scale - r["log_total"][rows, 0:1])
                probs = jnp.where(seen, probs, 0.0)
                delta = jnp.sum(
                    grad_rows.astype(wide) * r["attended"][rows], axis=-1, keepdims=True
                )
                d_probs = across(grad_rows, r["value"][:reach])
                d_scores = (probs * (d_probs - delta)).astype(low)
                d_query = wide_dot(d_scores, r["key"][:reach]) * scale
                d_query = d_query.astype(low)
                r["d_query"][rows, pl.ds(0, 128)] = d_query[:, :128]
                r["d_query"][rows, pl.ds(128, 128)] = rope_back(d_query[:, 128:].astype(wide), rows)
                r["d_key"][:reach] += t_dot(d_scores, mine)
                r["d_value"][:reach] += t_dot(probs.astype(low), grad_rows)

            def piece(k):
                return lambda i, s: (r["d_query"].at[pl.ds(64 * k, 64)], owned(blocks, k))

            first = start // 64
            return self.stage(
                1,
                [],
                [piece(first + k) for k in range(BLOCK // 64)],
                body,
                (ready + [clear]) if start == 0 else (),
            )

        def project(i, slot):
            at = span(i, BLOCK)
            rows = r["normed"][slot]
            r["q_sum"][...] += wide_dot(turned(r["d_query"][at]), rows)
            d_key = r["d_key"][at] * scale
            pair = jnp.concatenate([d_key[:, :NOPE], r["d_value"][at]], axis=1)
            high = pair.astype(low)
            rest = (pair - high.astype(wide)).astype(low)
            value = across(high, r["kvb"][...]) + across(rest, r["kvb"][...])
            r["part"][slot, :, pl.ds(0, RANK)] = value.astype(low)
            r["part"][slot, :, pl.ds(RANK, 128)] = d_key[:, NOPE:].astype(low)
            hidden = r["latent"][slot]
            r["kvb_sum"][...] += wide_dot(turned(high), hidden) + wide_dot(turned(rest), hidden)

        def finish(i, slot):
            r["q_grad"][...] = jnp.transpose(r["q_sum"][...]).astype(low)
            r["kvb_grad"][...] = jnp.transpose(r["kvb_sum"][...]).astype(low)

        return (
            [block(start) for start in range(0, self.seq, BLOCK)]
            + [
                self.stage(
                    self.seq // BLOCK,
                    [
                        lambda i, s: (normed.at[span(i, BLOCK)], r["normed"].at[s]),
                        lambda i, s: (latent.at[span(i, BLOCK)], r["latent"].at[s]),
                    ],
                    [lambda i, s: (r["part"].at[s], part.at[span(i, BLOCK)])],
                    project,
                )
            ]
            + [
                self.stage(
                    1,
                    [],
                    [lambda i, s: (r["q_grad"], q_grad), lambda i, s: (r["kvb_grad"], kvb_grad)],
                    finish,
                )
            ]
        )


def visible(starts, first, shape):
    row = first + lax.broadcasted_iota(jnp.int32, (shape[0], 128), 0)
    opening = jnp.zeros_like(row)
    for k in range(starts.shape[0]):
        start = starts[k : k + 1]
        opening = jnp.maximum(opening, jnp.where(start <= row, start, 0))
    column = lax.broadcasted_iota(jnp.int32, shape, 1)
    return (column >= opening[:, 0:1]) & (column <= row[:, 0:1])


def attend_kernel(causal, scale, query, key, value, bounds, attended, log_total):
    for start in range(0, query.shape[0], BLOCK):
        rows = pl.ds(start, BLOCK)
        reach = start + BLOCK if causal else key.shape[0]
        scores = lax.dot_general(
            query[rows], key[:reach], (((1,), (1,)), ((), ())), preferred_element_type=jnp.float32
        )
        column = lax.broadcasted_iota(jnp.int32, scores.shape, 1)
        seen = (column >= bounds[rows, 0:1]) & (column <= bounds[rows, 1:2])
        scores = jnp.where(seen, scores * scale, NEG)
        peak = jnp.max(scores, axis=-1, keepdims=True)
        shifted = jnp.exp(scores - peak)
        total = jnp.sum(shifted, axis=-1, keepdims=True)
        probs = (shifted * (1.0 / total)).astype(jnp.bfloat16)
        attended[rows] = jnp.dot(probs, value[:reach], preferred_element_type=jnp.float32)
        log_total[rows] = jnp.broadcast_to(peak + jnp.log(total), (BLOCK, 128))


def attend(query, key, value, bounds, causal, scale):
    whole = pl.BlockSpec(memory_space=pltpu.VMEM)
    return pl.pallas_call(
        functools.partial(attend_kernel, causal, scale),
        out_shape=[
            jax.ShapeDtypeStruct((query.shape[0], VDIM), jnp.float32),
            jax.ShapeDtypeStruct((query.shape[0], 128), jnp.float32),
        ],
        in_specs=[whole] * 4,
        out_specs=[whole] * 2,
        compiler_params=pltpu.CompilerParams(vmem_limit_bytes=48 << 20),
        name="attend",
    )(query, key, value, bounds)


def attend_back_kernel(
    causal, scale, query, key, value, bounds, log_total, attended, grad, d_query, d_key, d_value
):
    d_key[...] = jnp.zeros_like(d_key)
    d_value[...] = jnp.zeros_like(d_value)
    for start in range(0, query.shape[0], BLOCK):
        rows = pl.ds(start, BLOCK)
        reach = start + BLOCK if causal else key.shape[0]
        mine, grad_rows = query[rows], grad[rows]
        scores = lax.dot_general(
            mine, key[:reach], (((1,), (1,)), ((), ())), preferred_element_type=jnp.float32
        )
        column = lax.broadcasted_iota(jnp.int32, scores.shape, 1)
        seen = (column >= bounds[rows, 0:1]) & (column <= bounds[rows, 1:2])
        probs = jnp.where(seen, jnp.exp(scores * scale - log_total[rows, 0:1]), 0.0)
        delta = jnp.sum(grad_rows.astype(jnp.float32) * attended[rows], axis=-1, keepdims=True)
        d_probs = lax.dot_general(
            grad_rows, value[:reach], (((1,), (1,)), ((), ())), preferred_element_type=jnp.float32
        )
        d_scores = (probs * (d_probs - delta)).astype(jnp.bfloat16)
        d_query[rows] = (
            jnp.dot(d_scores, key[:reach], preferred_element_type=jnp.float32) * scale
        )
        d_key[:reach] += lax.dot_general(
            d_scores, mine, (((0,), (0,)), ((), ())), preferred_element_type=jnp.float32
        )
        d_value[:reach] += lax.dot_general(
            probs.astype(jnp.bfloat16),
            grad_rows,
            (((0,), (0,)), ((), ())),
            preferred_element_type=jnp.float32,
        )
    d_key[...] = d_key[...] * scale


def attend_back(query, key, value, bounds, log_total, attended, grad, causal, scale):
    whole = pl.BlockSpec(memory_space=pltpu.VMEM)
    return pl.pallas_call(
        functools.partial(attend_back_kernel, causal, scale),
        out_shape=[
            jax.ShapeDtypeStruct(query.shape, jnp.float32),
            jax.ShapeDtypeStruct(key.shape, jnp.float32),
            jax.ShapeDtypeStruct(value.shape, jnp.float32),
        ],
        in_specs=[whole] * 7,
        out_specs=[whole] * 3,
        compiler_params=pltpu.CompilerParams(vmem_limit_bytes=56 << 20),
        name="attend_back",
    )(query, key, value, bounds, log_total, attended, grad)


def doc_index(starts, positions):
    return jnp.sum((positions[:, None] >= starts[None, :]).astype(jnp.int32), axis=1) - 1


def rope_tables(positions):
    half = ROPE // 2
    frequency = THETA ** (-jnp.arange(half, dtype=jnp.float32) / half)
    angles = positions.astype(jnp.float32)[:, None] * frequency[None, :]
    return (jnp.cos(angles), jnp.sin(angles))


def rotate_pairs(values, cosines, sines):
    half = values.shape[-1] // 2
    first = values[..., :half]
    second = values[..., half:]
    return jnp.concatenate(
        [first * cosines - second * sines, second * cosines + first * sines], axis=-1
    )


def rms_forward(values, gain):
    factor = lax.rsqrt(jnp.mean(values * values, axis=-1, keepdims=True) + EPS)
    normal = values * factor
    return (normal * gain, normal, factor)


def rms_backward(grad_out, normal, factor, gain):
    scaled = grad_out * gain
    grad_in = factor * (scaled - normal * jnp.mean(scaled * normal, axis=-1, keepdims=True))
    return (grad_in, jnp.sum(grad_out * normal, axis=0))


def silu_parts(values):
    sigmoid = jax.nn.sigmoid(values)
    return (values * sigmoid, sigmoid * (1.0 + values * (1.0 - sigmoid)))


def dot(left, right):
    return jnp.dot(left, right, preferred_element_type=jnp.float32)


def dot_t(left, right):
    return lax.dot_general(left, right, (((1,), (1,)), ((), ())), preferred_element_type=jnp.float32)


def t_dot(left, right):
    return lax.dot_general(left, right, (((0,), (0,)), ((), ())), preferred_element_type=jnp.float32)


def two_parts(values):
    high = lax.reduce_precision(values, 8, 7)
    return high.astype(jnp.bfloat16), (values - high).astype(jnp.bfloat16)


def padded(values, columns):
    short = -values.shape[-1] % columns
    if not short:
        return values
    return jnp.pad(values, [(0, 0)] * (values.ndim - 1) + [(0, short)])


def shards(
    tokens,
    cotangent,
    doc_starts,
    routes,
    attn_gain,
    q_weight,
    kva_weight,
    kv_gain,
    kvb_weight,
    o_weight,
    ffn_gain,
    router_weight,
    shared_gate,
    shared_up,
    shared_down,
    expert_gate,
    expert_up,
    expert_down,
):
    low = jnp.bfloat16
    wide = jnp.float32
    n, cores = lax.axis_size("ctx"), lax.axis_size("fsdp")
    here = lax.axis_index("ctx")
    t = tokens.shape[1]
    half = t // 2
    seq = n * t
    ws = q_weight.shape[0]
    kr = kvb_weight.shape[0]
    copies = n // HEADS
    shared = shared_gate.shape[1]
    w = shared // n
    picks_count = routes.shape[2]
    capacity = 10 * t * picks_count // (7 * n)
    slots_count = -(-capacity // 8) * 8
    scale = HEAD ** (-0.5)
    starts = doc_starts[0]

    def run(name, number, ops, arrays, work=None):
        for op in ops:
            op.setup(n, cores)
        if work is None:
            return communicate(name, number, n, cores, ops, arrays)
        if vmem_bytes([s for op in ops for s in op.scratch] + work.scratch) < 54 << 20:
            return communicate(name, number, n, cores, ops, arrays, work, work.arrays)
        return list(communicate(name, number, n, cores, ops, arrays)) + list(
            communicate(name + "_work", None, n, cores, [], [], work, work.arrays)
        )

    def by_position(owner, start):
        if start < half:
            return pl.multiple_of(owner * half + start, 16)
        return pl.multiple_of((2 * n - 1 - owner) * half + start - half, 16)

    def by_row(rows):
        return lambda owner, start: pl.multiple_of(owner * rows + start, 16)

    def to_owners(values):
        columns = values.shape[-1]
        pair = values.reshape(2, n, half, columns)
        return jnp.concatenate([pair[0], pair[1][::-1]], axis=1)

    def to_positions(values):
        columns = values.shape[-1]
        return jnp.concatenate(
            [
                values[:, :half].reshape(n * half, columns),
                values[::-1, half:].reshape(n * half, columns),
            ]
        )

    small = jnp.concatenate(
        [
            kva_weight,
            router_weight,
            attn_gain[:, None],
            ffn_gain[:, None],
            jnp.pad(kv_gain, (0, ws - kr))[:, None],
        ],
        axis=1,
    ).astype(low)
    small = padded(small, 128)
    small_columns = small.shape[1]
    first = RANK + ROPE
    head_part = jnp.concatenate(
        [
            q_weight.astype(low).reshape(ws, HEADS, HEAD).transpose(1, 0, 2),
            kvb_weight.astype(low)
            .reshape(kr, HEADS, KV)
            .transpose(1, 0, 2)
            .reshape(HEADS, ws, kr * KV // ws),
        ],
        axis=-1,
    )
    if copies > 1:
        head_part = jnp.repeat(head_part, copies, axis=0)
    head_columns = head_part.shape[-1]
    shared_part = padded(
        jnp.concatenate(
            [
                v.astype(low).reshape(ws, n, w)
                for v in (shared_gate, shared_up, jnp.transpose(shared_down))
            ],
            axis=-1,
        ).transpose(1, 0, 2),
        128,
    )
    shared_columns = shared_part.shape[-1]

    pick_rows = -(-picks_count // 16) * 16
    pick_part = jnp.pad(jnp.transpose(routes[0]), ((0, pick_rows - picks_count), (0, 0))).astype(low)
    inputs_all, head_all, small, pick_blocks, *expert_parts = run(
        "gather_tokens",
        0,
        [
            Gather(t, D, low, by_position, light=True),
            Exchange(ws, head_columns, low, True),
            Gather(ws, small_columns, low, by_row(ws), True, light=True),
            Gather(pick_rows, t, low, by_row(pick_rows)),
        ],
        [tokens[0], head_part, small, pick_part],
        Cast([expert_gate[0], expert_up[0], expert_down[0]]),
    )
    kva_full = small[:, :first]
    router_full = small[:, first : first + n]
    gain_one = small[:, first + n].astype(wide)
    gain_two = small[:, first + n + 1].astype(wide)
    gain_latent = small[:, first + n + 2].reshape(n * cores, ws)[:, :kr].reshape(-1).astype(wide)
    picks_all = pick_blocks.reshape(n, pick_rows, t)[:, :picks_count].astype(jnp.int32)

    grad_low = cotangent[0]
    grad = grad_low.astype(wide)
    experts = (
        lax.all_gather(expert_parts[0], "fsdp", axis=0, tiled=True),
        lax.all_gather(expert_parts[1], "fsdp", axis=0, tiled=True),
        lax.all_gather(expert_parts[2], "fsdp", axis=1, tiled=True),
    )

    head_all = head_all.reshape(D, head_columns)
    q_head = head_all[:, :HEAD]
    kvb_head = head_all[:, HEAD:].reshape(RANK, KV)

    transfers = [
        Exchange(ws, shared_columns, low, True),
        Gather(ws, D, low, by_row(ws), True, light=True),
    ]
    carried = [shared_part, jnp.transpose(o_weight).astype(low)]
    positions = jnp.arange(seq, dtype=jnp.int32)
    cosines, sines = rope_tables(positions)
    lanes = ((0, 0), (0, 128 - ROPE))
    turns = jnp.concatenate(
        [
            jnp.pad(jnp.concatenate([cosines, cosines], axis=1), lanes),
            jnp.pad(jnp.concatenate([-sines, sines], axis=1), lanes),
        ],
        axis=1,
    )
    starts_rows = jnp.broadcast_to(starts[:, None], (starts.shape[0], 128))

    def eight(values):
        return jnp.broadcast_to(values[None], (8, values.shape[0]))

    def heads_apart():
        normed_all = rms_forward(inputs_all.astype(wide), gain_one)[0].astype(low)
        queries, latent_all, keys, values = project(normed_all)
        attended, log_total = attend(queries_here(queries), keys, values, bounds, False, scale)
        return (normed_all, latent_all, queries_here(queries), keys, values, attended, log_total)

    def project(normed_all):
        query_raw = dot(normed_all, q_head)
        blank = jnp.zeros((seq, 2 * NOPE - HEAD), low)
        queries = jnp.concatenate(
            [
                query_raw[:, :NOPE].astype(low),
                rotate_pairs(query_raw[:, NOPE:], cosines, sines).astype(low),
                blank,
            ],
            axis=-1,
        )
        compressed = dot(normed_all, kva_full)
        latent_all = rms_forward(compressed[:, :RANK], gain_latent)[0].astype(low)
        rope_all = rotate_pairs(compressed[:, RANK:], cosines, sines).astype(low)
        kv_head = dot(latent_all, kvb_head).astype(low)
        keys = jnp.concatenate([kv_head[:, :NOPE], rope_all, blank], axis=-1)
        values = kv_head[:, NOPE:]
        return queries, latent_all, keys, values

    opening = jnp.max(jnp.where(starts[None, :] <= positions[:, None], starts[None, :], 0), axis=1)

    def queries_here(rows):
        if copies == 1:
            return rows
        if rows.ndim == 1:
            return queries_here(rows[:, None])[:, 0]
        blocks = to_owners(rows).reshape(n // copies, copies, t, rows.shape[-1])
        return lax.dynamic_index_in_dim(blocks, here % copies, 1, False).reshape(-1, rows.shape[-1])

    def queries_back(rows):
        if copies == 1:
            return to_owners(rows)
        blocks = rows.reshape(n // copies, 1, t, rows.shape[-1])
        mine = (jnp.arange(copies) == here % copies)[None, :, None, None]
        return jnp.where(mine, blocks, jnp.zeros((), rows.dtype)).reshape(n, t, rows.shape[-1])

    def of_heads(blocks):
        columns = blocks.shape[-1]
        if copies > 1:
            blocks = blocks.reshape(HEADS, copies, t, columns)
            blocks = jnp.sum(blocks.astype(wide), axis=1).astype(blocks.dtype)
        return blocks.transpose(1, 0, 2).reshape(t, HEADS * columns)

    query_cos, query_sin = queries_here(cosines), queries_here(sines)
    bounds = queries_here(jnp.pad(jnp.stack([opening, positions], axis=1), ((0, 0), (0, 126))))
    if copies == 1:
        (
            shared_all,
            out_proj,
            normed_all,
            latent_all,
            queries,
            keys,
            values,
            attended,
            log_total,
            blocks,
        ) = run(
            "heads",
            1,
            transfers,
            carried,
            Heads(
                inputs_all,
                eight(gain_one),
                head_all,
                small,
                kvb_head,
                eight(gain_latent),
                turns,
                starts_rows,
                scale,
            ),
        )
    else:
        shared_all, out_proj = run("heads", 1, transfers, carried)
        normed_all, latent_all, queries, keys, values, attended, log_total = heads_apart()
        blocks = queries_back(attended.astype(low))
    (attn_blocks,) = run("attended", 9, [Exchange(t, VDIM, low)], [blocks])
    shared_all = shared_all.reshape(D, shared_columns)
    gate_cols, up_cols, down_rows = (shared_all[:, i * w : (i + 1) * w] for i in range(3))
    attn_values = of_heads(attn_blocks)

    inputs = tokens[0].astype(wide)
    normed_one, normal_one, factor_one = rms_forward(inputs, gain_one)
    normed_low = normed_one.astype(low)
    resid = inputs + dot_t(attn_values, out_proj)
    normed_two, normal_two, factor_two = rms_forward(resid, gain_two)
    ffn_in = normed_two.astype(low)

    (ffn_all,) = run("gather_ffn", 2, [Gather(t, D, low, by_row(t))], [ffn_in])

    chosen = jnp.any(
        picks_all[:, :, :, None] == jnp.arange(n, dtype=jnp.int32)[None, None, None, :], axis=1
    ).reshape(seq, n)
    taken = lax.dynamic_index_in_dim(chosen, here, 1, False).reshape(n, t)
    slots = jnp.where(taken, jnp.cumsum(taken.astype(jnp.int32), axis=1) - 1, -1)
    slots = slots + jnp.where(taken, slots_count * (jnp.arange(n, dtype=jnp.int32) % 2)[:, None], 0)
    slots = slots.astype(wide)
    slot_column = jnp.broadcast_to(slots.reshape(seq, 1), (seq, 128))
    slot_row = Slots(slots.reshape(n // 2, 1, 2 * t), 2 * slots_count)
    lane = first - RANK
    marks = jnp.pad(chosen.astype(low), ((0, 0), (lane, 128 - lane - n)))
    shared_rows = -(-w // 128) * 128

    def wider(values):
        return jnp.pad(values, ((0, 0), (0, shared_rows - w)))

    shared_in = jnp.concatenate([wider(gate_cols), wider(up_cols)], axis=1)
    shared_out = wider(down_rows)
    (
        grad_all,
        query_proj,
        pre,
        hidden_t,
        expert_result,
        arrived_t,
        shared_pre,
        shared_t,
        out_part,
        gates_all,
        row_gate,
    ) = run(
        "gather_grad",
        6,
        [Gather(t, D, low, by_row(t)), Gather(ws, HEADS * HEAD, low, by_row(ws), True)],
        [grad_low, q_weight.astype(low)],
        ExpertForward(
            *experts,
            ffn_all,
            shared_in,
            shared_out,
            small[:, RANK : RANK + 128],
            marks,
            slot_column,
            slot_row,
            lane,
        ),
    )
    routed, pick_grad, pre_gate_grad, pre_up_grad, shared_grad_t, gate_grads, ffn_part = run(
        "reduce_out",
        7,
        [Reduce(t, D, by_row(t))],
        [out_part],
        ExpertBackward(
            *experts,
            grad_all,
            expert_result,
            row_gate,
            pre,
            shared_pre,
            shared_in,
            shared_out,
            slot_column,
            slot_row,
        ),
    )
    output = (resid + routed).astype(low)

    results = run(
        "reduce_ffn",
        3,
        [Reduce(t, D, by_row(t)), Exchange(8, t, wide)],
        [ffn_part, gate_grads],
        Products(
            [
                shared_grad_t,
                ffn_all,
                hidden_t,
                pick_grad,
                arrived_t,
                pre_gate_grad,
                pre_up_grad,
                shared_t,
                grad_all,
            ],
            [(0, 1, 1, 512), (2, 3, 1, 256), (4, 5, 0, 256), (4, 6, 0, 256), (7, 8, 1, 512)],
            [(1, 8)],
        ),
    )
    ffn_in_grad, gate_blocks, shared_in_grad, out_w_grad, in_gate_grad, in_up_grad, shared_out_grad = (
        results
    )
    column = jnp.arange(shared_columns, dtype=jnp.int32)[None, :]
    wanted = jnp.arange(3 * shared_rows, dtype=jnp.int32)[:, None]
    wanted = jnp.where(wanted % shared_rows < w, wanted // shared_rows * w + wanted % shared_rows, -1)
    placed = (column == wanted).astype(low)
    shared_grads = (
        t_dot(shared_in_grad, placed[: 2 * shared_rows])
        + t_dot(shared_out_grad, placed[2 * shared_rows :])
    )
    shared_grads = shared_grads.astype(low).reshape(n, cores, ws, shared_columns)

    gates = lax.optimization_barrier(lax.dynamic_slice_in_dim(gates_all, here * t, t, 0))
    gates = gates[:, lane : lane + n]
    gate_grad = jnp.transpose(gate_blocks[:, 0, :])
    mixed = jnp.sum(gates * gate_grad, axis=-1, keepdims=True)
    logit_grad = (gates * (gate_grad - mixed)).astype(low)
    ffn_in_grad = ffn_in_grad + dot_t(logit_grad, router_full)
    resid_part, gain_two_grad = rms_backward(ffn_in_grad, normal_two, factor_two, gain_two)
    resid_grad = grad + resid_part
    attn_grad_low = resid_grad.astype(low)
    grad_attended = dot(attn_grad_low, out_proj).astype(low)
    grad_blocks = grad_attended.reshape(t, HEADS, VDIM).transpose(1, 0, 2)
    if copies > 1:
        grad_blocks = jnp.repeat(grad_blocks, copies, axis=0)
    (grad_att_blocks,) = run("grad_attended", 4, [Exchange(t, VDIM, low)], [grad_blocks])
    out_proj_grad = t_dot(attn_grad_low, attn_values).astype(low).reshape(n, cores, ws, D)

    expert_grads = [(in_gate_grad, 0), (in_up_grad, 0), (out_w_grad, 1)]
    transfers = [
        Exchange(ws, shared_columns, low, fold=True),
        Reduce(ws, D, by_row(ws), True, light=True),
    ] + [Halves(g.shape, low, axis) for g, axis in expert_grads]
    carried = [shared_grads, out_proj_grad] + [g for g, axis in expert_grads]
    if copies == 1:
        (
            shared_blocks,
            out_proj_sum,
            *expert_halves,
            query_blocks,
            latent_part,
            query_proj_grad,
            kvb_grad,
        ) = run(
            "heads_back",
            10,
            transfers,
            carried,
            HeadsBack(
                grad_att_blocks,
                queries,
                keys,
                values,
                attended,
                log_total,
                starts_rows,
                turns,
                kvb_head,
                normed_all,
                latent_all,
                scale,
            ),
        )
    else:
        shared_blocks, out_proj_sum, *expert_halves = run("heads_back", 10, transfers, carried)
        grad_att = queries_here(to_positions(grad_att_blocks))
        query_grad, key_grad, value_grad = attend_back(
            queries, keys, values, bounds, log_total, attended, grad_att, False, scale
        )
        query_grad = query_grad.astype(low).astype(wide)
        raw_grad = jnp.concatenate(
            [
                query_grad[:, :NOPE],
                rotate_pairs(query_grad[:, NOPE:HEAD], query_cos, -query_sin),
                jnp.zeros((query_grad.shape[0], 2 * NOPE - HEAD), wide),
            ],
            axis=-1,
        ).astype(low)
        kv_grad = jnp.concatenate([key_grad[:, :NOPE], value_grad], axis=-1)
        kv_high, kv_rest = two_parts(kv_grad)
        latent_part = dot_t(kv_high, kvb_head) + dot_t(kv_rest, kvb_head)
        latent_part = padded(
            jnp.concatenate([latent_part, key_grad[:, NOPE:HEAD]], axis=1).astype(low), 128
        )
        query_blocks = queries_back(raw_grad)
        kvb_grad = (t_dot(latent_all, kv_high) + t_dot(latent_all, kv_rest)).astype(low)
        query_proj_grad = t_dot(queries_here(normed_all), raw_grad).astype(low)
    kvb_rows = -(-kr // 16) * 16
    kvb_grad = jnp.pad(
        kvb_grad.reshape(n, cores, kr, KV), ((0, 0), (0, 0), (0, kvb_rows - kr), (0, 0))
    )
    core = lax.axis_index("fsdp")
    for k, (whole, axis) in enumerate(expert_grads):
        size = whole.shape[axis] // cores
        mine = lax.dynamic_slice_in_dim(whole, core * size, size, axis).astype(wide)
        expert_grads[k] = mine + jnp.sum(expert_halves[k].astype(wide), axis=0)
    query_blocks, latent_sum, query_grad_blocks, kvb_blocks = run(
        "reduce_latent",
        5,
        [
            Exchange(t, 2 * NOPE, low),
            Reduce(t, latent_part.shape[1], by_position, light=True),
            Exchange(ws, 2 * NOPE, low, fold=True),
            Exchange(kvb_rows, KV, low, fold=True),
        ],
        [query_blocks, latent_part, query_proj_grad.reshape(n, cores, ws, 2 * NOPE), kvb_grad],
    )

    compressed_here = dot(normed_low, kva_full)
    unused, latent_normal, latent_factor = rms_forward(compressed_here[:, :RANK], gain_latent)
    my_rows = jnp.arange(t, dtype=jnp.int32)
    my_positions = jnp.where(
        my_rows < half, here * half + my_rows, (2 * n - 1 - here) * half + my_rows - half
    )
    my_cosines, my_sines = rope_tables(my_positions)
    comp_latent_grad, gain_latent_grad = rms_backward(
        latent_sum[:, :RANK], latent_normal, latent_factor, gain_latent
    )
    rope_sum = latent_sum[:, RANK : RANK + ROPE].astype(low).astype(wide)
    rope_back = rotate_pairs(rope_sum, my_cosines, -my_sines)
    comp_grad = jnp.concatenate([comp_latent_grad, rope_back], axis=-1).astype(low)
    raw_here = of_heads(query_blocks[:, :, :HEAD])
    normed_grad = dot_t(raw_here, query_proj) + dot_t(comp_grad, kva_full)
    input_part, gain_one_grad = rms_backward(normed_grad, normal_one, factor_one, gain_one)
    input_grad = (resid_grad + input_part).astype(low)

    spare = small_columns - first
    small_grads = t_dot(normed_low, jnp.pad(comp_grad, ((0, 0), (0, spare)))) + t_dot(
        ffn_in, jnp.pad(logit_grad, ((0, 0), (first, spare - n)))
    )
    gain_grads = jnp.stack(
        [
            gain_one_grad.reshape(n, cores, ws),
            gain_two_grad.reshape(n, cores, ws),
            jnp.pad(gain_latent_grad.reshape(n, cores, kr), ((0, 0), (0, 0), (0, ws - kr))),
        ],
        axis=2,
    ).astype(low)
    gain_grads = jnp.pad(gain_grads, ((0, 0), (0, 0), (0, 13), (0, 128 - ws)))
    small_sum, gain_sum = run(
        "weight_grads",
        8,
        [Reduce(ws, small_columns, by_row(ws), True), Reduce(16, 128, by_row(16), True)],
        [small_grads.astype(low).reshape(n, cores, ws, small_columns), gain_grads],
    )

    def to_shards(blocks, rows, columns):
        values = blocks[:, :rows, :columns].astype(wide).reshape(HEADS, copies, rows, columns)
        return jnp.sum(values, axis=1).transpose(1, 0, 2).reshape(rows, HEADS * columns)

    q_weight_grad = to_shards(query_grad_blocks, ws, HEAD)
    kvb_weight_grad = to_shards(kvb_blocks, kr, KV)
    shared_sums = [
        shared_blocks[:, :, i * w : (i + 1) * w]
        .transpose(1, 0, 2)
        .reshape(ws, shared)
        .astype(wide)
        for i in range(3)
    ]
    return (
        output[None],
        input_grad[None],
        gain_sum[0, :ws],
        q_weight_grad,
        small_sum[:, :first],
        gain_sum[2, :kr],
        kvb_weight_grad,
        jnp.transpose(out_proj_sum),
        gain_sum[1, :ws],
        small_sum[:, first : first + n],
        shared_sums[0],
        shared_sums[1],
        jnp.transpose(shared_sums[2]),
        expert_grads[0][None],
        expert_grads[1][None],
        expert_grads[2][None],
    )


def solution(mesh):
    return jax.shard_map(
        shards,
        mesh=mesh,
        in_specs=(
            P("fsdp", "ctx", None),
            P("fsdp", "ctx", None),
            P("fsdp", None),
            P("fsdp", "ctx", None),
            P(("ctx", "fsdp")),
            P(("ctx", "fsdp"), None),
            P(("ctx", "fsdp"), None),
            P(("ctx", "fsdp")),
            P(("ctx", "fsdp"), None),
            P(None, ("ctx", "fsdp")),
            P(("ctx", "fsdp")),
            P(("ctx", "fsdp"), None),
            P(("ctx", "fsdp"), None),
            P(("ctx", "fsdp"), None),
            P(None, ("ctx", "fsdp")),
            P("ctx", "fsdp", None),
            P("ctx", "fsdp", None),
            P("ctx", None, "fsdp"),
        ),
        out_specs=(
            P("fsdp", "ctx", None),
            P("fsdp", "ctx", None),
            P(("ctx", "fsdp")),
            P(("ctx", "fsdp"), None),
            P(("ctx", "fsdp"), None),
            P(("ctx", "fsdp")),
            P(("ctx", "fsdp"), None),
            P(None, ("ctx", "fsdp")),
            P(("ctx", "fsdp")),
            P(("ctx", "fsdp"), None),
            P(("ctx", "fsdp"), None),
            P(("ctx", "fsdp"), None),
            P(None, ("ctx", "fsdp")),
            P("ctx", "fsdp", None),
            P("ctx", "fsdp", None),
            P("ctx", None, "fsdp"),
        ),
        check_vma=False,
    )
```

```python
import functools

import jax
import jax.numpy as jnp
import numpy as np
from jax import lax
from jax.experimental import pallas as pl
from jax.experimental.pallas import tpu as pltpu
from jax.sharding import PartitionSpec as P

D = 2048
HEADS = 16
NOPE = 128
ROPE = 64
VDIM = 128
RANK = 512
HEAD = NOPE + ROPE
KV = NOPE + VDIM

EPS = 1e-06
THETA = 10000.0
NEG = -1e30
MESH = pl.DeviceIdType.MESH
BLOCK = 256

ZXY, ZYX = ("z", "x", "y"), ("z", "y", "x")
XYZ, YXZ = ("x", "y", "z"), ("y", "x", "z")


def pieces(rows, light=False):
    if rows == 128 and not light:
        return (
            (0, 32, ZXY),
            (32, 32, ZYX),
            (64, 16, ZXY),
            (80, 16, ZYX),
            (96, 16, XYZ),
            (112, 16, YXZ),
        )
    if rows == 128:
        return ((0, 32, ZXY), (32, 32, ZYX), (64, 32, ZXY), (96, 32, ZYX))
    if rows == 64 and not light:
        return ((0, 32, ZXY), (32, 16, ZYX), (48, 16, YXZ))
    if rows % 32 == 0:
        return ((0, rows // 2, ZXY), (rows // 2, rows // 2, ZYX))
    return ((0, rows, ZXY),)


def maybe(cond, fn):
    if cond is None:
        fn()
    else:
        pl.when(cond)(fn)


def both(first, second):
    if first is None:
        return second
    if second is None:
        return first
    return jnp.logical_and(first, second)


class Place:
    def __init__(self, n, cores):
        self.n, self.cores, self.lines = n, cores, n // 4
        self.c, self.f = lax.axis_index("ctx"), lax.axis_index("fsdp")
        self.z, self.y, self.x = self.split(self.c)
        z, y, x, top = self.z, self.y, self.x, self.lines - 1
        self.peers = {
            ("z", 1): (self.index(jnp.minimum(z + 1, top), y, x), z < top),
            ("z", -1): (self.index(jnp.maximum(z - 1, 0), y, x), z > 0),
            ("y", 1): (self.index(z, 1 - y, x), None),
            ("x", 1): (self.index(z, y, 1 - x), None),
        }

    @staticmethod
    def split(c):
        return c // 4, (c // 2) % 2, c % 2

    @staticmethod
    def index(z, y, x):
        return z * 4 + y * 2 + x

    def owner(self, rel):
        oz = self.z + rel["z"]
        cond = None if rel["z"] == 0 else (oz >= 0) & (oz < self.lines)
        oz = jnp.clip(oz, 0, self.lines - 1)
        oy = 1 - self.y if rel["y"] else self.y
        ox = 1 - self.x if rel["x"] else self.x
        return cond, self.index(oz, oy, ox)


SLOT = {("z", 1): 0, ("z", -1): 1, ("y", 1): 2, ("x", 1): 3}


def offsets(n, order):
    lines = n // 4
    found = []
    for a in range(1 - lines, lines):
        for y in range(2):
            for x in range(2):
                rel = {"z": a, "y": y, "x": x}
                used = [k for k, d in enumerate(order) if rel[d] != 0]
                found.append((rel, used[-1] if used else -1, abs(a) + y + x))
    return found


class Gather:
    peers = "near"

    def __init__(self, rows, cols, dtype, place, spread=False, light=False):
        self.rows, self.cols, self.dtype, self.place = rows, cols, dtype, place
        self.spread, self.light = spread, light

    def setup(self, n, cores):
        self.n, self.cores, self.parts = n, cores, pieces(self.rows, self.light)
        k = len(self.parts)
        count = n * cores if self.spread else n
        self.out = jax.ShapeDtypeStruct((count * self.rows, self.cols), self.dtype)
        self.out_spec = pl.BlockSpec(memory_space=pl.ANY)
        self.scratch = [
            pltpu.SemaphoreType.DMA((k, 4, n)),
            pltpu.SemaphoreType.DMA((k, n)),
            pltpu.SemaphoreType.DMA((k,)),
        ]
        if self.spread:
            self.scratch += [pltpu.SemaphoreType.DMA((k, n, cores))] * 2

    def events(self, at, src, out, send_sem, recv_sem, own_sem, *pair_sems):
        n, cores, parts = self.n, self.cores, self.parts
        sent, kept, events = [], [], []

        def rows_of(i, owner, core=None):
            if self.spread:
                owner = owner * cores + (at.f if core is None else core)
            return pl.ds(self.place(owner, parts[i][0]), parts[i][1])

        def pair_copy(i, rel, k):
            cond, owner = at.owner(rel)
            core = lax.rem(at.f + k, cores)
            there = out.at[rows_of(i, owner)]
            here = src.at[pl.ds(parts[i][0], parts[i][1])]
            return cond, pltpu.make_async_remote_copy(
                src_ref=there if any(rel.values()) else here,
                dst_ref=there,
                send_sem=pair_sems[0].at[i, owner, core],
                recv_sem=pair_sems[1].at[i, owner, at.f],
                device_id={"fsdp": core},
                device_id_type=MESH,
            )

        def go(make):
            cond, copy = make()
            maybe(cond, copy.start)
            sent.append(make)

        def share(i, rel):
            for k in range(1, cores):
                go(functools.partial(pair_copy, i, rel, k))

        def link_copy(i, rel, key):
            cond, owner = at.owner(rel)
            peer, ok = at.peers[key]
            there = out.at[rows_of(i, owner)]
            here = src.at[pl.ds(parts[i][0], parts[i][1])]
            return both(cond, ok), pltpu.make_async_remote_copy(
                src_ref=there if any(rel.values()) else here,
                dst_ref=there,
                send_sem=send_sem.at[i, SLOT[key], owner],
                recv_sem=recv_sem.at[i, owner],
                device_id={"ctx": peer},
                device_id_type=MESH,
            )

        def onward(i, rel, last):
            order = parts[i][2]
            keys = []
            if last >= 0 and order[last] == "z":
                keys.append(("z", 1 if rel["z"] < 0 else -1))
            for d in order[last + 1 :]:
                keys += [("z", 1), ("z", -1)] if d == "z" else [(d, 1)]
            for key in keys:
                go(functools.partial(link_copy, i, rel, key))

        def begin():
            still = {"z": 0, "y": 0, "x": 0}
            for i in range(len(parts)):
                onward(i, still, -1)
            for i, (start, rows, order) in enumerate(parts):
                copy = pltpu.make_async_copy(
                    src.at[pl.ds(start, rows)], out.at[rows_of(i, at.c)], own_sem.at[i]
                )
                copy.start()
                kept.append(copy)
                if self.spread:
                    share(i, still)

        def arrive(i, rel, last):
            cond, owner = at.owner(rel)
            there = out.at[rows_of(i, owner)]
            maybe(
                cond,
                lambda: pltpu.make_async_copy(there, there, recv_sem.at[i, owner]).wait(),
            )
            onward(i, rel, last)
            if self.spread:
                share(i, rel)

        def end():
            if self.spread:
                for i in range(len(parts)):
                    for owner in range(n):
                        for k in range(1, cores):
                            core = lax.rem(at.f + k, cores)
                            there = out.at[rows_of(i, owner, core)]
                            pltpu.make_async_copy(
                                there, there, pair_sems[1].at[i, owner, core]
                            ).wait()
            for make in sent:
                cond, copy = make()
                maybe(cond, copy.wait_send)
            for copy in kept:
                copy.wait()

        events.append((-1, begin))
        for i, part in enumerate(parts):
            for rel, last, hops in offsets(n, part[2]):
                if last >= 0:
                    events.append((hops, functools.partial(arrive, i, rel, last)))
        events.append((1000, end))
        return events


class Fold:
    def __init__(self, n, cores, rows, cols, dtype):
        self.n, self.cores, self.rows, self.cols, self.dtype = n, cores, rows, cols, dtype
        self.scratch = [
            pltpu.VMEM((cores - 1, n, rows, cols), dtype),
            pltpu.VMEM((n, rows, cols), dtype),
            pltpu.SemaphoreType.DMA((cores,)),
            pltpu.SemaphoreType.DMA((cores,)),
            pltpu.SemaphoreType.DMA((1,)),
        ]

    def events(self, at, src, held, total, send_sem, recv_sem, own_sem):
        cores, sent = self.cores, []

        def begin():
            for k in range(1, cores):
                core = lax.rem(at.f + k, cores)
                copy = pltpu.make_async_remote_copy(
                    src_ref=src.at[:, core],
                    dst_ref=held.at[cores - 1 - k],
                    send_sem=send_sem.at[k],
                    recv_sem=recv_sem.at[cores - k],
                    device_id={"fsdp": core},
                    device_id_type=MESH,
                )
                copy.start()
                sent.append(copy)
            pltpu.make_async_copy(src.at[:, at.f], total, own_sem.at[0]).start()

        def work():
            pltpu.make_async_copy(src.at[:, at.f], total, own_sem.at[0]).wait()
            for k in range(1, cores):
                pltpu.make_async_copy(held.at[k - 1], held.at[k - 1], recv_sem.at[k]).wait()
            tiles = self.rows // 16

            def step(j, carry):
                owner, to = j // tiles, pl.ds(pl.multiple_of(lax.rem(j, tiles) * 16, 16), 16)
                value = total[owner, to].astype(jnp.float32)
                for k in range(cores - 1):
                    value = value + held[k, owner, to].astype(jnp.float32)
                total[owner, to] = value.astype(self.dtype)
                return carry

            lax.fori_loop(0, self.n * tiles, step, 0)
            for copy in sent:
                copy.wait_send()

        return [(-3, begin), (-2, work)]


class Halves:
    peers, spread = "near", True

    def __init__(self, shape, dtype, axis):
        self.shape, self.dtype, self.axis = shape, dtype, axis

    def setup(self, n, cores):
        self.cores, self.part = cores, list(self.shape)
        self.part[self.axis] //= cores
        self.out = jax.ShapeDtypeStruct((cores - 1,) + tuple(self.part), self.dtype)
        self.out_spec = pl.BlockSpec(memory_space=pl.ANY)
        self.scratch = [pltpu.SemaphoreType.DMA((2, cores))]

    def events(self, at, src, out, sems):
        cores, size = self.cores, self.part[self.axis]

        def copy(k):
            other = lax.rem(at.f + k, cores)
            place = pl.ds(pl.multiple_of(other * size, 128), size)
            return pltpu.make_async_remote_copy(
                src_ref=src.at[place] if self.axis == 0 else src.at[:, place],
                dst_ref=out.at[cores - 1 - k],
                send_sem=sems.at[0, k],
                recv_sem=sems.at[1, cores - k],
                device_id={"fsdp": other},
                device_id_type=MESH,
            )

        def begin():
            for k in range(1, cores):
                copy(k).start()

        def end():
            for k in range(1, cores):
                there = out.at[k - 1]
                pltpu.make_async_copy(there, there, sems.at[1, k]).wait()
                copy(k).wait_send()

        return [(-1, begin), (1000, end)]


class Reduce:
    peers = "near"

    def __init__(self, rows, cols, place, fold=False, light=False):
        self.rows, self.cols, self.place, self.light = rows, cols, place, light
        self.dtype = jnp.bfloat16
        self.spread = fold

    def setup(self, n, cores):
        self.n, self.parts = n, pieces(self.rows, self.light)
        lines, k = n // 4, len(self.parts)
        self.size = {"z": lines, "y": 2, "x": 2}
        self.table, total = [], 0
        for start, rows, order in self.parts:
            entry, ahead = {}, 1
            for d in order:
                entry[d] = total
                total += rows * ahead * (lines + 1 if d == "z" else 1)
                ahead *= self.size[d]
            self.table.append(entry)
        self.out = jax.ShapeDtypeStruct((self.rows, self.cols), jnp.float32)
        self.out_spec = pl.BlockSpec(memory_space=pltpu.VMEM)
        self.scratch = [
            pltpu.VMEM((total, self.cols), self.dtype),
            pltpu.SemaphoreType.DMA((k, 4, n)),
            pltpu.SemaphoreType.DMA((k, 4, n)),
        ]
        if self.spread:
            self.fold = Fold(n, cores, self.rows, self.cols, self.dtype)
            self.scratch += self.fold.scratch
        else:
            self.own_first, own_total = [], 0
            for start, rows, order in self.parts:
                self.own_first.append(own_total)
                own_total += rows * (n if order[2] == "z" else n // 2)
            self.scratch += [
                pltpu.VMEM((own_total, self.cols), self.dtype),
                pltpu.SemaphoreType.DMA((k, n)),
            ]

    def own_rows(self, i, owner, first, count):
        start, rows, order = self.parts[i]
        if self.spread:
            return owner, pl.ds(pl.multiple_of(start + first, 16), count)
        oz, oy, ox = Place.split(owner)
        number = {"z": owner, "y": oz * 2 + ox, "x": oz * 2 + oy}[order[2]]
        at = self.own_first[i] + number * rows + first
        return (pl.ds(pl.multiple_of(at, 16), count),)

    def held_rows(self, i, d, owner, line, up):
        start, rows, order = self.parts[i]
        oz, oy, ox = Place.split(owner)
        have = {"z": oz, "y": oy, "x": ox}
        number = 0
        for e in order[: order.index(d)]:
            number = number * self.size[e] + have[e]
        if d == "z":
            lines = self.size["z"]
            number = number * (lines + 1) + (oz if up else jnp.where(oz == line, lines, oz))
        return pl.ds(pl.multiple_of(self.table[i][d] + number * rows, 16), rows)

    def events(self, at, src, out, held, send_sem, recv_sem, *more):
        n, parts, lines = self.n, self.parts, self.n // 4
        sent, events = [], []
        if self.spread:
            events += self.fold.events(at, src, *more)
            own = more[1]
        else:
            own, own_sem = more

        def coming(i, rel, last):
            order = parts[i][2]
            come = []
            if last >= 0 and order[last] == "z":
                come.append(("z", 1 if rel["z"] < 0 else -1))
            for d in order[last + 1 :]:
                come += [("z", 1), ("z", -1)] if d == "z" else [(d, 1)]
            return come

        def fetch(i, owner):
            start, rows, order = parts[i]
            return pltpu.make_async_copy(
                src.at[pl.ds(self.place(owner, start), rows)],
                own.at[self.own_rows(i, owner, 0, rows)],
                own_sem.at[i, owner],
            )

        def begin(i, rel, last):
            if coming(i, rel, last):
                cond, owner = at.owner(rel)
                maybe(cond, fetch(i, owner).start)

        def tiles(rows, body):
            def step(r, carry):
                body(r * 16)
                return carry

            lax.fori_loop(0, rows // 16, step, 0)

        def tile(start, r):
            return pl.ds(pl.multiple_of(start + r, 16), 16)

        def work(i, rel, last):
            start, rows, order = parts[i]
            cond, owner = at.owner(rel)
            come = coming(i, rel, last)

            def arrived(d, way, add):
                ok = at.peers[(d, way)][1]
                got = self.held_rows(i, d, owner, at.z, way < 0)

                def take():
                    there = held.at[got]
                    pltpu.make_async_copy(there, there, recv_sem.at[i, SLOT[(d, way)], owner]).wait()
                    tiles(rows, lambda r: add(r, tile(got.start, r)))

                maybe(ok, take)

            def add_on(r, got):
                to = self.own_rows(i, owner, r, 16)
                own[to] = (own[to].astype(jnp.float32) + held[got].astype(jnp.float32)).astype(
                    self.dtype
                )

            def add_last(r, got):
                to = tile(start, r)
                out[to] = out[to] + held[got].astype(jnp.float32)

            def keep(r):
                out[tile(start, r)] = own[self.own_rows(i, owner, r, 16)].astype(jnp.float32)

            def take_all():
                if not self.spread:
                    fetch(i, owner).wait()
                if last < 0:
                    tiles(rows, keep)
                for d, way in come:
                    arrived(d, way, add_last if last < 0 else add_on)

            if come:
                maybe(cond, take_all)
            if last >= 0:
                make = functools.partial(link_copy, i, rel, last)
                cond, copy = make()
                maybe(cond, copy.start)
                sent.append(make)

        def link_copy(i, rel, last):
            start, rows, order = parts[i]
            cond, owner = at.owner(rel)
            d = order[last]
            way = 1 if d != "z" or rel["z"] > 0 else -1
            peer, ok = at.peers[(d, way)]
            there = self.held_rows(i, d, owner, at.z + (way if d == "z" else 0), way > 0)
            if coming(i, rel, last) or self.spread:
                mine = own.at[self.own_rows(i, owner, 0, rows)]
            else:
                mine = src.at[pl.ds(self.place(owner, start), rows)]
            return cond, pltpu.make_async_remote_copy(
                src_ref=mine,
                dst_ref=held.at[there],
                send_sem=send_sem.at[i, SLOT[(d, way)], owner],
                recv_sem=recv_sem.at[i, SLOT[(d, -way if d == "z" else 1)], owner],
                device_id={"ctx": peer},
                device_id_type=MESH,
            )

        def end():
            for make in sent:
                cond, copy = make()
                maybe(cond, copy.wait_send)

        for i, part in enumerate(parts):
            for rel, last, hops in offsets(n, part[2]):
                if not self.spread:
                    events.append((-1, functools.partial(begin, i, rel, last)))
                events.append((lines + 2 - hops, functools.partial(work, i, rel, last)))
        events.append((1000, end))
        return events


class Exchange:
    peers = "all"

    def __init__(self, rows, cols, dtype, spread=False, fold=False, wide_in=False, wide_out=False):
        self.rows, self.cols, self.dtype = rows, cols, dtype
        self.share, self.spread, self.folds = spread, spread or fold, fold
        self.wide_in, self.wide_out = wide_in, wide_out

    def setup(self, n, cores):
        self.n, self.cores = n, cores
        shape = (n, cores, self.rows, self.cols) if self.share else (n, self.rows, self.cols)
        if self.wide_out:
            shape = (self.rows, n * self.cols)
        self.out = jax.ShapeDtypeStruct(shape, self.dtype)
        self.out_spec = pl.BlockSpec(memory_space=pl.ANY)
        self.scratch = [
            pltpu.SemaphoreType.DMA((n,)),
            pltpu.SemaphoreType.DMA((n,)),
            pltpu.SemaphoreType.DMA((1,)),
        ]
        if self.share:
            self.scratch += [pltpu.SemaphoreType.DMA((n, cores))] * 2
        if self.folds:
            self.fold = Fold(n, cores, self.rows, self.cols, self.dtype)
            self.scratch += self.fold.scratch

    def events(self, at, src, out, send_sem, recv_sem, own_sem, *more):
        n, cores = self.n, self.cores
        sent, kept, events = [], [], []
        pair_sems = more[:2]
        if self.folds:
            events += self.fold.events(at, src, *more)
            src = more[1]

        def side(ref, owner):
            return ref.at[:, pl.ds(pl.multiple_of(owner * self.cols, 128), self.cols)]

        def source(owner):
            return side(src, owner) if self.wide_in else src.at[owner]

        def there(owner):
            if self.wide_out:
                return side(out, owner)
            return out.at[owner, at.f] if self.share else out.at[owner]

        def pair_copy(k, step):
            owner, core = lax.rem(at.c + step, n), lax.rem(at.f + k, cores)
            return pltpu.make_async_remote_copy(
                src_ref=there(owner) if step else source(owner),
                dst_ref=there(owner),
                send_sem=pair_sems[0].at[owner, core],
                recv_sem=pair_sems[1].at[owner, at.f],
                device_id={"fsdp": core},
                device_id_type=MESH,
            )

        def link_copy(k):
            peer = lax.rem(at.c + k, n)
            return pltpu.make_async_remote_copy(
                src_ref=source(peer),
                dst_ref=there(at.c),
                send_sem=send_sem.at[peer],
                recv_sem=recv_sem.at[at.c],
                device_id={"ctx": peer},
                device_id_type=MESH,
            )

        def go(make):
            make().start()
            sent.append(make)

        def share(step):
            for k in range(1, cores):
                go(functools.partial(pair_copy, k, step))

        def begin():
            for k in range(1, n):
                go(functools.partial(link_copy, k))
            copy = pltpu.make_async_copy(source(at.c), there(at.c), own_sem.at[0])
            copy.start()
            kept.append(copy)
            if self.share:
                share(0)

        def arrive(k):
            owner = lax.rem(at.c + k, n)
            block = there(owner)
            pltpu.make_async_copy(block, block, recv_sem.at[owner]).wait()
            if self.share:
                share(k)

        def end():
            if self.share:
                for owner in range(n):
                    for k in range(1, cores):
                        core = lax.rem(at.f + k, cores)
                        block = out.at[owner, core]
                        pltpu.make_async_copy(block, block, pair_sems[1].at[owner, core]).wait()
            for make in sent:
                make().wait_send()
            for copy in kept:
                copy.wait()

        events.append((-1, begin))
        for k in range(1, n):
            events.append((100 + k, functools.partial(arrive, k)))
        events.append((1000, end))
        return events


def vmem_bytes(scratch):
    total = 0
    for s in scratch:
        if hasattr(s, "shape") and s.dtype in (jnp.bfloat16, jnp.float32, jnp.int32):
            size = s.dtype.itemsize * -(-s.shape[-1] // 128) * 128
            for k in s.shape[:-1]:
                size *= k
            total += size
    return total


def communicate(name, number, n, cores, ops, arrays, work=None, work_arrays=()):
    everyone = any(op.peers == "all" for op in ops)
    spread = any(op.spread for op in ops) or getattr(work, "spread", False)
    outs = [op.out for op in ops] + (work.outs if work else [])
    anywhere = pl.BlockSpec(memory_space=pl.ANY)

    def kernel(*refs):
        at = Place(n, cores)
        if ops:
            barrier = pltpu.get_barrier_semaphore()
        if not ops:
            pass
        elif everyone:
            for j in range(1, n):
                pl.semaphore_signal(
                    barrier, 1, device_id={"ctx": lax.rem(at.c + j, n)}, device_id_type=MESH
                )
            count = n - 1
        else:
            for peer, ok in at.peers.values():
                maybe(
                    ok,
                    lambda peer=peer: pl.semaphore_signal(
                        barrier, 1, device_id={"ctx": peer}, device_id_type=MESH
                    ),
                )
            count = 2 + (at.z > 0).astype(jnp.int32) + (at.z < at.lines - 1).astype(jnp.int32)
        if ops and spread:
            for j in range(1, cores):
                pl.semaphore_signal(
                    barrier, 1, device_id={"fsdp": lax.rem(at.f + j, cores)}, device_id_type=MESH
                )
            count = count + cores - 1
        if ops:
            pl.semaphore_wait(barrier, count)
        k, inputs = len(ops), len(ops) + len(work_arrays)
        events, first = [], inputs + len(outs)
        for j, op in enumerate(ops):
            mine = refs[first : first + len(op.scratch)]
            first += len(op.scratch)
            events += op.events(at, refs[j], refs[inputs + j], *mine)
        events = sorted(events, key=lambda e: e[0])
        if not work:
            for _, event in events:
                event()
            return
        for time, event in events:
            if time < 0:
                event()
        between = [event for time, event in events if 0 <= time < 1000]
        loops = work.loops(refs[k:inputs], refs[inputs + k : inputs + len(outs)], refs[first:])
        steps, done = sum(loop[1] for loop in loops), 0
        for before, turns, body, after in loops:
            before()

            def turn(i, carry, done=done, turns=turns, body=body):
                for j in range(turns):
                    low, high = ((done + j + d) * len(between) // steps for d in range(2))
                    if high > low:

                        @pl.when(i == j)
                        def _(low=low, high=high):
                            for event in between[low:high]:
                                event()

                body(i)
                return carry

            lax.fori_loop(0, turns, turn, 0)
            after()
            done += turns
        for time, event in events:
            if time >= 1000:
                event()

    return pl.pallas_call(
        kernel,
        out_shape=outs,
        in_specs=[anywhere] * (len(ops) + len(work_arrays)),
        out_specs=[op.out_spec for op in ops] + [anywhere] * (len(outs) - len(ops)),
        scratch_shapes=[s for op in ops for s in op.scratch] + (work.scratch if work else []),
        compiler_params=pltpu.CompilerParams(
            collective_id=number if ops else None,
            has_side_effects=bool(ops),
            vmem_limit_bytes=(60 if work else 48) << 20,
        ),
        name=name,
    )(*arrays, *work_arrays)


class Products:
    def __init__(self, arrays, jobs, shared):
        self.arrays, self.jobs, self.shared = arrays, jobs, shared
        self.outs, self.scratch = [], []
        for left, right, axis, width in jobs:
            shape = (arrays[left].shape[0], arrays[right].shape[1])
            self.outs.append(jax.ShapeDtypeStruct(shape, jnp.bfloat16))
            piece = (width, shape[1]) if axis == 0 else (shape[0], width)
            self.scratch.append(pltpu.VMEM((2,) + piece, jnp.bfloat16))
        self.scratch.append(pltpu.SemaphoreType.DMA((len(jobs), 2)))
        self.scratch.append(pltpu.SemaphoreType.DMA((len(arrays),)))
        later = [second for first, second in shared]
        self.held = [i for i in range(len(arrays)) if i not in later]
        self.scratch += [pltpu.VMEM(arrays[i].shape, arrays[i].dtype) for i in self.held]

    def loops(self, ins, outs, scratch):
        jobs = self.jobs
        stages, (out_sem, in_sem) = scratch[: len(jobs)], scratch[len(jobs) : len(jobs) + 2]
        kept = dict(zip(self.held, scratch[len(jobs) + 2 :]))
        for first, second in self.shared:
            kept[second] = kept[first]
        ready = set()
        follows = dict(self.shared)
        begun = set(self.held)

        def load(i):
            return pltpu.make_async_copy(ins[i], kept[i], in_sem.at[i])

        def make(number):
            left, right, axis, width = jobs[number]
            shape = self.outs[number].shape
            turns = shape[axis] // width
            stage = stages[number]

            def out_copy(i):
                slot = lax.rem(i, 2)
                at = pl.ds(pl.multiple_of(i * width, 128), width)
                there = outs[number].at[at] if axis == 0 else outs[number].at[:, at]
                return pltpu.make_async_copy(stage.at[slot], there, out_sem.at[number, slot])

            def before():
                if number == 0:
                    for i in self.held:
                        load(i).start()
                for i in (left, right):
                    if i not in ready:
                        load(i).wait()
                        ready.add(i)

            def body(i):
                @pl.when(i >= 2)
                def _():
                    out_copy(i - 2).wait()

                at = pl.ds(pl.multiple_of(i * width, 128), width)
                a = kept[left][at] if axis == 0 else kept[left][...]
                b = kept[right][...] if axis == 0 else kept[right][:, at]
                stage[lax.rem(i, 2)] = jnp.dot(a, b, preferred_element_type=jnp.float32).astype(
                    jnp.bfloat16
                )
                out_copy(i).start()

            def after():
                for i in range(max(0, turns - 2), turns):
                    out_copy(i).wait()
                for i in (left, right):
                    if i in follows:
                        load(follows.pop(i)).start()

            return before, turns, body, after

        return [make(number) for number in range(len(jobs))]


class Staged:
    def __init__(self):
        self.arrays, self.outs, self.scratch = [], [], []
        self.sem_rows = 0
        self.sems = self.add(pltpu.SemaphoreType.DMA((128, 2)))

    def add(self, scratch):
        self.scratch.append(scratch)
        return len(self.scratch) - 1

    def hold(self, shape, dtype):
        return self.add(pltpu.VMEM(shape, dtype))

    def take(self, array):
        self.arrays.append(array)
        return len(self.arrays) - 1

    def give(self, shape, dtype):
        self.outs.append(jax.ShapeDtypeStruct(shape, dtype))
        return len(self.outs) - 1

    def loops(self, ins, outs, scratch):
        self.ins, self.gives, self.refs = ins, outs, scratch
        self.sem_rows, self.first = 0, []
        found = self.build()
        start = found[0][0]

        def begin():
            for copy in self.first:
                copy.start()
            start()

        return [(begin,) + found[0][1:]] + found[1:]

    def new_sems(self, count):
        self.sem_rows += count
        return [self.refs[self.sems].at[self.sem_rows - count + k] for k in range(count)]

    def whole(self, number, held):
        (sem,) = self.new_sems(1)
        copy = pltpu.make_async_copy(self.ins[number], self.refs[held], sem.at[0])
        self.first.append(copy)
        return copy.wait

    def stage(self, turns, loads, stores, body, ready=(), late=False):
        load_sems, store_sems = self.new_sems(len(loads)), self.new_sems(len(stores))

        def load(k, i, slot):
            return pltpu.make_async_copy(*loads[k](i, slot), load_sems[k].at[slot])

        def store(k, i, slot):
            return pltpu.make_async_copy(*stores[k](i, slot), store_sems[k].at[slot])

        if not late:
            for k in range(len(loads)):
                self.first.append(load(k, 0, 0))

        def before():
            for wait in ready:
                wait()
            if late:
                for k in range(len(loads)):
                    load(k, 0, 0).start()

        def turn(i):
            slot = lax.rem(i, 2)
            for k in range(len(loads)):
                load(k, i, slot).wait()

            @pl.when(i + 1 < turns)
            def _():
                for k in range(len(loads)):
                    load(k, i + 1, 1 - slot).start()

            @pl.when(i >= 2)
            def _():
                for k in range(len(stores)):
                    store(k, i - 2, slot).wait()

            body(i, slot)
            for k in range(len(stores)):
                store(k, i, slot).start()

        def after():
            for i in range(max(0, turns - 2), turns):
                for k in range(len(stores)):
                    store(k, i, i % 2).wait()

        return before, turns, turn, after


def span(i, width, unit=128):
    return pl.ds(pl.multiple_of(i * width, unit), width)


class PackShared(Staged):
    def __init__(self, first, second, third, n, columns):
        super().__init__()
        low = jnp.bfloat16
        rows, total = first.shape
        self.w, self.columns, self.total, self.n = total // n, columns, total, n
        self.window = min((self.w + 254) // 128 * 128, total)
        for a in (first, second, third):
            self.take(a)
        self.give((n, rows, columns), low)
        self.held = [self.hold(a.shape, jnp.float32) for a in (first, second, third)]
        self.stage_out = self.hold((2, rows, columns), low)

    def build(self):
        low = jnp.bfloat16
        refs = [self.refs[k] for k in self.held]
        stage_out, out = self.refs[self.stage_out], self.gives[0]
        w, window = self.w, self.window
        ready = [self.whole(k, self.held[k]) for k in range(3)]

        def body(i, slot):
            start = jnp.minimum(i * w // 128 * 128, self.total - window)
            at = pl.ds(pl.multiple_of(start, 128), window)
            shape = (window, self.columns)
            source = lax.broadcasted_iota(jnp.int32, shape, 0) + (start - i * w)
            target = lax.broadcasted_iota(jnp.int32, shape, 1)

            def placed(k):
                inside = (source >= 0) & (source < w) & (target == source + k * w)
                return jnp.where(inside, 1.0, 0.0).astype(low)

            value = wide_dot(refs[0][:, at].astype(low), placed(0))
            value = value + wide_dot(refs[1][:, at].astype(low), placed(1))
            value = value + lax.dot_general(
                refs[2][at].astype(low),
                placed(2),
                (((0,), (0,)), ((), ())),
                preferred_element_type=jnp.float32,
            )
            stage_out[slot] = value.astype(low)

        return [
            self.stage(
                self.n,
                [],
                [lambda i, s: (stage_out.at[s], out.at[i])],
                body,
                ready,
            )
        ]


class CastShare(Staged):
    spread = True

    def __init__(self, arrays, axes, cores):
        super().__init__()
        self.axes, self.cores, self.held = axes, cores, []
        for a, axis in zip(arrays, axes):
            shape = list(a.shape)
            shape[axis] *= cores
            self.take(a)
            self.give(tuple(shape), jnp.bfloat16)
            self.held.append(
                (
                    self.hold((2, 128, a.shape[1]), jnp.float32),
                    self.hold((2, 128, a.shape[1]), jnp.bfloat16),
                )
            )
        self.pair_sems = self.add(pltpu.SemaphoreType.DMA((2, len(arrays), cores)))

    def build(self):
        cores, core = self.cores, lax.axis_index("fsdp")
        sems = self.refs[self.pair_sems]

        def part(k, which):
            rows, columns = self.ins[k].shape
            if self.axes[k] == 0:
                return self.gives[k].at[pl.ds(pl.multiple_of(which * rows, 128), rows)]
            return self.gives[k].at[:, pl.ds(pl.multiple_of(which * columns, 128), columns)]

        def pair_copy(k, j):
            return pltpu.make_async_remote_copy(
                src_ref=part(k, core),
                dst_ref=part(k, core),
                send_sem=sems.at[0, k, j],
                recv_sem=sems.at[1, k, core],
                device_id={"fsdp": lax.rem(core + j, cores)},
                device_id_type=MESH,
            )

        def one(k):
            wide, low = (self.refs[j] for j in self.held[k])
            src, out = self.ins[k], self.gives[k]
            rows, columns = src.shape

            def body(i, slot):
                low[slot] = wide[slot].astype(jnp.bfloat16)

            def there(i):
                if self.axes[k] == 0:
                    return out.at[pl.ds(pl.multiple_of(core * rows + i * 128, 128), 128)]
                return out.at[span(i, 128), pl.ds(pl.multiple_of(core * columns, 128), columns)]

            before, turns, turn, after = self.stage(
                rows // 128,
                [lambda i, s: (src.at[span(i, 128)], wide.at[s])],
                [lambda i, s: (low.at[s], there(i))],
                body,
            )

            def share():
                after()
                for j in range(1, cores):
                    pair_copy(k, j).start()
                if k + 1 == len(self.axes):
                    end()

            return before, turns, turn, share

        def end():
            for k in range(len(self.axes)):
                for j in range(1, cores):
                    other = lax.rem(core + j, cores)
                    pltpu.make_async_copy(
                        part(k, other), part(k, other), sems.at[1, k, other]
                    ).wait()
                    pair_copy(k, j).wait_send()

        return [one(k) for k in range(len(self.axes))]


def wide_dot(left, right):
    return jnp.dot(left, right, preferred_element_type=jnp.float32)


def across(left, right):
    return lax.dot_general(
        left, right, (((1,), (1,)), ((), ())), preferred_element_type=jnp.float32
    )


def norm_rows(values):
    return values * lax.rsqrt(jnp.mean(values * values, axis=-1, keepdims=True) + EPS)


def turned(values):
    return jnp.transpose(values.astype(jnp.float32)).astype(values.dtype)


def select(slots, column):
    place = lax.broadcasted_iota(jnp.int32, (column.shape[0], slots), 1).astype(jnp.float32)
    return jnp.where(place == column, 1.0, 0.0).astype(jnp.bfloat16)


def select_t(slots, row):
    place = lax.broadcasted_iota(jnp.int32, (slots, row.shape[1]), 0).astype(jnp.float32)
    return jnp.where(place == row, 1.0, 0.0).astype(jnp.bfloat16)


class ExpertForward(Staged):
    def __init__(self, gate, up, down, ffn, shared, w, router, chosen, column, row, lane):
        super().__init__()
        low, wide = jnp.bfloat16, jnp.float32
        self.pairs, self.slots, self.tokens = row.shape[0], row.slots, row.shape[2]
        rows, fe, seq = self.pairs * self.slots, gate.shape[1], ffn.shape[0]
        wp = -(-w // 128) * 128
        self.fe, self.w, self.wp, self.lane = fe, w, wp, lane
        for a in (gate, up, down, ffn, shared, router, chosen, column, row.array):
            self.take(a)
        self.give((rows, 2 * fe), wide)
        self.give((fe, rows), low)
        self.give((rows, D), low)
        self.give((D, rows), low)
        self.give((seq, 2 * wp), wide)
        self.give((wp, seq), low)
        self.give((seq, D), low)
        self.give((seq, 128), wide)
        self.give((seq, 128), wide)
        self.give((D, 2 * wp), low)
        self.give((D, wp), low)
        self.held = {
            "shared": self.hold(shared.shape, low),
            "arrived": self.hold((rows, D), low),
            "tile": self.hold((2, D, 256), low),
            "hidden": self.hold((rows, fe), low),
            "pre": self.hold((2, rows, 256), wide),
            "hidden_t": self.hold((2, 128, rows), low),
            "down": self.hold((2, fe, 256), low),
            "y": self.hold((rows, D), low),
            "y_out": self.hold((2, rows, 256), low),
            "arrived_t": self.hold((2, 256, rows), low),
            "ffn": self.hold((2, self.tokens, D), low),
            "chosen": self.hold((2, self.tokens, 128), low),
            "gates": self.hold((2, self.tokens, 128), wide),
            "gate_out": self.hold((2, self.tokens, 128), wide),
            "gate": self.hold((seq, 128), wide),
            "shared_in": self.hold((D, 2 * wp), low),
            "shared_hidden": self.hold((seq, wp), low),
            "shared_pre": self.hold((2, self.tokens, 2 * wp), wide),
            "shared_t": self.hold((2, wp, self.tokens), low),
            "shared_out": self.hold((D, wp), low),
            "router": self.hold((D, 128), low),
            "column": self.hold((seq, 128), wide),
            "row": self.hold(row.shape, wide),
            "out": self.hold((2, self.tokens, D), low),
        }

    def build(self):
        low = jnp.bfloat16
        r = {name: self.refs[k] for name, k in self.held.items()}
        gate, up, down, ffn = self.ins[:4]
        chosen = self.ins[6]
        pre, hidden_t, y, arrived_t, shared_pre, shared_t, out, gates, gate_out = self.gives[:9]
        fe, wp, tokens, slots = self.fe, self.wp, self.tokens, self.slots
        mine = self.lane + lax.axis_index("ctx")
        ready = {
            name: self.whole(k, self.held[name])
            for name, k in (
                ("shared", 4),
                ("router", 5),
                ("column", 7),
                ("row", 8),
            )
        }

        def part():
            columns = r["shared"].shape[1]
            at = lax.broadcasted_iota(jnp.int32, (columns, 3 * wp), 0)
            to = lax.broadcasted_iota(jnp.int32, (columns, 3 * wp), 1)
            block = jnp.where(to >= 2 * wp, 2, jnp.where(to >= wp, 1, 0))
            inside = to - block * wp
            placed = jnp.where((at == block * self.w + inside) & (inside < self.w), 1.0, 0.0)
            placed = placed.astype(low)
            r["shared_in"][...] = wide_dot(r["shared"][...], placed[:, : 2 * wp]).astype(low)
            r["shared_out"][...] = wide_dot(r["shared"][...], placed[:, 2 * wp :]).astype(low)

        def rows_in(i, slot):
            at = span(i, tokens)
            rows = r["ffn"][slot]
            marks = r["chosen"][slot].astype(jnp.float32) > 0.5
            logits = jnp.where(marks, wide_dot(rows, r["router"][...]), NEG)
            shifted = jnp.exp(logits - jnp.max(logits, axis=-1, keepdims=True))
            shifted = jnp.where(marks, shifted, 0.0)
            parts = shifted / jnp.sum(shifted, axis=-1, keepdims=True)
            r["gates"][slot] = parts
            lanes = lax.broadcasted_iota(jnp.int32, parts.shape, 1)
            part = jnp.sum(jnp.where(lanes == mine, parts, 0.0), axis=-1, keepdims=True)
            part = jnp.broadcast_to(part, parts.shape)
            r["gate"][at] = part
            r["gate_out"][slot] = part
            r["arrived"][span(i, slots, 16)] = wide_dot(select_t(slots, r["row"][i]), rows).astype(
                low
            )
            both_ = wide_dot(rows, r["shared_in"][...])
            r["shared_pre"][slot] = both_
            first = both_[:, :wp]
            value = (first * jax.nn.sigmoid(first) * both_[:, wp:]).astype(low)
            r["shared_hidden"][at] = value
            r["shared_t"][slot] = turned(value)

        def expert_in(i, slot):
            both_ = wide_dot(r["arrived"][...], r["tile"][slot])
            r["pre"][slot] = both_
            first = both_[:, :128]
            value = (first * jax.nn.sigmoid(first) * both_[:, 128:]).astype(low)
            r["hidden"][:, span(i, 128)] = value
            r["hidden_t"][slot] = turned(value)

        def expert_out(i, slot):
            value = wide_dot(r["hidden"][...], r["down"][slot]).astype(low)
            r["y"][:, span(i, 256)] = value
            r["y_out"][slot] = value
            r["arrived_t"][slot] = turned(r["arrived"][:, span(i, 256)])

        def result(i, slot):
            at = span(i, tokens)
            routed = wide_dot(select(slots, r["column"][at, 0:1]), r["y"][span(i, slots, 16)])
            more = across(r["shared_hidden"][at], r["shared_out"][...])
            r["out"][slot] = (r["gate"][at, 0:1] * routed + more).astype(low)

        return [
            self.stage(
                self.pairs,
                [
                    lambda i, s: (ffn.at[span(i, tokens)], r["ffn"].at[s]),
                    lambda i, s: (chosen.at[span(i, tokens)], r["chosen"].at[s]),
                ],
                [
                    lambda i, s: (r["shared_pre"].at[s], shared_pre.at[span(i, tokens)]),
                    lambda i, s: (r["shared_t"].at[s], shared_t.at[:, span(i, tokens)]),
                    lambda i, s: (r["gates"].at[s], gates.at[span(i, tokens)]),
                    lambda i, s: (r["gate_out"].at[s], gate_out.at[span(i, tokens)]),
                ],
                rows_in,
                [ready["shared"], ready["router"], ready["row"], part],
            ),
            self.stage(
                fe // 128,
                [
                    lambda i, s: (gate.at[:, span(i, 128)], r["tile"].at[s, :, pl.ds(0, 128)]),
                    lambda i, s: (up.at[:, span(i, 128)], r["tile"].at[s, :, pl.ds(128, 128)]),
                ],
                [
                    lambda i, s: (r["pre"].at[s], pre.at[:, span(i, 256)]),
                    lambda i, s: (r["hidden_t"].at[s], hidden_t.at[span(i, 128)]),
                ],
                expert_in,
            ),
            self.stage(
                D // 256,
                [lambda i, s: (down.at[:, span(i, 256)], r["down"].at[s])],
                [
                    lambda i, s: (r["y_out"].at[s], y.at[:, span(i, 256)]),
                    lambda i, s: (r["arrived_t"].at[s], arrived_t.at[span(i, 256)]),
                ],
                expert_out,
            ),
            self.stage(
                self.pairs,
                [],
                [lambda i, s: (r["out"].at[s], out.at[span(i, tokens)])],
                result,
                [ready["column"]],
            ),
            self.stage(
                1,
                [],
                [
                    lambda i, s: (r["shared_in"], self.gives[9]),
                    lambda i, s: (r["shared_out"], self.gives[10]),
                ],
                lambda i, s: None,
            ),
        ]


class Slots:
    def __init__(self, array, slots):
        self.array, self.shape, self.slots = array, array.shape, slots


class ExpertBackward(Staged):
    def __init__(
        self, gate, up, down, grad, y, row_gate, pre, shared_pre, shared_in, shared_out, column, row
    ):
        super().__init__()
        low, wide = jnp.bfloat16, jnp.float32
        self.pairs, self.slots, self.tokens = row.shape[0], row.slots, row.shape[2]
        rows, fe, seq = self.pairs * self.slots, gate.shape[1], grad.shape[0]
        wp = shared_out.shape[1]
        self.fe, self.wp = fe, wp
        for a in (gate, up, down, grad, y, row_gate, pre, shared_pre, shared_in, shared_out, column):
            self.take(a)
        self.take(row.array)
        self.give((rows, D), low)
        self.give((rows, fe), low)
        self.give((rows, fe), low)
        self.give((2 * wp, seq), low)
        self.give((2 * self.pairs, 8, self.tokens // 2), wide)
        self.give((seq, D), low)
        self.held = {
            "rows": self.hold((rows, D), low),
            "pre": self.hold((2, rows, 512), wide),
            "down": self.hold((2, 256, D), low),
            "pre_last": self.hold((2, rows, 256), wide),
            "down_last": self.hold((2, 128, D), low),
            "d_gate": self.hold((rows, fe), low),
            "d_up": self.hold((rows, fe), low),
            "gate": self.hold((2, 256, fe), low),
            "up": self.hold((2, 256, fe), low),
            "grad": self.hold((2, self.tokens, D), low),
            "y": self.hold((2, self.slots, D), low),
            "row_gate": self.hold((2, self.tokens, 128), wide),
            "gate_grad": self.hold((2, 2, 8, self.tokens // 2), wide),
            "shared_pre": self.hold((2, self.tokens, 2 * wp), wide),
            "shared_out": self.hold((D, wp), low),
            "d_shared": self.hold((seq, 2 * wp), low),
            "shared_t": self.hold((2, 2 * wp, self.tokens), low),
            "shared_in": self.hold((D, 2 * wp), low),
            "column": self.hold((seq, 128), wide),
            "row": self.hold(row.shape, wide),
            "out": self.hold((2, self.tokens, D), low),
        }

    def build(self):
        low, wide = jnp.bfloat16, jnp.float32
        r = {name: self.refs[k] for name, k in self.held.items()}
        gate, up, down, grad, y, row_gate, pre, shared_pre = self.ins[:8]
        grad_rows, d_gate, d_up, shared_t, gate_grad, out = self.gives
        fe, wp, tokens, slots = self.fe, self.wp, self.tokens, self.slots
        ready = {
            name: self.whole(k, self.held[name])
            for name, k in (("shared_in", 8), ("shared_out", 9), ("column", 10), ("row", 11))
        }

        def slopes(first, second, grads):
            sigmoid = jax.nn.sigmoid(first)
            act = first * sigmoid
            slope = sigmoid * (1.0 + first * (1.0 - sigmoid))
            return (grads * second * slope).astype(low), (grads * act).astype(low)

        def rows_in(i, slot):
            at = span(i, tokens)
            grads = r["grad"][slot]
            exact = grads.astype(wide)
            weighted = (r["row_gate"][slot, :, 0:1] * exact).astype(low)
            r["rows"][span(i, slots, 16)] = wide_dot(
                select_t(slots, r["row"][i]), weighted
            ).astype(low)
            results = wide_dot(select(slots, r["column"][at, 0:1]), r["y"][slot])
            gained = jnp.sum(results * exact, axis=-1, keepdims=True)
            gained = jnp.transpose(jnp.broadcast_to(gained, (tokens, 128)))
            for k in range(2):
                r["gate_grad"][slot, k] = gained[:8, k * (tokens // 2) : (k + 1) * (tokens // 2)]
            hidden_grads = wide_dot(grads, r["shared_out"][...])
            values = r["shared_pre"][slot]
            one, two = slopes(values[:, :wp], values[:, wp:], hidden_grads)
            value = jnp.concatenate([one, two], axis=1)
            r["d_shared"][at] = value
            r["shared_t"][slot] = turned(value)

        def expert_hidden(i, slot):
            grads = across(r["rows"][...], r["down"][slot])
            values = r["pre"][slot]
            first = jnp.concatenate([values[:, :128], values[:, 256:384]], axis=1)
            second = jnp.concatenate([values[:, 128:256], values[:, 384:]], axis=1)
            one, two = slopes(first, second, grads)
            r["d_gate"][:, span(i, 256)] = one
            r["d_up"][:, span(i, 256)] = two

        def expert_hidden_last(i, slot):
            grads = across(r["rows"][...], r["down_last"][slot])
            values = r["pre_last"][slot]
            one, two = slopes(values[:, :128], values[:, 128:], grads)
            at = pl.ds(even, 128)
            r["d_gate"][:, at] = one
            r["d_up"][:, at] = two

        def expert_rows(i, slot):
            value = across(r["d_gate"][...], r["gate"][slot])
            value = value + across(r["d_up"][...], r["up"][slot])
            r["rows"][:, span(i, 256)] = value.astype(low)

        def result(i, slot):
            at = span(i, tokens)
            value = wide_dot(select(slots, r["column"][at, 0:1]), r["rows"][span(i, slots, 16)])
            value = value + across(r["d_shared"][at], r["shared_in"][...])
            r["out"][slot] = value.astype(low)

        even = fe // 256 * 256
        found = [
            self.stage(
                self.pairs,
                [
                    lambda i, s: (grad.at[span(i, tokens)], r["grad"].at[s]),
                    lambda i, s: (y.at[span(i, slots, 16)], r["y"].at[s]),
                    lambda i, s: (row_gate.at[span(i, tokens)], r["row_gate"].at[s]),
                    lambda i, s: (shared_pre.at[span(i, tokens)], r["shared_pre"].at[s]),
                ],
                [
                    lambda i, s: (r["shared_t"].at[s], shared_t.at[:, span(i, tokens)]),
                    lambda i, s: (r["gate_grad"].at[s], gate_grad.at[pl.ds(2 * i, 2)]),
                    lambda i, s: (
                        r["rows"].at[span(i, slots, 16)],
                        grad_rows.at[span(i, slots, 16)],
                    ),
                ],
                rows_in,
                [ready["shared_out"], ready["column"], ready["row"]],
            ),
            self.stage(
                even // 256,
                [
                    lambda i, s: (down.at[span(i, 256)], r["down"].at[s]),
                    lambda i, s: (pre.at[:, span(i, 512)], r["pre"].at[s]),
                ],
                [],
                expert_hidden,
            ),
        ]
        if even < fe:
            found.append(
                self.stage(
                    1,
                    [
                        lambda i, s: (down.at[pl.ds(even, 128)], r["down_last"].at[s]),
                        lambda i, s: (pre.at[:, pl.ds(2 * even, 256)], r["pre_last"].at[s]),
                    ],
                    [],
                    expert_hidden_last,
                )
            )
        return found + [
            self.stage(
                D // 256,
                [
                    lambda i, s: (gate.at[span(i, 256)], r["gate"].at[s]),
                    lambda i, s: (up.at[span(i, 256)], r["up"].at[s]),
                ],
                [],
                expert_rows,
            ),
            self.stage(
                1,
                [],
                [lambda i, s: (r["d_gate"], d_gate), lambda i, s: (r["d_up"], d_up)],
                lambda i, s: None,
            ),
            self.stage(
                self.pairs,
                [],
                [lambda i, s: (r["out"].at[s], out.at[span(i, tokens)])],
                result,
                [ready["shared_in"]],
            ),
        ]


class Heads(Staged):
    def __init__(self, inputs, gain, head, small, kvb, gain_latent, turns, starts, scale):
        super().__init__()
        low, wide = jnp.bfloat16, jnp.float32
        seq = inputs.shape[0]
        self.seq, self.scale, self.n = seq, scale, seq // 128
        for a in (inputs, gain, head, small, kvb, gain_latent, turns, starts):
            self.take(a)
        self.give((seq, D), low)
        self.give((seq, RANK), low)
        self.give((seq, 256), low)
        self.give((seq, 256), low)
        self.give((seq, VDIM), low)
        self.give((seq, VDIM), wide)
        self.give((seq, 128), wide)
        self.give((self.n, 128, VDIM), low)
        self.held = {
            "inputs": self.hold((2, BLOCK, D), low),
            "normed": self.hold((2, BLOCK, D), low),
            "latent": self.hold((2, BLOCK, RANK), low),
            "turns": self.hold((2, BLOCK, 256), wide),
            "gain": self.hold((8, D), wide),
            "head": self.hold(head.shape, low),
            "small": self.hold(small.shape, low),
            "kvb": self.hold(kvb.shape, low),
            "gain_latent": self.hold((8, RANK), wide),
            "starts": self.hold(starts.shape, jnp.int32),
            "query": self.hold((seq, 256), low),
            "key": self.hold((seq, 256), low),
            "value": self.hold((seq, VDIM), low),
            "attended": self.hold((seq, VDIM), wide),
            "log_total": self.hold((seq, 128), wide),
            "result": self.hold((seq, VDIM), low),
        }

    def build(self):
        low, wide = jnp.bfloat16, jnp.float32
        r = {name: self.refs[k] for name, k in self.held.items()}
        inputs, turns = self.ins[0], self.ins[6]
        normed, latent, query, key, value, attended, log_total, blocks = self.gives
        n = self.n
        ready = [
            self.whole(k, self.held[name])
            for name, k in (
                ("gain", 1),
                ("head", 2),
                ("small", 3),
                ("kvb", 4),
                ("gain_latent", 5),
                ("starts", 7),
            )
        ]

        def rope(values, slot):
            lanes = lax.broadcasted_iota(jnp.int32, values.shape, 1)
            half = ROPE // 2
            partner = jnp.where(
                lanes < half, pltpu.roll(values, 128 - half, 1), pltpu.roll(values, half, 1)
            )
            turned_ = values * r["turns"][slot, :, :128] + partner * r["turns"][slot, :, 128:]
            return jnp.where(lanes < ROPE, turned_, 0.0).astype(low)

        def project(i, slot):
            at = span(i, BLOCK)
            rows = norm_rows(r["inputs"][slot].astype(wide)) * r["gain"][0:1]
            rows = rows.astype(low)
            r["normed"][slot] = rows
            raw = wide_dot(rows, r["head"][...])
            r["query"][at, pl.ds(0, 128)] = raw[:, :128].astype(low)
            r["query"][at, pl.ds(128, 128)] = rope(raw[:, 128:256], slot)
            packed = wide_dot(rows, r["small"][...])
            rows = (norm_rows(packed[:, :RANK]) * r["gain_latent"][0:1]).astype(low)
            r["latent"][slot] = rows
            pair = wide_dot(rows, r["kvb"][...]).astype(low)
            r["key"][at, pl.ds(0, 128)] = pair[:, :128]
            r["key"][at, pl.ds(128, 128)] = rope(packed[:, RANK : RANK + 128], slot)
            r["value"][at] = pair[:, 128:]

        def block(start):
            def body(i, slot):
                rows, reach = pl.ds(start, BLOCK), start + BLOCK
                scores = across(r["query"][rows], r["key"][:reach])
                seen = visible(r["starts"], start, scores.shape)
                scores = jnp.where(seen, scores * self.scale, NEG)
                peak = jnp.max(scores, axis=-1, keepdims=True)
                shifted = jnp.exp(scores - peak)
                total = jnp.sum(shifted, axis=-1, keepdims=True)
                probs = (shifted * (1.0 / total)).astype(low)
                found = wide_dot(probs, r["value"][:reach])
                r["attended"][rows] = found
                r["result"][rows] = found.astype(low)
                r["log_total"][rows] = jnp.broadcast_to(peak + jnp.log(total), (BLOCK, 128))

            def piece(k):
                owner, first = (k, 0) if k < n else (2 * n - 1 - k, 64)
                return lambda i, s: (
                    r["result"].at[pl.ds(64 * k, 64)],
                    blocks.at[owner, pl.ds(first, 64)],
                )

            first = start // 64
            return self.stage(1, [], [piece(first + k) for k in range(BLOCK // 64)], body)

        def whole_out(name, there):
            return lambda i, s: (r[name], there)

        return (
            [
                self.stage(
                    self.seq // BLOCK,
                    [
                        lambda i, s: (inputs.at[span(i, BLOCK)], r["inputs"].at[s]),
                        lambda i, s: (turns.at[span(i, BLOCK)], r["turns"].at[s]),
                    ],
                    [
                        lambda i, s: (r["normed"].at[s], normed.at[span(i, BLOCK)]),
                        lambda i, s: (r["latent"].at[s], latent.at[span(i, BLOCK)]),
                    ],
                    project,
                    ready,
                )
            ]
            + [block(start) for start in range(0, self.seq, BLOCK)]
            + [
                self.stage(
                    1,
                    [],
                    [
                        whole_out("query", query),
                        whole_out("key", key),
                        whole_out("value", value),
                        whole_out("attended", attended),
                        whole_out("log_total", log_total),
                    ],
                    lambda i, s: None,
                )
            ]
        )


class HeadsBack(Staged):
    def __init__(
        self, grads, query, key, value, attended, log_total, starts, turns, kvb, normed, latent, scale
    ):
        super().__init__()
        low, wide = jnp.bfloat16, jnp.float32
        seq = query.shape[0]
        self.seq, self.scale, self.n, self.columns = seq, scale, seq // 128, RANK + 128
        for a in (grads, query, key, value, attended, log_total, starts, turns, kvb, normed, latent):
            self.take(a)
        self.give((self.n, 128, 256), low)
        self.give((seq, self.columns), low)
        self.give((D, 256), low)
        self.give((RANK, KV), low)
        self.held = {
            "grad": self.hold((seq, VDIM), low),
            "query": self.hold((seq, 256), low),
            "key": self.hold((seq, 256), low),
            "value": self.hold((seq, VDIM), low),
            "attended": self.hold((seq, VDIM), wide),
            "log_total": self.hold((seq, 128), wide),
            "starts": self.hold(starts.shape, jnp.int32),
            "turns": self.hold((seq, 256), wide),
            "kvb": self.hold(kvb.shape, low),
            "normed": self.hold((2, BLOCK, D), low),
            "latent": self.hold((2, BLOCK, RANK), low),
            "d_query": self.hold((seq, 256), low),
            "d_key": self.hold((seq, 256), wide),
            "d_value": self.hold((seq, VDIM), wide),
            "part": self.hold((2, BLOCK, self.columns), low),
            "q_sum": self.hold((256, D), wide),
            "kvb_sum": self.hold((KV, RANK), wide),
            "q_grad": self.hold((D, 256), low),
            "kvb_grad": self.hold((RANK, KV), low),
        }

    def build(self):
        low, wide = jnp.bfloat16, jnp.float32
        r = {name: self.refs[k] for name, k in self.held.items()}
        grads, normed, latent = self.ins[0], self.ins[9], self.ins[10]
        blocks, part, q_grad, kvb_grad = self.gives
        n, scale = self.n, self.scale
        ready = [
            self.whole(k, self.held[name])
            for name, k in (
                ("query", 1),
                ("key", 2),
                ("value", 3),
                ("attended", 4),
                ("log_total", 5),
                ("starts", 6),
                ("turns", 7),
                ("kvb", 8),
            )
        ]

        def owned(there, k):
            owner, first = (k, 0) if k < n else (2 * n - 1 - k, 64)
            return there.at[owner, pl.ds(first, 64)]

        for k in range(2 * n):
            (sem,) = self.new_sems(1)
            copy = pltpu.make_async_copy(
                owned(grads, k), r["grad"].at[pl.ds(64 * k, 64)], sem.at[0]
            )
            self.first.append(copy)
            ready.append(copy.wait)

        def clear():
            r["d_key"][...] = jnp.zeros_like(r["d_key"])
            r["d_value"][...] = jnp.zeros_like(r["d_value"])
            r["q_sum"][...] = jnp.zeros_like(r["q_sum"])
            r["kvb_sum"][...] = jnp.zeros_like(r["kvb_sum"])

        def rope_back(values, rows):
            lanes = lax.broadcasted_iota(jnp.int32, values.shape, 1)
            half = ROPE // 2
            partner = jnp.where(
                lanes < half, pltpu.roll(values, 128 - half, 1), pltpu.roll(values, half, 1)
            )
            turned_ = values * r["turns"][rows, 0:128] - partner * r["turns"][rows, 128:256]
            return jnp.where(lanes < ROPE, turned_, 0.0).astype(low)

        def t_dot(left, right):
            return lax.dot_general(
                left, right, (((0,), (0,)), ((), ())), preferred_element_type=wide
            )

        def block(start):
            def body(i, slot):
                rows, reach = pl.ds(start, BLOCK), start + BLOCK
                mine, grad_rows = r["query"][rows], r["grad"][rows]
                scores = across(mine, r["key"][:reach])
                seen = visible(r["starts"], start, scores.shape)
                probs = jnp.exp(scores * scale - r["log_total"][rows, 0:1])
                probs = jnp.where(seen, probs, 0.0)
                delta = jnp.sum(
                    grad_rows.astype(wide) * r["attended"][rows], axis=-1, keepdims=True
                )
                d_probs = across(grad_rows, r["value"][:reach])
                d_scores = (probs * (d_probs - delta)).astype(low)
                d_query = wide_dot(d_scores, r["key"][:reach]) * scale
                d_query = d_query.astype(low)
                r["d_query"][rows, pl.ds(0, 128)] = d_query[:, :128]
                r["d_query"][rows, pl.ds(128, 128)] = rope_back(d_query[:, 128:].astype(wide), rows)
                r["d_key"][:reach] += t_dot(d_scores, mine)
                r["d_value"][:reach] += t_dot(probs.astype(low), grad_rows)

            def piece(k):
                return lambda i, s: (r["d_query"].at[pl.ds(64 * k, 64)], owned(blocks, k))

            first = start // 64
            return self.stage(
                1,
                [],
                [piece(first + k) for k in range(BLOCK // 64)],
                body,
                (ready + [clear]) if start == 0 else (),
            )

        def project(i, slot):
            at = span(i, BLOCK)
            rows = r["normed"][slot]
            r["q_sum"][...] += wide_dot(turned(r["d_query"][at]), rows)
            d_key = r["d_key"][at] * scale
            pair = jnp.concatenate([d_key[:, :NOPE], r["d_value"][at]], axis=1)
            high = pair.astype(low)
            rest = (pair - high.astype(wide)).astype(low)
            value = across(high, r["kvb"][...]) + across(rest, r["kvb"][...])
            r["part"][slot, :, pl.ds(0, RANK)] = value.astype(low)
            r["part"][slot, :, pl.ds(RANK, 128)] = d_key[:, NOPE:].astype(low)
            hidden = r["latent"][slot]
            r["kvb_sum"][...] += wide_dot(turned(high), hidden) + wide_dot(turned(rest), hidden)

        def finish(i, slot):
            r["q_grad"][...] = jnp.transpose(r["q_sum"][...]).astype(low)
            r["kvb_grad"][...] = jnp.transpose(r["kvb_sum"][...]).astype(low)

        return (
            [block(start) for start in range(0, self.seq, BLOCK)]
            + [
                self.stage(
                    self.seq // BLOCK,
                    [
                        lambda i, s: (normed.at[span(i, BLOCK)], r["normed"].at[s]),
                        lambda i, s: (latent.at[span(i, BLOCK)], r["latent"].at[s]),
                    ],
                    [lambda i, s: (r["part"].at[s], part.at[span(i, BLOCK)])],
                    project,
                )
            ]
            + [
                self.stage(
                    1,
                    [],
                    [lambda i, s: (r["q_grad"], q_grad), lambda i, s: (r["kvb_grad"], kvb_grad)],
                    finish,
                )
            ]
        )


def visible(starts, first, shape):
    row = first + lax.broadcasted_iota(jnp.int32, (shape[0], 128), 0)
    opening = jnp.zeros_like(row)
    for k in range(starts.shape[0]):
        start = starts[k : k + 1]
        opening = jnp.maximum(opening, jnp.where(start <= row, start, 0))
    column = lax.broadcasted_iota(jnp.int32, shape, 1)
    return (column >= opening[:, 0:1]) & (column <= row[:, 0:1])


def attend_kernel(causal, scale, query, key, value, bounds, attended, log_total):
    for start in range(0, query.shape[0], BLOCK):
        rows = pl.ds(start, BLOCK)
        reach = start + BLOCK if causal else key.shape[0]
        scores = lax.dot_general(
            query[rows], key[:reach], (((1,), (1,)), ((), ())), preferred_element_type=jnp.float32
        )
        column = lax.broadcasted_iota(jnp.int32, scores.shape, 1)
        seen = (column >= bounds[rows, 0:1]) & (column <= bounds[rows, 1:2])
        scores = jnp.where(seen, scores * scale, NEG)
        peak = jnp.max(scores, axis=-1, keepdims=True)
        shifted = jnp.exp(scores - peak)
        total = jnp.sum(shifted, axis=-1, keepdims=True)
        probs = (shifted * (1.0 / total)).astype(jnp.bfloat16)
        attended[rows] = jnp.dot(probs, value[:reach], preferred_element_type=jnp.float32)
        log_total[rows] = jnp.broadcast_to(peak + jnp.log(total), (BLOCK, 128))


def attend(query, key, value, bounds, causal, scale):
    whole = pl.BlockSpec(memory_space=pltpu.VMEM)
    return pl.pallas_call(
        functools.partial(attend_kernel, causal, scale),
        out_shape=[
            jax.ShapeDtypeStruct((query.shape[0], VDIM), jnp.float32),
            jax.ShapeDtypeStruct((query.shape[0], 128), jnp.float32),
        ],
        in_specs=[whole] * 4,
        out_specs=[whole] * 2,
        compiler_params=pltpu.CompilerParams(vmem_limit_bytes=48 << 20),
        name="attend",
    )(query, key, value, bounds)


def attend_back_kernel(
    causal, scale, query, key, value, bounds, log_total, attended, grad, d_query, d_key, d_value
):
    d_key[...] = jnp.zeros_like(d_key)
    d_value[...] = jnp.zeros_like(d_value)
    for start in range(0, query.shape[0], BLOCK):
        rows = pl.ds(start, BLOCK)
        reach = start + BLOCK if causal else key.shape[0]
        mine, grad_rows = query[rows], grad[rows]
        scores = lax.dot_general(
            mine, key[:reach], (((1,), (1,)), ((), ())), preferred_element_type=jnp.float32
        )
        column = lax.broadcasted_iota(jnp.int32, scores.shape, 1)
        seen = (column >= bounds[rows, 0:1]) & (column <= bounds[rows, 1:2])
        probs = jnp.where(seen, jnp.exp(scores * scale - log_total[rows, 0:1]), 0.0)
        delta = jnp.sum(grad_rows.astype(jnp.float32) * attended[rows], axis=-1, keepdims=True)
        d_probs = lax.dot_general(
            grad_rows, value[:reach], (((1,), (1,)), ((), ())), preferred_element_type=jnp.float32
        )
        d_scores = (probs * (d_probs - delta)).astype(jnp.bfloat16)
        d_query[rows] = (
            jnp.dot(d_scores, key[:reach], preferred_element_type=jnp.float32) * scale
        )
        d_key[:reach] += lax.dot_general(
            d_scores, mine, (((0,), (0,)), ((), ())), preferred_element_type=jnp.float32
        )
        d_value[:reach] += lax.dot_general(
            probs.astype(jnp.bfloat16),
            grad_rows,
            (((0,), (0,)), ((), ())),
            preferred_element_type=jnp.float32,
        )
    d_key[...] = d_key[...] * scale


def attend_back(query, key, value, bounds, log_total, attended, grad, causal, scale):
    whole = pl.BlockSpec(memory_space=pltpu.VMEM)
    return pl.pallas_call(
        functools.partial(attend_back_kernel, causal, scale),
        out_shape=[
            jax.ShapeDtypeStruct(query.shape, jnp.float32),
            jax.ShapeDtypeStruct(key.shape, jnp.float32),
            jax.ShapeDtypeStruct(value.shape, jnp.float32),
        ],
        in_specs=[whole] * 7,
        out_specs=[whole] * 3,
        compiler_params=pltpu.CompilerParams(vmem_limit_bytes=56 << 20),
        name="attend_back",
    )(query, key, value, bounds, log_total, attended, grad)


def doc_index(starts, positions):
    return jnp.sum((positions[:, None] >= starts[None, :]).astype(jnp.int32), axis=1) - 1


def rope_tables(count):
    half = ROPE // 2
    frequency = np.float32(THETA) ** (-np.arange(half, dtype=np.float32) / np.float32(half))
    angles = np.arange(count, dtype=np.float32)[:, None] * frequency[None, :]
    return (np.cos(angles), np.sin(angles))


def rotate_pairs(values, cosines, sines):
    half = values.shape[-1] // 2
    first = values[..., :half]
    second = values[..., half:]
    return jnp.concatenate(
        [first * cosines - second * sines, second * cosines + first * sines], axis=-1
    )


def rms_forward(values, gain):
    factor = lax.rsqrt(jnp.mean(values * values, axis=-1, keepdims=True) + EPS)
    normal = values * factor
    return (normal * gain, normal, factor)


def rms_backward(grad_out, normal, factor, gain):
    scaled = grad_out * gain
    grad_in = factor * (scaled - normal * jnp.mean(scaled * normal, axis=-1, keepdims=True))
    return (grad_in, jnp.sum(grad_out * normal, axis=0))


def silu_parts(values):
    sigmoid = jax.nn.sigmoid(values)
    return (values * sigmoid, sigmoid * (1.0 + values * (1.0 - sigmoid)))


def dot(left, right):
    return jnp.dot(left, right, preferred_element_type=jnp.float32)


def dot_t(left, right):
    return lax.dot_general(left, right, (((1,), (1,)), ((), ())), preferred_element_type=jnp.float32)


def t_dot(left, right):
    return lax.dot_general(left, right, (((0,), (0,)), ((), ())), preferred_element_type=jnp.float32)


def two_parts(values):
    high = lax.reduce_precision(values, 8, 7)
    return high.astype(jnp.bfloat16), (values - high).astype(jnp.bfloat16)


def padded(values, columns):
    short = -values.shape[-1] % columns
    if not short:
        return values
    return jnp.pad(values, [(0, 0)] * (values.ndim - 1) + [(0, short)])


def shards(
    tokens,
    cotangent,
    doc_starts,
    routes,
    attn_gain,
    q_weight,
    kva_weight,
    kv_gain,
    kvb_weight,
    o_weight,
    ffn_gain,
    router_weight,
    shared_gate,
    shared_up,
    shared_down,
    expert_gate,
    expert_up,
    expert_down,
):
    low = jnp.bfloat16
    wide = jnp.float32
    n, cores = lax.axis_size("ctx"), lax.axis_size("fsdp")
    here = lax.axis_index("ctx")
    t = tokens.shape[1]
    half = t // 2
    seq = n * t
    ws = q_weight.shape[0]
    kr = kvb_weight.shape[0]
    copies = n // HEADS
    shared = shared_gate.shape[1]
    w = shared // n
    picks_count = routes.shape[2]
    capacity = 10 * t * picks_count // (7 * n)
    slots_count = -(-capacity // 8) * 8
    scale = HEAD ** (-0.5)
    starts = doc_starts[0]

    def run(name, number, ops, arrays, work=None):
        for op in ops:
            op.setup(n, cores)
        if work is None:
            return communicate(name, number, n, cores, ops, arrays)
        if vmem_bytes([s for op in ops for s in op.scratch] + work.scratch) < 54 << 20:
            return communicate(name, number, n, cores, ops, arrays, work, work.arrays)
        return list(communicate(name, number, n, cores, ops, arrays)) + list(
            communicate(name + "_work", None, n, cores, [], [], work, work.arrays)
        )

    def by_position(owner, start):
        if start < half:
            return pl.multiple_of(owner * half + start, 16)
        return pl.multiple_of((2 * n - 1 - owner) * half + start - half, 16)

    def by_row(rows):
        return lambda owner, start: pl.multiple_of(owner * rows + start, 16)

    def to_owners(values):
        columns = values.shape[-1]
        pair = values.reshape(2, n, half, columns)
        return jnp.concatenate([pair[0], pair[1][::-1]], axis=1)

    def to_positions(values):
        columns = values.shape[-1]
        return jnp.concatenate(
            [
                values[:, :half].reshape(n * half, columns),
                values[::-1, half:].reshape(n * half, columns),
            ]
        )

    small = jnp.concatenate(
        [
            kva_weight,
            router_weight,
            attn_gain[:, None],
            ffn_gain[:, None],
            jnp.pad(kv_gain, (0, ws - kr))[:, None],
        ],
        axis=1,
    ).astype(low)
    small = padded(small, 128)
    small_columns = small.shape[1]
    first = RANK + ROPE
    head_part = jnp.concatenate(
        [
            q_weight.astype(low).reshape(ws, HEADS, HEAD).transpose(1, 0, 2),
            kvb_weight.astype(low)
            .reshape(kr, HEADS, KV)
            .transpose(1, 0, 2)
            .reshape(HEADS, ws, kr * KV // ws),
        ],
        axis=-1,
    )
    if copies > 1:
        head_part = jnp.repeat(head_part, copies, axis=0)
    head_columns = head_part.shape[-1]
    shared_columns = -(-3 * w // 128) * 128
    pick_rows = -(-picks_count // 16) * 16
    pick_part = jnp.pad(jnp.transpose(routes[0]), ((0, pick_rows - picks_count), (0, 0))).astype(low)
    inputs_all, head_all, small, pick_blocks, shared_part = run(
        "gather_tokens",
        0,
        [
            Gather(t, D, low, by_position),
            Exchange(ws, head_columns, low, True),
            Gather(ws, small_columns, low, by_row(ws), True),
            Gather(pick_rows, t, low, by_row(pick_rows)),
        ],
        [tokens[0], head_part, small, pick_part],
        PackShared(shared_gate, shared_up, shared_down, n, shared_columns),
    )
    kva_full = small[:, :first]
    router_full = small[:, first : first + n]
    gain_one = small[:, first + n].astype(wide)
    gain_two = small[:, first + n + 1].astype(wide)
    gain_latent = small[:, first + n + 2].reshape(n * cores, ws)[:, :kr].reshape(-1).astype(wide)
    picks_all = pick_blocks.reshape(n, pick_rows, t)[:, :picks_count].astype(jnp.int32)

    grad_low = cotangent[0]
    grad = grad_low.astype(wide)
    head_all = head_all.reshape(D, head_columns)
    q_head = head_all[:, :HEAD]
    kvb_head = head_all[:, HEAD:].reshape(RANK, KV)

    transfers = [
        Exchange(ws, shared_columns, low, True),
        Gather(ws, D, low, by_row(ws), True, light=True),
    ]
    carried = [shared_part, jnp.transpose(o_weight).astype(low)]
    positions = jnp.arange(seq, dtype=jnp.int32)
    cosines, sines = rope_tables(seq)
    lanes = ((0, 0), (0, 128 - ROPE))
    turns = jnp.asarray(
        np.concatenate(
            [
                np.pad(np.concatenate([cosines, cosines], axis=1), lanes),
                np.pad(np.concatenate([-sines, sines], axis=1), lanes),
            ],
            axis=1,
        )
    )
    cosines, sines = jnp.asarray(cosines), jnp.asarray(sines)
    starts_rows = jnp.broadcast_to(starts[:, None], (starts.shape[0], 128))

    def eight(values):
        return jnp.broadcast_to(values[None], (8, values.shape[0]))

    def heads_apart():
        normed_all = rms_forward(inputs_all.astype(wide), gain_one)[0].astype(low)
        queries, latent_all, keys, values = project(normed_all)
        attended, log_total = attend(queries_here(queries), keys, values, bounds, False, scale)
        return (normed_all, latent_all, queries_here(queries), keys, values, attended, log_total)

    def project(normed_all):
        query_raw = dot(normed_all, q_head)
        blank = jnp.zeros((seq, 2 * NOPE - HEAD), low)
        queries = jnp.concatenate(
            [
                query_raw[:, :NOPE].astype(low),
                rotate_pairs(query_raw[:, NOPE:], cosines, sines).astype(low),
                blank,
            ],
            axis=-1,
        )
        compressed = dot(normed_all, kva_full)
        latent_all = rms_forward(compressed[:, :RANK], gain_latent)[0].astype(low)
        rope_all = rotate_pairs(compressed[:, RANK:], cosines, sines).astype(low)
        kv_head = dot(latent_all, kvb_head).astype(low)
        keys = jnp.concatenate([kv_head[:, :NOPE], rope_all, blank], axis=-1)
        values = kv_head[:, NOPE:]
        return queries, latent_all, keys, values

    opening = jnp.max(jnp.where(starts[None, :] <= positions[:, None], starts[None, :], 0), axis=1)

    def queries_here(rows):
        if copies == 1:
            return rows
        if rows.ndim == 1:
            return queries_here(rows[:, None])[:, 0]
        blocks = to_owners(rows).reshape(n // copies, copies, t, rows.shape[-1])
        return lax.dynamic_index_in_dim(blocks, here % copies, 1, False).reshape(-1, rows.shape[-1])

    def queries_back(rows):
        if copies == 1:
            return to_owners(rows)
        blocks = rows.reshape(n // copies, 1, t, rows.shape[-1])
        mine = (jnp.arange(copies) == here % copies)[None, :, None, None]
        return jnp.where(mine, blocks, jnp.zeros((), rows.dtype)).reshape(n, t, rows.shape[-1])

    def of_heads(blocks):
        columns = blocks.shape[-1]
        if copies > 1:
            blocks = blocks.reshape(HEADS, copies, t, columns)
            blocks = jnp.sum(blocks.astype(wide), axis=1).astype(blocks.dtype)
        return blocks.transpose(1, 0, 2).reshape(t, HEADS * columns)

    query_cos, query_sin = queries_here(cosines), queries_here(sines)
    bounds = queries_here(jnp.pad(jnp.stack([opening, positions], axis=1), ((0, 0), (0, 126))))
    if copies == 1:
        (
            shared_all,
            out_proj,
            normed_all,
            latent_all,
            queries,
            keys,
            values,
            attended,
            log_total,
            blocks,
        ) = run(
            "heads",
            1,
            transfers,
            carried,
            Heads(
                inputs_all,
                eight(gain_one),
                head_all,
                small,
                kvb_head,
                eight(gain_latent),
                turns,
                starts_rows,
                scale,
            ),
        )
    else:
        shared_all, out_proj = run("heads", 1, transfers, carried)
        normed_all, latent_all, queries, keys, values, attended, log_total = heads_apart()
        blocks = queries_back(attended.astype(low))
    side = copies == 1
    (attn_values,) = run("attended", 9, [Exchange(t, VDIM, low, wide_out=side)], [blocks])
    if not side:
        attn_values = of_heads(attn_values)
    shared_all = shared_all.reshape(D, shared_columns)

    inputs = tokens[0].astype(wide)
    normed_one, normal_one, factor_one = rms_forward(inputs, gain_one)
    normed_low = normed_one.astype(low)
    resid = inputs + dot_t(attn_values, out_proj)
    normed_two, normal_two, factor_two = rms_forward(resid, gain_two)
    ffn_in = normed_two.astype(low)

    ffn_all, *experts = run(
        "gather_ffn",
        2,
        [Gather(t, D, low, by_row(t))],
        [ffn_in],
        CastShare([expert_gate[0], expert_up[0], expert_down[0]], (0, 0, 1), cores),
    )

    chosen = jnp.any(
        picks_all[:, :, :, None] == jnp.arange(n, dtype=jnp.int32)[None, None, None, :], axis=1
    ).reshape(seq, n)
    taken = lax.dynamic_index_in_dim(chosen, here, 1, False).reshape(n, t)
    slots = jnp.where(taken, jnp.cumsum(taken.astype(jnp.int32), axis=1) - 1, -1)
    slots = slots + jnp.where(taken, slots_count * (jnp.arange(n, dtype=jnp.int32) % 2)[:, None], 0)
    slots = slots.astype(wide)
    slot_column = jnp.broadcast_to(slots.reshape(seq, 1), (seq, 128))
    slot_row = Slots(slots.reshape(n // 2, 1, 2 * t), 2 * slots_count)
    lane = first - RANK
    marks = jnp.pad(chosen.astype(low), ((0, 0), (lane, 128 - lane - n)))
    shared_rows = -(-w // 128) * 128

    (
        grad_all,
        query_proj,
        pre,
        hidden_t,
        expert_result,
        arrived_t,
        shared_pre,
        shared_t,
        out_part,
        gates_all,
        row_gate,
        shared_in,
        shared_out,
    ) = run(
        "gather_grad",
        6,
        [Gather(t, D, low, by_row(t)), Gather(ws, HEADS * HEAD, low, by_row(ws), True)],
        [grad_low, q_weight.astype(low)],
        ExpertForward(
            *experts,
            ffn_all,
            shared_all,
            w,
            small[:, RANK : RANK + 128],
            marks,
            slot_column,
            slot_row,
            lane,
        ),
    )
    routed, pick_grad, pre_gate_grad, pre_up_grad, shared_grad_t, gate_grads, ffn_part = run(
        "reduce_out",
        7,
        [Reduce(t, D, by_row(t))],
        [out_part],
        ExpertBackward(
            *experts,
            grad_all,
            expert_result,
            row_gate,
            pre,
            shared_pre,
            shared_in,
            shared_out,
            slot_column,
            slot_row,
        ),
    )
    output = (resid + routed).astype(low)

    results = run(
        "reduce_ffn",
        3,
        [Reduce(t, D, by_row(t)), Exchange(8, t, wide)],
        [ffn_part, gate_grads],
        Products(
            [
                shared_grad_t,
                ffn_all,
                hidden_t,
                pick_grad,
                arrived_t,
                pre_gate_grad,
                pre_up_grad,
                shared_t,
                grad_all,
            ],
            [(0, 1, 1, 512), (2, 3, 1, 256), (4, 5, 0, 256), (4, 6, 0, 256), (7, 8, 1, 512)],
            [(1, 8)],
        ),
    )
    ffn_in_grad, gate_blocks, shared_in_grad, out_w_grad, in_gate_grad, in_up_grad, shared_out_grad = (
        results
    )
    column = jnp.arange(shared_columns, dtype=jnp.int32)[None, :]
    wanted = jnp.arange(3 * shared_rows, dtype=jnp.int32)[:, None]
    wanted = jnp.where(wanted % shared_rows < w, wanted // shared_rows * w + wanted % shared_rows, -1)
    placed = (column == wanted).astype(low)
    shared_grads = (
        t_dot(shared_in_grad, placed[: 2 * shared_rows])
        + t_dot(shared_out_grad, placed[2 * shared_rows :])
    )
    shared_grads = shared_grads.astype(low).reshape(n, cores, ws, shared_columns)

    gates = lax.optimization_barrier(lax.dynamic_slice_in_dim(gates_all, here * t, t, 0))
    gates = gates[:, lane : lane + n]
    gate_grad = jnp.transpose(gate_blocks[:, 0, :])
    mixed = jnp.sum(gates * gate_grad, axis=-1, keepdims=True)
    logit_grad = (gates * (gate_grad - mixed)).astype(low)
    ffn_in_grad = ffn_in_grad + dot_t(logit_grad, router_full)
    resid_part, gain_two_grad = rms_backward(ffn_in_grad, normal_two, factor_two, gain_two)
    resid_grad = grad + resid_part
    attn_grad_low = resid_grad.astype(low)
    grad_attended = dot(attn_grad_low, out_proj).astype(low)
    grad_blocks = grad_attended
    if not side:
        grad_blocks = grad_attended.reshape(t, HEADS, VDIM).transpose(1, 0, 2)
        grad_blocks = jnp.repeat(grad_blocks, copies, axis=0)
    (grad_att_blocks,) = run(
        "grad_attended", 4, [Exchange(t, VDIM, low, wide_in=side)], [grad_blocks]
    )
    out_proj_grad = t_dot(attn_grad_low, attn_values).astype(low).reshape(n, cores, ws, D)

    expert_grads = [(in_gate_grad, 0), (in_up_grad, 0), (out_w_grad, 1)]
    transfers = [
        Exchange(ws, shared_columns, low, fold=True),
        Reduce(ws, D, by_row(ws), True, light=True),
    ] + [Halves(g.shape, low, axis) for g, axis in expert_grads]
    carried = [shared_grads, out_proj_grad] + [g for g, axis in expert_grads]
    if copies == 1:
        (
            shared_blocks,
            out_proj_sum,
            *expert_halves,
            query_blocks,
            latent_part,
            query_proj_grad,
            kvb_grad,
        ) = run(
            "heads_back",
            10,
            transfers,
            carried,
            HeadsBack(
                grad_att_blocks,
                queries,
                keys,
                values,
                attended,
                log_total,
                starts_rows,
                turns,
                kvb_head,
                normed_all,
                latent_all,
                scale,
            ),
        )
    else:
        shared_blocks, out_proj_sum, *expert_halves = run("heads_back", 10, transfers, carried)
        grad_att = queries_here(to_positions(grad_att_blocks))
        query_grad, key_grad, value_grad = attend_back(
            queries, keys, values, bounds, log_total, attended, grad_att, False, scale
        )
        query_grad = query_grad.astype(low).astype(wide)
        raw_grad = jnp.concatenate(
            [
                query_grad[:, :NOPE],
                rotate_pairs(query_grad[:, NOPE:HEAD], query_cos, -query_sin),
                jnp.zeros((query_grad.shape[0], 2 * NOPE - HEAD), wide),
            ],
            axis=-1,
        ).astype(low)
        kv_grad = jnp.concatenate([key_grad[:, :NOPE], value_grad], axis=-1)
        kv_high, kv_rest = two_parts(kv_grad)
        latent_part = dot_t(kv_high, kvb_head) + dot_t(kv_rest, kvb_head)
        latent_part = padded(
            jnp.concatenate([latent_part, key_grad[:, NOPE:HEAD]], axis=1).astype(low), 128
        )
        query_blocks = queries_back(raw_grad)
        kvb_grad = (t_dot(latent_all, kv_high) + t_dot(latent_all, kv_rest)).astype(low)
        query_proj_grad = t_dot(queries_here(normed_all), raw_grad).astype(low)
    kvb_rows = -(-kr // 16) * 16
    kvb_grad = jnp.pad(
        kvb_grad.reshape(n, cores, kr, KV), ((0, 0), (0, 0), (0, kvb_rows - kr), (0, 0))
    )
    core = lax.axis_index("fsdp")
    for k, (whole, axis) in enumerate(expert_grads):
        size = whole.shape[axis] // cores
        mine = lax.dynamic_slice_in_dim(whole, core * size, size, axis).astype(wide)
        expert_grads[k] = mine + jnp.sum(expert_halves[k].astype(wide), axis=0)
    query_blocks, latent_sum, query_grad_blocks, kvb_blocks = run(
        "reduce_latent",
        5,
        [
            Exchange(t, 2 * NOPE, low),
            Reduce(t, latent_part.shape[1], by_position, light=True),
            Exchange(ws, 2 * NOPE, low, fold=True),
            Exchange(kvb_rows, KV, low, fold=True),
        ],
        [query_blocks, latent_part, query_proj_grad.reshape(n, cores, ws, 2 * NOPE), kvb_grad],
    )

    compressed_here = dot(normed_low, kva_full)
    unused, latent_normal, latent_factor = rms_forward(compressed_here[:, :RANK], gain_latent)
    my_cosines, my_sines = (
        jnp.concatenate(
            [
                lax.dynamic_slice_in_dim(v, here * half, half),
                lax.dynamic_slice_in_dim(v, (2 * n - 1 - here) * half, half),
            ]
        )
        for v in (cosines, sines)
    )
    comp_latent_grad, gain_latent_grad = rms_backward(
        latent_sum[:, :RANK], latent_normal, latent_factor, gain_latent
    )
    rope_sum = latent_sum[:, RANK : RANK + ROPE].astype(low).astype(wide)
    rope_back = rotate_pairs(rope_sum, my_cosines, -my_sines)
    comp_grad = jnp.concatenate([comp_latent_grad, rope_back], axis=-1).astype(low)
    raw_here = of_heads(query_blocks[:, :, :HEAD])
    normed_grad = dot_t(raw_here, query_proj) + dot_t(comp_grad, kva_full)
    input_part, gain_one_grad = rms_backward(normed_grad, normal_one, factor_one, gain_one)
    input_grad = (resid_grad + input_part).astype(low)

    spare = small_columns - first
    small_grads = t_dot(normed_low, jnp.pad(comp_grad, ((0, 0), (0, spare)))) + t_dot(
        ffn_in, jnp.pad(logit_grad, ((0, 0), (first, spare - n)))
    )
    gain_grads = jnp.stack(
        [
            gain_one_grad.reshape(n, cores, ws),
            gain_two_grad.reshape(n, cores, ws),
            jnp.pad(gain_latent_grad.reshape(n, cores, kr), ((0, 0), (0, 0), (0, ws - kr))),
        ],
        axis=2,
    ).astype(low)
    gain_grads = jnp.pad(gain_grads, ((0, 0), (0, 0), (0, 13), (0, 128 - ws)))
    small_sum, gain_sum = run(
        "weight_grads",
        8,
        [Reduce(ws, small_columns, by_row(ws), True), Reduce(16, 128, by_row(16), True)],
        [small_grads.astype(low).reshape(n, cores, ws, small_columns), gain_grads],
    )

    def to_shards(blocks, rows, columns):
        values = blocks[:, :rows, :columns].astype(wide).reshape(HEADS, copies, rows, columns)
        return jnp.sum(values, axis=1).transpose(1, 0, 2).reshape(rows, HEADS * columns)

    q_weight_grad = to_shards(query_grad_blocks, ws, HEAD)
    kvb_weight_grad = to_shards(kvb_blocks, kr, KV)
    shared_sums = [
        shared_blocks[:, :, i * w : (i + 1) * w]
        .transpose(1, 0, 2)
        .reshape(ws, shared)
        .astype(wide)
        for i in range(3)
    ]
    return (
        output[None],
        input_grad[None],
        gain_sum[0, :ws],
        q_weight_grad,
        small_sum[:, :first],
        gain_sum[2, :kr],
        kvb_weight_grad,
        jnp.transpose(out_proj_sum),
        gain_sum[1, :ws],
        small_sum[:, first : first + n],
        shared_sums[0],
        shared_sums[1],
        jnp.transpose(shared_sums[2]),
        expert_grads[0][None],
        expert_grads[1][None],
        expert_grads[2][None],
    )


def solution(mesh):
    return jax.shard_map(
        shards,
        mesh=mesh,
        in_specs=(
            P("fsdp", "ctx", None),
            P("fsdp", "ctx", None),
            P("fsdp", None),
            P("fsdp", "ctx", None),
            P(("ctx", "fsdp")),
            P(("ctx", "fsdp"), None),
            P(("ctx", "fsdp"), None),
            P(("ctx", "fsdp")),
            P(("ctx", "fsdp"), None),
            P(None, ("ctx", "fsdp")),
            P(("ctx", "fsdp")),
            P(("ctx", "fsdp"), None),
            P(("ctx", "fsdp"), None),
            P(("ctx", "fsdp"), None),
            P(None, ("ctx", "fsdp")),
            P("ctx", "fsdp", None),
            P("ctx", "fsdp", None),
            P("ctx", None, "fsdp"),
        ),
        out_specs=(
            P("fsdp", "ctx", None),
            P("fsdp", "ctx", None),
            P(("ctx", "fsdp")),
            P(("ctx", "fsdp"), None),
            P(("ctx", "fsdp"), None),
            P(("ctx", "fsdp")),
            P(("ctx", "fsdp"), None),
            P(None, ("ctx", "fsdp")),
            P(("ctx", "fsdp")),
            P(("ctx", "fsdp"), None),
            P(("ctx", "fsdp"), None),
            P(("ctx", "fsdp"), None),
            P(None, ("ctx", "fsdp")),
            P("ctx", "fsdp", None),
            P("ctx", "fsdp", None),
            P("ctx", None, "fsdp"),
        ),
        check_vma=False,
    )
```
